768 devices in a mesh: blk: 64 (over x, y, core), row: 12 (over z).
Axes of the slice: x: 4, y: 8, z: 12, core: 2. Of those that a mesh axis runs over, the one named last changes fastest.
Arguments:
- fields: float32 [256, 48, 5, 512], P('blk', 'row'), may hold values from -6 to 6
- orders: int32 [256, 48], P('blk', 'row'), may hold values from 3 to 7
- metric: float32 [3, 256, 48], P(None, 'blk', 'row'), may hold values from 0.5 to 2
- face_turn: int32 [2, 256, 48], P(None, 'blk', 'row'), may hold values from 0 to 3, as said below
- migration: int32 [64, 12, 16, 1], P('blk', 'row'), may hold values from 0 to 4; in each aligned block of 16 rows (0 to 15, 16 to 31, ..., all dimensions but the last counted through in order) at most 5 rows name the same one
Outputs:
- moved: float32 [64, 12, 25, 5, 512], P('blk', 'row')
The draws below stay inside these ranges and needn't reach their ends.
Inputs may be any that keep to these rules, and one draw needn't show every extreme that they name: face_turn[0, x, y] equals face_turn[1, x - 1, y], x counted around the closed curve. `migration`: at most 5 elements of one device share a destination, and some device sends exactly 5 to one destination.
All inputs are finite; a program needn't handle non-finite values.
Results may differ from the reference program's by a relative error of at most 0.0003.
Values sent between devices are 32-bit elements; how exact they have to be, the bound alone decides.
No kernel may reach another device: no remote copies, remote signals or barrier semaphores. Data moves between devices by JAX's collectives and lax.ppermute only.
A program may use at most 128 MiB of HBM per device.

```python
import math
import jax
import jax.numpy as jnp
import numpy as np
from jax import lax

PMAX = 7
PMIN = 3
VARS = 5
REACH = 2
LX = 4
LY = 4
NQ = 8
NODES = 512
NORD = 5
NB = 16
SPREAD = 5
CAP = 5
GX = 256
GY = 48
N_BLK = 64
N_ROW = 12


def draw_face_turn(key, part):
    key = jax.random.fold_in(key, 11)
    base_codes = jax.random.randint(key, (GX, GY), 0, 4).astype(jnp.int32)
    return jnp.stack([jnp.roll(base_codes, 1, axis=0), base_codes])


def set_ends(values, key, low, largest):
    spot = [jax.random.randint(jax.random.fold_in(key, axis), (), 0, length) for axis, length in enumerate(values.shape)]
    main_axis = values.shape.index(max(values.shape))
    neighbour = spot[:main_axis] + [(spot[main_axis] + 1) % values.shape[main_axis]] + spot[main_axis + 1:]
    return values.at[tuple(spot)].set(low).at[tuple(neighbour)].set(largest)


def shard_levels(stream_key, extent, cuts, smallest, largest):
    level, own = 1.0, jax.random.fold_in(stream_key, 6)
    for dim, blocks in cuts:
        draws = jnp.exp(jax.random.uniform(jax.random.fold_in(own, dim), (blocks,), jnp.float32, smallest / len(cuts), largest / len(cuts)))
        level = level * jnp.repeat(draws, extent[dim] // blocks).reshape([-1 if axis == dim else 1 for axis in range(len(extent))])
    return level


def shared_out(stream_key, own, number, rows, amount, top, limit, lean):
    order = jax.random.permutation(stream_key, amount)
    crowded, ordinary = portions_of(amount, rows * top, limit, lean, True), portions_of(amount, rows * top, limit, lean, False)
    places = jnp.arange(amount)

    def named(lengths, rotation):
        used = int((lengths > 0).sum())
        fixed = max(1, used // 4)
        shifted = fixed + (places - fixed + rotation * (used - fixed)) % max(1, amount - fixed)
        return jnp.zeros((amount,), jnp.int32).at[order[jnp.where(places < fixed, places, shifted)]].set(jnp.asarray(lengths, jnp.int32))

    lengths = jnp.where(number % 4 == 0, named(crowded, number // 4), named(ordinary, number - number // 4 - 1))
    mixed = jax.random.permutation(jax.random.fold_in(own, 3), amount)
    giver, receiver = mixed[0:amount // 2 * 2:2], mixed[1:amount // 2 * 2:2]
    slack = jnp.minimum(lengths[giver] - 1, limit - lengths[receiver]) // 2
    slack = jnp.where((giver == order[0]) | (receiver == order[0]) | (lengths[receiver] == 0), 0, jnp.maximum(slack, 0))
    shifted = jax.random.randint(jax.random.fold_in(own, 4), (amount // 2,), 0, 1 << 20) % (slack + 1)
    lengths = lengths.at[giver].add(-shifted).at[receiver].add(shifted)
    members = jnp.searchsorted(jnp.cumsum(lengths), jnp.arange(rows * top), side="right").astype(jnp.int32)
    listing = members.reshape(top, rows).T
    listing = listing[jax.random.permutation(jax.random.fold_in(own, 1), rows)]
    rotation = jax.random.randint(jax.random.fold_in(own, 2), (rows, 1), 0, top)
    return jnp.take_along_axis(listing, (jnp.arange(top)[None, :] + rotation) % top, axis=1)


def portions_of(count, total, bound, slope, full):
    portions = [(1 << 20) // math.isqrt(grade ** slope) + 1 for grade in range(1, count + 1)]
    largest = bound if full else min(bound, max(-(-total // count), total * portions[0] // sum(portions)))
    least = 1 if total - largest >= count - 1 else 0
    counts, rest = [largest] + [least] * (count - 1), total - largest - least * (count - 1)
    while rest > 0:
        free = [i for i in range(1, count) if counts[i] < largest] or [i for i in range(1, count) if counts[i] < bound]
        pool, left = sum([portions[i] for i in free]), rest
        for i in free:
            extra = min(bound - counts[i], max(1, left * portions[i] // pool), rest)
            counts[i] = counts[i] + extra
            rest = rest - extra
    return np.array(counts)


def scatter_about(own_key, extent, scale, reach, cuts=(), held_as=jnp.bfloat16):
    level = shard_levels(own_key, extent, cuts, -0.22, 0.18) if cuts else 1.0
    entries = jax.random.normal(own_key, extent, jnp.float32) * scale * level
    return jnp.minimum(jnp.maximum(entries, -reach), reach).astype(held_as)


def setup_inputs(seed: int = 0) -> dict:
    arg_keys = jax.random.split(jax.random.key(seed), 6)
    fields = scatter_about(arg_keys[0], (GX, GY, VARS, NODES), 1.0, 6.0, ((0, 64), (1, 12)), jnp.float32)
    orders = set_ends(jax.random.randint(arg_keys[1], (GX, GY), PMIN, PMAX + 1), jax.random.fold_in(arg_keys[1], 1), PMIN, PMAX).astype(jnp.int32)
    metric = jnp.clip(jnp.exp(math.log(2.0) - 1.3862944 * jax.random.uniform(arg_keys[2], (3, GX, GY), jnp.float32) ** shard_levels(arg_keys[2], (3, GX, GY), ((1, 64), (2, 12)), -0.2, 0.2)), 0.5, 2.0)
    face_turn = draw_face_turn(jax.random.fold_in(arg_keys[5], 71), 0)
    migration_keys = jax.random.split(jax.random.fold_in(arg_keys[4], 1), N_BLK * N_ROW * NB // NB)
    migration_turns = jax.random.permutation(jax.random.fold_in(arg_keys[4], 3), N_BLK * N_ROW * NB // NB)
    migration = jax.vmap(lambda own, number: shared_out(jax.random.fold_in(arg_keys[4], 2), own, number, NB, SPREAD, 1, CAP, 2))(migration_keys, migration_turns).reshape((N_BLK, N_ROW, NB, 1))
    return dict(fields=fields, orders=orders, metric=metric, face_turn=face_turn, migration=migration)


mean_flow = (0.4, 0.0, 0.2)
time_step = 0.008
highest_mode = lax.Precision.HIGHEST


def legendre_points(degree):
    point_count = degree + 1
    estimate = np.cos(np.pi * np.arange(point_count) / degree)
    for sweep_idx in range(40):
        values = np.zeros((point_count, point_count))
        values[:, 0] = 1.0
        values[:, 1] = estimate
        for order_idx in range(2, point_count):
            values[:, order_idx] = ((2 * order_idx - 1) * estimate * values[:, order_idx - 1] - (order_idx - 1) * values[:, order_idx - 2]) / order_idx
        estimate = estimate - (estimate * values[:, degree] - values[:, degree - 1]) / (point_count * values[:, degree])
    return np.sort(estimate)


def lagrange_matrix(points, targets):
    result = np.ones((len(targets), len(points)))
    for column in range(len(points)):
        for other_idx in range(len(points)):
            if other_idx != column:
                result[:, column] *= (targets - points[other_idx]) / (points[column] - points[other_idx])
    return result


def build_tables(lowest, highest):
    node_count = highest + 1
    level_count = highest - lowest + 1
    common = legendre_points(highest)
    derive = np.zeros((level_count, node_count, node_count))
    to_grid = np.zeros((level_count, node_count, node_count))
    from_grid = np.zeros((level_count, node_count, node_count))
    lifting = np.zeros((level_count,))
    last_node = np.zeros((level_count, node_count))
    active = np.zeros((level_count, node_count))
    for level_idx in range(level_count):
        degree = lowest + level_idx
        points = legendre_points(degree)
        filled = degree + 1
        weights = np.array([1.0 / np.prod([points[column] - points[other_idx] for other_idx in range(filled) if other_idx != column]) for column in range(filled)])
        local_diff = np.zeros((filled, filled))
        for row_idx in range(filled):
            for column in range(filled):
                if column != row_idx:
                    local_diff[row_idx, column] = weights[column] / weights[row_idx] / (points[row_idx] - points[column])
            local_diff[row_idx, row_idx] = -np.sum(local_diff[row_idx])
        derive[level_idx, :filled, :filled] = local_diff
        to_grid[level_idx, :, :filled] = lagrange_matrix(points, common)
        from_grid[level_idx, :filled, :] = lagrange_matrix(common, points)
        lifting[level_idx] = degree * (degree + 1) / 2.0
        last_node[level_idx, degree] = 1.0
        active[level_idx, :filled] = 1.0
    return tuple(jnp.asarray(table_arr, dtype=jnp.float32) for table_arr in (derive, to_grid, from_grid, lifting, last_node, active))


def select_rows(one_hot, table_arr):
    flattened = table_arr.reshape(table_arr.shape[0], -1)
    picked = jnp.dot(one_hot, flattened, precision=highest_mode)
    return picked.reshape((one_hot.shape[0],) + table_arr.shape[1:])


def flux_along(values, direction):
    velocity = values[:, 1 + direction]
    pressure = values[:, 4]
    coupling = [velocity] + [pressure if component == direction else jnp.zeros_like(pressure) for component in range(3)] + [velocity]
    return mean_flow[direction] * values + jnp.stack(coupling, axis=1)


def mirror_normal(face_vals, direction):
    factor = np.ones((5, 1, 1))
    factor[1 + direction] = -1.0
    return face_vals * jnp.asarray(factor, dtype=jnp.float32)


def rusanov(left_state, right_state, direction):
    wave_speed = abs(mean_flow[direction]) + 1.0
    return 0.5 * (flux_along(left_state, direction) + flux_along(right_state, direction)) - 0.5 * wave_speed * (right_state - left_state)


def to_common(face_vals, interp):
    return jnp.einsum('eaj,ebk,evjk->evab', interp, interp, face_vals, precision=highest_mode)


def from_common(face_vals, interp):
    return jnp.einsum('eja,ekb,evab->evjk', interp, interp, face_vals, precision=highest_mode)


def own_traces(volume, last_node, to_interp):
    faces = [volume[:, :, 0],
             jnp.einsum('ei,evijk->evjk', last_node, volume, precision=highest_mode),
             volume[:, :, :, 0],
             jnp.einsum('ej,evijk->evik', last_node, volume, precision=highest_mode),
             volume[:, :, :, :, 0],
             jnp.einsum('ek,evijk->evij', last_node, volume, precision=highest_mode)]
    return [to_common(face_vals, to_interp) for face_vals in faces]


def apply_turn(face_vals, codes):
    variants = [jnp.flip(face_vals, 2), jnp.flip(face_vals, 3), jnp.swapaxes(face_vals, 2, 3)]
    result = face_vals
    for level_idx in range(3):
        result = jnp.where((codes == level_idx + 1)[:, None, None, None], variants[level_idx], result)
    return result


def element_rates(volume, params, own_faces, across):
    derive, to_interp, from_interp, lifting, last_node, scales = params
    node_count = volume.shape[-1]
    first_node = (jnp.arange(node_count) == 0).astype(volume.dtype)
    einsum_forms = (('eai,evijk->evajk', 'i,evjk->evijk', 'ei,evjk->evijk'),
                    ('eaj,evijk->eviak', 'j,evik->evijk', 'ej,evik->evijk'),
                    ('eak,evijk->evija', 'k,evij->evijk', 'ek,evij->evijk'))
    accumulated = jnp.zeros_like(volume)
    for direction in range(3):
        slope_form, low_form, high_form = einsum_forms[direction]
        derived = jnp.einsum(slope_form, derive, flux_along(volume, direction), precision=highest_mode)
        low_own = own_faces[2 * direction]
        high_own = own_faces[2 * direction + 1]
        low_gap = rusanov(across[2 * direction], low_own, direction) - flux_along(low_own, direction)
        high_gap = rusanov(high_own, across[2 * direction + 1], direction) - flux_along(high_own, direction)
        surface = jnp.einsum(low_form, first_node, from_common(low_gap, from_interp), precision=highest_mode) - jnp.einsum(high_form, last_node, from_common(high_gap, from_interp), precision=highest_mode)
        accumulated = accumulated + scales[:, direction][:, None, None, None, None] * (lifting[:, None, None, None, None] * surface - derived)
    return accumulated


def pack_slots(flat_rows, target):
    length = target.shape[-1]
    positions_n = jnp.arange(length, dtype=jnp.int32)
    earlier = positions_n[None, :] < positions_n[:, None]
    same_dest = target[..., :, None] == target[..., None, :]
    rank_in = jnp.sum((same_dest & earlier).astype(jnp.int32), axis=-1)
    offsets = jnp.arange(SPREAD, dtype=jnp.int32)
    places = jnp.arange(CAP, dtype=jnp.int32)
    chosen = (target[..., None, None, :] == offsets[:, None, None]) & (rank_in[..., None, None, :] == places[None, :, None])
    return jnp.einsum('...scn,...nw->...scw', chosen.astype(flat_rows.dtype), flat_rows, precision=highest_mode)


def reference(fields, orders, metric, face_turn, migration):
    derive_t, to_t, from_t, lift_t, last_t, active_t = build_tables(PMIN, PMAX)
    elements = GX * GY
    levels = jnp.arange(NORD, dtype=jnp.int32) + PMIN
    one_hot = (orders.reshape(elements)[:, None] == levels[None, :]).astype(jnp.float32)
    params = (select_rows(one_hot, derive_t), select_rows(one_hot, to_t), select_rows(one_hot, from_t),
              select_rows(one_hot, lift_t), select_rows(one_hot, last_t), jnp.transpose(metric.reshape(3, elements)))
    active = select_rows(one_hot, active_t)
    node_mask = active[:, :, None, None] * active[:, None, :, None] * active[:, None, None, :]
    volume = fields.reshape(elements, VARS, NQ, NQ, NQ) * node_mask[:, None]

    def apply_operator(current):
        own_faces = own_traces(current, params[4], params[1])
        turned_lo = apply_turn(own_faces[0], face_turn[0].reshape(elements)).reshape(GX, GY, VARS, NQ, NQ)
        turned_hi = apply_turn(own_faces[1], face_turn[1].reshape(elements)).reshape(GX, GY, VARS, NQ, NQ)
        on_grid = [face_vals.reshape(GX, GY, VARS, NQ, NQ) for face_vals in own_faces]
        across = [jnp.roll(turned_hi, 1, axis=0), jnp.roll(turned_lo, -1, axis=0),
                  jnp.concatenate([mirror_normal(on_grid[2][:, :1], 1), on_grid[3][:, :-1]], axis=1),
                  jnp.concatenate([on_grid[2][:, 1:], jnp.zeros_like(on_grid[2][:, :1])], axis=1),
                  on_grid[5], on_grid[4]]
        by_rows = jax.tree.map(lambda leaf_arr: leaf_arr.reshape((GX, GY) + leaf_arr.shape[1:]), (current, params, own_faces))
        result = lax.map(lambda pieces: element_rates(pieces[0], pieces[1], pieces[2], pieces[3]), by_rows + (across,))
        return result.reshape(elements, VARS, NQ, NQ, NQ)

    first_rate = apply_operator(volume)
    middle = volume + time_step * first_rate
    second = apply_operator(middle)
    change = (0.5 * time_step) * (first_rate + second)
    flat_rows = change.reshape(N_BLK, LX, N_ROW, LY, VARS * NODES).transpose(0, 2, 1, 3, 4).reshape(N_BLK, N_ROW, NB, VARS * NODES)
    buffers = pack_slots(flat_rows, migration[..., 0])
    pieces = [jnp.roll(buffers[:, :, position], position - REACH, axis=0) for position in range(SPREAD)]
    return jnp.stack(pieces, axis=2).reshape(N_BLK, N_ROW, SPREAD * CAP, VARS, NODES)
```

```python
import functools

import jax
import jax.numpy as jnp
import numpy as np
from jax import lax
from jax.experimental import pallas as pl
from jax.experimental.pallas import tpu as pltpu
from jax.sharding import PartitionSpec as P

PMAX = 7
PMIN = 3
VARS = 5
NQ = 8
NB = 16
SPREAD = 5
CAP = 5
LANES = 128

mean_flow = (0.4, 0.0, 0.2)
time_step = 0.008


def legendre_points(degree):
    point_count = degree + 1
    estimate = np.cos(np.pi * np.arange(point_count) / degree)
    for sweep_idx in range(40):
        values = np.zeros((point_count, point_count))
        values[:, 0] = 1.0
        values[:, 1] = estimate
        for order_idx in range(2, point_count):
            values[:, order_idx] = (
                (2 * order_idx - 1) * estimate * values[:, order_idx - 1]
                - (order_idx - 1) * values[:, order_idx - 2]
            ) / order_idx
        estimate = estimate - (estimate * values[:, degree] - values[:, degree - 1]) / (
            point_count * values[:, degree]
        )
    return np.sort(estimate)


def lagrange_matrix(points, targets):
    result = np.ones((len(targets), len(points)))
    for column in range(len(points)):
        for other_idx in range(len(points)):
            if other_idx != column:
                result[:, column] *= (targets - points[other_idx]) / (
                    points[column] - points[other_idx]
                )
    return result


def build_tables(lowest, highest):
    node_count = highest + 1
    level_count = highest - lowest + 1
    common = legendre_points(highest)
    derive = np.zeros((level_count, node_count, node_count))
    to_grid = np.zeros((level_count, node_count, node_count))
    from_grid = np.zeros((level_count, node_count, node_count))
    lifting = np.zeros((level_count,))
    last_node = np.zeros((level_count, node_count))
    active = np.zeros((level_count, node_count))
    for level_idx in range(level_count):
        degree = lowest + level_idx
        points = legendre_points(degree)
        filled = degree + 1
        weights = np.array(
            [
                1.0
                / np.prod(
                    [
                        points[column] - points[other_idx]
                        for other_idx in range(filled)
                        if other_idx != column
                    ]
                )
                for column in range(filled)
            ]
        )
        local_diff = np.zeros((filled, filled))
        for row_idx in range(filled):
            for column in range(filled):
                if column != row_idx:
                    local_diff[row_idx, column] = (
                        weights[column] / weights[row_idx] / (points[row_idx] - points[column])
                    )
            local_diff[row_idx, row_idx] = -np.sum(local_diff[row_idx])
        derive[level_idx, :filled, :filled] = local_diff
        to_grid[level_idx, :, :filled] = lagrange_matrix(points, common)
        from_grid[level_idx, :filled, :] = lagrange_matrix(common, points)
        lifting[level_idx] = degree * (degree + 1) / 2.0
        last_node[level_idx, degree] = 1.0
        active[level_idx, :filled] = 1.0
    return derive, to_grid, from_grid, lifting, last_node, active


D_AT, DK_AT, I_AT, IK_AT, B_AT, BK_AT, W_AT, A_AT, LIFT_AT = (
    0, 64, 128, 192, 256, 320, 384, 392, 400)
TAB_ROWS = 408


def table_rows():
    derive, to_grid, from_grid, lifting, last_node, active = build_tables(PMIN, PMAX)
    rows = np.zeros((TAB_ROWS, LANES))
    for level in range(PMAX - PMIN + 1):
        for at, turned_at, mat in (
            (D_AT, DK_AT, derive[level]),
            (I_AT, IK_AT, to_grid[level]),
            (B_AT, BK_AT, from_grid[level]),
        ):
            rows[at : at + 64, level] = mat.reshape(-1)
            for turn in range(8):
                for a in range(8):
                    rows[turned_at + turn * 8 + a, level] = mat[a, (a + turn) % 8]
        rows[W_AT : W_AT + 8, level] = last_node[level]
        rows[A_AT : A_AT + 8, level] = active[level]
        rows[LIFT_AT : LIFT_AT + 8, level] = lifting[level]
    return rows.astype(np.float32)


def lane_ids():
    lane = lax.broadcasted_iota(jnp.int32, (8, LANES), 1)
    return lane, lane & 15, lane >> 4


def spread(read, dtype):
    _, elem, _ = lane_ids()
    out = jnp.zeros((8, LANES), dtype)
    for e in range(NB):
        out = jnp.where(elem == e, read(e // 4, e % 4), out)
    return out


def rolled(x, by):
    return pltpu.roll(x, by % LANES, 1)


def subrolled(x, by):
    return x if by % 8 == 0 else pltpu.roll(x, by % 8, 0)


def row_of(ref, at):
    return jnp.broadcast_to(ref[pl.ds(at, 1), :], (8, LANES))


def along_first(tab, at, face):
    out = []
    for a in range(8):
        total = row_of(tab, at + a * 8) * face[0]
        for j in range(1, 8):
            total = total + row_of(tab, at + a * 8 + j) * face[j]
        out.append(total)
    return out


def along_second(tab, at, face):
    coefs = [tab[pl.ds(at + 8 * turn, 8), :] for turn in range(8)]
    out = []
    for x in face:
        total = coefs[0] * x
        for turn in range(1, 8):
            total = total + coefs[turn] * subrolled(x, -turn)
        out.append(total)
    return out


def to_common(tab, face):
    return along_second(tab, IK_AT, along_first(tab, I_AT, face))


def from_common(tab, face):
    return along_second(tab, BK_AT, along_first(tab, B_AT, face))


def turned(face, codes, buf):
    for a in range(8):
        buf[pl.ds(8 * a, 8), :] = face[a]
    back = lax.broadcasted_iota(jnp.int32, (8, LANES), 0) * -1 + 7
    out = []
    for a in range(8):
        x = jnp.where(codes == 1, face[7 - a], face[a])
        x = jnp.where(codes == 2, jnp.take_along_axis(face[a], back, axis=0), x)
        x = jnp.where(codes == 3, buf[pl.ds(a, 8, stride=8), :], x)
        out.append(x)
    return out


def coupling_of(direction):
    lane, elem, var = lane_ids()
    vel = elem + 16 * (1 + direction)
    source = jnp.where((var == 0) | (var == 4), vel, lane)
    source = jnp.where(var == 1 + direction, elem + 64, source)
    has = (var == 0) | (var == 4) | (var == 1 + direction)
    return source, jnp.where(has, 1.0, 0.0).astype(jnp.float32)


def jump_flux(gap, direction, sign):
    source, has = coupling_of(direction)
    speed = abs(mean_flow[direction]) + 1.0
    factor = 0.5 * (mean_flow[direction] + sign * speed)
    half = 0.5 * has
    return [factor * x + half * jnp.take_along_axis(x, source, axis=1) for x in gap]


def load_face(ref):
    return [ref[pl.ds(8 * a, 8), :] for a in range(8)]


def store_face(ref, face):
    for a in range(8):
        ref[pl.ds(8 * a, 8), :] = face[a]


def picked(tab, read):
    out = None
    for n in range(PMIN, NQ):
        w = row_of(tab, W_AT + n)
        layer = [w * x for x in read(n)]
        out = layer if out is None else [s + x for s, x in zip(out, layer)]
    return out


def node(i, j):
    return pl.ds((i * 8 + j) * 8, 8)


def x_faces(q, tab):
    low = [q[node(0, j), :] for j in range(8)]
    high = picked(tab, lambda n: [q[node(n, j), :] for j in range(8)])
    return low, high


def y_faces(q, tab):
    low = [q[node(i, 0), :] for i in range(8)]
    high = picked(tab, lambda n: [q[node(i, n), :] for i in range(8)])
    return low, high


def z_faces(q, tab):
    low = [q[pl.ds(i * 64, 8, stride=8), :] for i in range(8)]
    high = picked(tab, lambda n: [q[pl.ds(i * 64 + n, 8, stride=8), :] for i in range(8)])
    return low, high


def make_traces(q, tab, code_low, code_high, outs, buf):
    tx_low, tx_high, ty_low, ty_high, right, left, up, down = outs
    low, high = x_faces(q, tab)
    face = turned(to_common(tab, low), code_low, buf)
    store_face(tx_low, face)
    store_face(left, [rolled(x, 12) for x in face])
    face = turned(to_common(tab, high), code_high, buf)
    store_face(tx_high, face)
    store_face(right, [rolled(x, -12) for x in face])
    low, high = y_faces(q, tab)
    face = to_common(tab, low)
    store_face(ty_low, face)
    store_face(down, [rolled(x, 3) for x in face])
    face = to_common(tab, high)
    store_face(ty_high, face)
    store_face(up, [rolled(x, -3) for x in face])


def gaps_to(q, tab, lift, traces, arrived, wall, metric, out):
    tx_low, tx_high, ty_low, ty_high = traces
    from_left, from_right, from_below, from_above = arrived
    _, elem, var = lane_ids()
    scale = lift * metric[0]
    low, high = x_faces(q, tab)
    near = [
        jnp.where(elem < 4, r, rolled(t, 4))
        for r, t in zip(load_face(from_left), load_face(tx_high))
    ]
    gap = jump_flux([n - o for n, o in zip(from_common(tab, near), low)], 0, 1.0)
    for j in range(8):
        out[node(0, j), :] = out[node(0, j), :] + scale * gap[j]
    near = [
        jnp.where(elem >= 12, r, rolled(t, -4))
        for r, t in zip(load_face(from_right), load_face(tx_low))
    ]
    gap = jump_flux([n - o for n, o in zip(from_common(tab, near), high)], 0, -1.0)
    gap = [scale * x for x in gap]
    for n in range(PMIN, NQ):
        w = row_of(tab, W_AT + n)
        for j in range(8):
            out[node(n, j), :] = out[node(n, j), :] - w * gap[j]
    scale = lift * metric[1]
    low, high = y_faces(q, tab)
    own_low = load_face(ty_low)
    flip = jnp.where(var == 2, -1.0, 1.0).astype(jnp.float32)
    first = (elem & 3) == 0
    near = [
        jnp.where(first, jnp.where(wall, flip * o, r), rolled(t, 1))
        for r, t, o in zip(load_face(from_below), load_face(ty_high), own_low)
    ]
    gap = jump_flux([n - o for n, o in zip(from_common(tab, near), low)], 1, 1.0)
    for i in range(8):
        out[node(i, 0), :] = out[node(i, 0), :] + scale * gap[i]
    near = [
        jnp.where((elem & 3) == 3, r, rolled(t, -1))
        for r, t in zip(load_face(from_above), own_low)
    ]
    gap = jump_flux([n - o for n, o in zip(from_common(tab, near), high)], 1, -1.0)
    gap = [scale * x for x in gap]
    for n in range(PMIN, NQ):
        w = row_of(tab, W_AT + n)
        for i in range(8):
            out[node(i, n), :] = out[node(i, n), :] - w * gap[i]
    scale = lift * metric[2]
    low, high = z_faces(q, tab)
    gap_low = jump_flux([h - o for h, o in zip(high, low)], 2, 1.0)
    gap_high = jump_flux([o - h for h, o in zip(high, low)], 2, -1.0)
    sub = lax.broadcasted_iota(jnp.int32, (8, LANES), 0)
    at_low = jnp.where(sub == 0, scale, 0.0)
    at_high = -scale * tab[pl.ds(W_AT, 8), :]
    for i in range(8):
        for j in range(8):
            pick = jnp.full((8, LANES), j, jnp.int32)
            lo = jnp.take_along_axis(gap_low[i], pick, axis=0)
            hi = jnp.take_along_axis(gap_high[i], pick, axis=0)
            out[node(i, j), :] = out[node(i, j), :] + at_low * lo + at_high * hi


def volume_terms(q, tab, metric, out):
    couplings = [coupling_of(d) for d in range(3)]

    def flux(x, d):
        source, has = couplings[d]
        y = metric[d] * x
        mixed = has * jnp.take_along_axis(y, source, axis=1)
        return mixed if mean_flow[d] == 0.0 else mean_flow[d] * y + mixed

    def along_x(j, carry):
        face = [q[node(i, j), :] for i in range(8)]
        for i, x in enumerate(along_first(tab, D_AT, face)):
            out[node(i, j), :] = -flux(x, 0)
        return carry

    lax.fori_loop(0, 8, along_x, 0)

    def along_yz(i, carry):
        face = [q[node(i, j), :] for j in range(8)]
        by_y = along_first(tab, D_AT, face)
        by_z = along_second(tab, DK_AT, face)
        for j in range(8):
            out[node(i, j), :] = out[node(i, j), :] - (flux(by_y[j], 1) + flux(by_z[j], 2))
        return carry

    lax.fori_loop(0, 8, along_yz, 0)


def all_metrics(metric_ref):
    return [spread(lambda x, y, d=d: metric_ref[d, x, y], jnp.float32) for d in range(3)]


def all_codes(turn_ref):
    return [spread(lambda x, y, s=s: turn_ref[s, x, y], jnp.int32) for s in range(2)]


def first_kernel(fields, orders, turn, rows, q, tab, *rest):
    outs, flat, buf = rest[:8], rest[8], rest[9]
    order = spread(lambda x, y: orders[x, y], jnp.int32)
    level = lax.broadcasted_iota(jnp.int32, (LANES, LANES), 0) + PMIN
    one_hot = jnp.where(
        level == jnp.broadcast_to(order[0:1, :], (LANES, LANES)), 1.0, 0.0
    ).astype(jnp.float32)
    tab[...] = jnp.dot(
        rows[...], one_hot, precision=lax.Precision.HIGHEST, preferred_element_type=jnp.float32
    )
    flat[pl.ds(80, 48), :] = jnp.zeros((48, 512), jnp.float32)
    for v in range(VARS):
        for x in range(4):
            flat[pl.ds(v * 16 + x * 4, 4), :] = fields[x, v]
    in_k = tab[pl.ds(A_AT, 8), :]
    for part in range(4):
        block = flat[:, pl.ds(part * LANES, LANES)].T
        for half in range(2):
            in_ik = in_k * row_of(tab, A_AT + part * 2 + half)
            for j in range(8):
                at = (half * 8 + j) * 8
                q[node(part * 2 + half, j), :] = (
                    block[at : at + 8] * in_ik * row_of(tab, A_AT + j)
                )
    code_low, code_high = all_codes(turn)
    make_traces(q, tab, code_low, code_high, outs, buf)


def second_kernel(q, tab, metric_ref, turn, wall_ref, *rest):
    traces, arrived = rest[:4], rest[4:8]
    rate, middle = rest[8], rest[9]
    outs, buf = rest[10:18], rest[18]
    metric = all_metrics(metric_ref)
    lift = tab[pl.ds(LIFT_AT, 8), :]
    volume_terms(q, tab, metric, rate)
    gaps_to(q, tab, lift, traces, arrived, wall_ref[0] == 0, metric, rate)
    for n in range(64):
        at = pl.ds(8 * n, 8)
        middle[at, :] = q[at, :] + time_step * rate[at, :]
    code_low, code_high = all_codes(turn)
    make_traces(middle, tab, code_low, code_high, outs, buf)


def third_kernel(rate, middle, tab, metric_ref, migration, wall_ref, *rest):
    traces, arrived = rest[:4], rest[4:8]
    outs = rest[8:13]
    second, flat, slots, count = rest[13:]
    metric = all_metrics(metric_ref)
    lift = tab[pl.ds(LIFT_AT, 8), :]
    volume_terms(middle, tab, metric, second)
    gaps_to(middle, tab, lift, traces, arrived, wall_ref[0] == 0, metric, second)
    for part in range(4):
        at = pl.ds(part * LANES, LANES)
        flat[at, :] = ((0.5 * time_step) * (rate[at, :] + second[at, :])).T
    slots[...] = jnp.zeros_like(slots)
    for m in range(SPREAD):
        count[m] = 0
    for e in range(NB):
        m = migration[0, 0, e, 0]
        c = count[m]
        count[m] = c + 1
        row = m * 104 + c * 20
        for part in range(4):
            slots[pl.ds(row + part, VARS, stride=4), :] = flat[
                pl.ds(part * LANES + e, VARS, stride=16), :
            ]
    for m in range(SPREAD):
        outs[m][...] = slots[pl.ds(m * 104, 100), :]


def last_kernel(*refs):
    out = refs[SPREAD]
    for m in range(SPREAD):
        out[pl.ds(m * 100, 100), :] = refs[m][...]


def f32(*shape):
    return jax.ShapeDtypeStruct(shape, jnp.float32)


VMEM = pl.BlockSpec(memory_space=pltpu.VMEM)
SMEM = pl.BlockSpec(memory_space=pltpu.SMEM)
PARAMS = pltpu.CompilerParams(vmem_limit_bytes=32 * 1024 * 1024)
FACE = f32(64, LANES)
VOLUME = f32(512, LANES)


def shifted(array, axis, by, periodic):
    count = lax.axis_size(axis)
    pairs = [(i, (i + by) % count) for i in range(count) if periodic or 0 <= i + by < count]
    return lax.ppermute(array, axis, pairs)


def exchanged(sends):
    right, left, up, down = sends
    return [
        shifted(right, "blk", 1, True),
        shifted(left, "blk", -1, True),
        shifted(up, "row", 1, False),
        shifted(down, "row", -1, False),
    ]


def local(fields, orders, metric, face_turn, migration):
    by_var = jnp.transpose(fields, (0, 2, 1, 3))
    wall = lax.axis_index("row").astype(jnp.int32).reshape(1)
    rows = jnp.asarray(table_rows())
    q, tab, *faces = pl.pallas_call(
        first_kernel,
        out_shape=[VOLUME, f32(TAB_ROWS, LANES)] + [FACE] * 8,
        in_specs=[VMEM, SMEM, SMEM, VMEM],
        out_specs=[VMEM] * 10,
        scratch_shapes=[pltpu.VMEM((LANES, 512), jnp.float32), pltpu.VMEM((64, LANES), jnp.float32)],
        compiler_params=PARAMS,
    )(by_var, orders, face_turn, rows)
    arrived = exchanged(faces[4:])
    rate, middle, *next_faces = pl.pallas_call(
        second_kernel,
        out_shape=[VOLUME, VOLUME] + [FACE] * 8,
        in_specs=[VMEM, VMEM, SMEM, SMEM, SMEM] + [VMEM] * 8,
        out_specs=[VMEM] * 10,
        scratch_shapes=[pltpu.VMEM((64, LANES), jnp.float32)],
        compiler_params=PARAMS,
    )(q, tab, metric, face_turn, wall, *faces[:4], *arrived)
    arrived = exchanged(next_faces[4:])
    packed = pl.pallas_call(
        third_kernel,
        out_shape=[f32(100, LANES)] * SPREAD,
        in_specs=[VMEM, VMEM, VMEM, SMEM, SMEM, SMEM] + [VMEM] * 8,
        out_specs=[VMEM] * SPREAD,
        scratch_shapes=[
            pltpu.VMEM((512, LANES), jnp.float32),
            pltpu.VMEM((512, LANES), jnp.float32),
            pltpu.VMEM((SPREAD * 104, LANES), jnp.float32),
            pltpu.SMEM((8,), jnp.int32),
        ],
        compiler_params=PARAMS,
    )(rate, middle, tab, metric, migration, wall, *next_faces[:4], *arrived)
    pieces = [
        packed[m] if m == 2 else shifted(packed[m], "blk", m - 2, True) for m in range(SPREAD)
    ]
    moved = pl.pallas_call(
        last_kernel,
        out_shape=f32(500, LANES),
        in_specs=[VMEM] * SPREAD,
        out_specs=VMEM,
        compiler_params=PARAMS,
    )(*pieces)
    return moved.reshape(1, 1, SPREAD * CAP, VARS, 512)


def solution(mesh):
    placed = (
        P("blk", "row", None, None),
        P("blk", "row"),
        P(None, "blk", "row"),
        P(None, "blk", "row"),
        P("blk", "row", None, None),
    )
    return jax.shard_map(
        local,
        mesh=mesh,
        in_specs=placed,
        out_specs=P("blk", "row", None, None, None),
        check_vma=False,
    )
```

```python
import functools

import jax
import jax.numpy as jnp
import numpy as np
from jax import lax
from jax.experimental import pallas as pl
from jax.experimental.pallas import tpu as pltpu
from jax.sharding import PartitionSpec as P

PMAX = 7
PMIN = 3
VARS = 5
NQ = 8
NB = 16
SPREAD = 5
CAP = 5
LANES = 128

mean_flow = (0.4, 0.0, 0.2)
time_step = 0.008


def legendre_points(degree):
    point_count = degree + 1
    estimate = np.cos(np.pi * np.arange(point_count) / degree)
    for sweep_idx in range(40):
        values = np.zeros((point_count, point_count))
        values[:, 0] = 1.0
        values[:, 1] = estimate
        for order_idx in range(2, point_count):
            values[:, order_idx] = (
                (2 * order_idx - 1) * estimate * values[:, order_idx - 1]
                - (order_idx - 1) * values[:, order_idx - 2]
            ) / order_idx
        estimate = estimate - (estimate * values[:, degree] - values[:, degree - 1]) / (
            point_count * values[:, degree]
        )
    return np.sort(estimate)


def lagrange_matrix(points, targets):
    result = np.ones((len(targets), len(points)))
    for column in range(len(points)):
        for other_idx in range(len(points)):
            if other_idx != column:
                result[:, column] *= (targets - points[other_idx]) / (
                    points[column] - points[other_idx]
                )
    return result


def build_tables(lowest, highest):
    node_count = highest + 1
    level_count = highest - lowest + 1
    common = legendre_points(highest)
    derive = np.zeros((level_count, node_count, node_count))
    to_grid = np.zeros((level_count, node_count, node_count))
    from_grid = np.zeros((level_count, node_count, node_count))
    lifting = np.zeros((level_count,))
    last_node = np.zeros((level_count, node_count))
    active = np.zeros((level_count, node_count))
    for level_idx in range(level_count):
        degree = lowest + level_idx
        points = legendre_points(degree)
        filled = degree + 1
        weights = np.array(
            [
                1.0
                / np.prod(
                    [
                        points[column] - points[other_idx]
                        for other_idx in range(filled)
                        if other_idx != column
                    ]
                )
                for column in range(filled)
            ]
        )
        local_diff = np.zeros((filled, filled))
        for row_idx in range(filled):
            for column in range(filled):
                if column != row_idx:
                    local_diff[row_idx, column] = (
                        weights[column] / weights[row_idx] / (points[row_idx] - points[column])
                    )
            local_diff[row_idx, row_idx] = -np.sum(local_diff[row_idx])
        derive[level_idx, :filled, :filled] = local_diff
        to_grid[level_idx, :, :filled] = lagrange_matrix(points, common)
        from_grid[level_idx, :filled, :] = lagrange_matrix(common, points)
        lifting[level_idx] = degree * (degree + 1) / 2.0
        last_node[level_idx, degree] = 1.0
        active[level_idx, :filled] = 1.0
    return derive, to_grid, from_grid, lifting, last_node, active


D_AT, DK_AT, I_AT, IK_AT, B_AT, BK_AT, W_AT, A_AT, LIFT_AT = (
    0, 64, 128, 192, 256, 320, 384, 392, 400)
TAB_ROWS = 408


def table_rows():
    derive, to_grid, from_grid, lifting, last_node, active = build_tables(PMIN, PMAX)
    rows = np.zeros((TAB_ROWS, LANES))
    for level in range(PMAX - PMIN + 1):
        for at, turned_at, mat in (
            (D_AT, DK_AT, derive[level]),
            (I_AT, IK_AT, to_grid[level]),
            (B_AT, BK_AT, from_grid[level]),
        ):
            rows[at : at + 64, level] = mat.reshape(-1)
            for turn in range(8):
                for a in range(8):
                    rows[turned_at + turn * 8 + a, level] = mat[a, (a + turn) % 8]
        rows[W_AT : W_AT + 8, level] = last_node[level]
        rows[A_AT : A_AT + 8, level] = active[level]
        rows[LIFT_AT : LIFT_AT + 8, level] = lifting[level]
    return rows.astype(np.float32)


def lane_ids():
    lane = lax.broadcasted_iota(jnp.int32, (8, LANES), 1)
    return lane, lane & 15, lane >> 4


def spread(read, dtype):
    _, elem, _ = lane_ids()
    out = jnp.zeros((8, LANES), dtype)
    for e in range(NB):
        out = jnp.where(elem == e, read(e // 4, e % 4), out)
    return out


def rolled(x, by):
    return pltpu.roll(x, by % LANES, 1)


def subrolled(x, by):
    return x if by % 8 == 0 else pltpu.roll(x, by % 8, 0)


def row_of(ref, at):
    return jnp.broadcast_to(ref[pl.ds(at, 1), :], (8, LANES))


def along_first(tab, at, face):
    out = []
    for a in range(8):
        total = row_of(tab, at + a * 8) * face[0]
        for j in range(1, 8):
            total = total + row_of(tab, at + a * 8 + j) * face[j]
        out.append(total)
    return out


def along_second(tab, at, face):
    coefs = [tab[pl.ds(at + 8 * turn, 8), :] for turn in range(8)]
    out = []
    for x in face:
        total = coefs[0] * x
        for turn in range(1, 8):
            total = total + coefs[turn] * subrolled(x, -turn)
        out.append(total)
    return out


def to_common(tab, face):
    return along_second(tab, IK_AT, along_first(tab, I_AT, face))


def from_common(tab, face):
    return along_second(tab, BK_AT, along_first(tab, B_AT, face))


def turned(face, codes, buf):
    for a in range(8):
        buf[pl.ds(8 * a, 8), :] = face[a]
    back = lax.broadcasted_iota(jnp.int32, (8, LANES), 0) * -1 + 7
    out = []
    for a in range(8):
        x = jnp.where(codes == 1, face[7 - a], face[a])
        x = jnp.where(codes == 2, jnp.take_along_axis(face[a], back, axis=0), x)
        x = jnp.where(codes == 3, buf[pl.ds(a, 8, stride=8), :], x)
        out.append(x)
    return out


def coupling_of(direction):
    lane, elem, var = lane_ids()
    vel = elem + 16 * (1 + direction)
    source = jnp.where((var == 0) | (var == 4), vel, lane)
    source = jnp.where(var == 1 + direction, elem + 64, source)
    has = (var == 0) | (var == 4) | (var == 1 + direction)
    return source, jnp.where(has, 1.0, 0.0).astype(jnp.float32)


def jump_flux(gap, direction, sign):
    source, has = coupling_of(direction)
    speed = abs(mean_flow[direction]) + 1.0
    factor = 0.5 * (mean_flow[direction] + sign * speed)
    half = 0.5 * has
    return [factor * x + half * jnp.take_along_axis(x, source, axis=1) for x in gap]


def load_face(ref):
    return [ref[pl.ds(8 * a, 8), :] for a in range(8)]


def store_face(ref, face):
    for a in range(8):
        ref[pl.ds(8 * a, 8), :] = face[a]


def picked(tab, read):
    out = None
    for n in range(PMIN, NQ):
        w = row_of(tab, W_AT + n)
        layer = [w * x for x in read(n)]
        out = layer if out is None else [s + x for s, x in zip(out, layer)]
    return out


def node(i, j):
    return pl.ds((i * 8 + j) * 8, 8)


def x_faces(q, tab):
    low = [q[node(0, j), :] for j in range(8)]
    high = picked(tab, lambda n: [q[node(n, j), :] for j in range(8)])
    return low, high


def y_faces(q, tab):
    low = [q[node(i, 0), :] for i in range(8)]
    high = picked(tab, lambda n: [q[node(i, n), :] for i in range(8)])
    return low, high


def z_faces(q, tab):
    low = [q[pl.ds(i * 64, 8, stride=8), :] for i in range(8)]
    high = picked(tab, lambda n: [q[pl.ds(i * 64 + n, 8, stride=8), :] for i in range(8)])
    return low, high


def make_traces(q, tab, code_low, code_high, place, outs, buf):
    tx_low, tx_high, ty_low, ty_high, chip_send, blk_send, pair_send, row_send = outs
    first_core, even_row = place
    low, high = x_faces(q, tab)
    low = turned(to_common(tab, low), code_low, buf)
    store_face(tx_low, low)
    high = turned(to_common(tab, high), code_high, buf)
    store_face(tx_high, high)
    low = [rolled(x, 12) for x in low]
    high = [rolled(x, -12) for x in high]
    store_face(chip_send, [jnp.where(first_core, h, l) for l, h in zip(low, high)])
    store_face(blk_send, [jnp.where(first_core, l, h) for l, h in zip(low, high)])
    low, high = y_faces(q, tab)
    low = to_common(tab, low)
    store_face(ty_low, low)
    high = to_common(tab, high)
    store_face(ty_high, high)
    low = [rolled(x, 3) for x in low]
    high = [rolled(x, -3) for x in high]
    store_face(pair_send, [jnp.where(even_row, h, l) for l, h in zip(low, high)])
    store_face(row_send, [jnp.where(even_row, l, h) for l, h in zip(low, high)])


def sorted_arrivals(arrived, place):
    chip, blk, pair, row = arrived
    first_core, even_row = place
    chip = load_face(chip.at[jnp.where(first_core, 1, 0)])
    pair = load_face(pair.at[jnp.where(even_row, 1, 0)])
    blk, row = load_face(blk), load_face(row)

    def pick(cond, a, b):
        return [jnp.where(cond, x, y) for x, y in zip(a, b)]

    return (
        pick(first_core, blk, chip),
        pick(first_core, chip, blk),
        pick(even_row, row, pair),
        pick(even_row, pair, row),
    )


def places(core_ref, row_ref):
    return core_ref[0] == 0, lax.rem(row_ref[0], 2) == 0


def gaps_to(q, tab, lift, traces, arrived, wall, metric, out):
    tx_low, tx_high, ty_low, ty_high = traces
    from_left, from_right, from_below, from_above = arrived
    _, elem, var = lane_ids()
    scale = lift * metric[0]
    low, high = x_faces(q, tab)
    near = [
        jnp.where(elem < 4, r, rolled(t, 4))
        for r, t in zip(from_left, load_face(tx_high))
    ]
    gap = jump_flux([n - o for n, o in zip(from_common(tab, near), low)], 0, 1.0)
    for j in range(8):
        out[node(0, j), :] = out[node(0, j), :] + scale * gap[j]
    near = [
        jnp.where(elem >= 12, r, rolled(t, -4))
        for r, t in zip(from_right, load_face(tx_low))
    ]
    gap = jump_flux([n - o for n, o in zip(from_common(tab, near), high)], 0, -1.0)
    gap = [scale * x for x in gap]
    for n in range(PMIN, NQ):
        w = row_of(tab, W_AT + n)
        for j in range(8):
            out[node(n, j), :] = out[node(n, j), :] - w * gap[j]
    scale = lift * metric[1]
    low, high = y_faces(q, tab)
    own_low = load_face(ty_low)
    flip = jnp.where(var == 2, -1.0, 1.0).astype(jnp.float32)
    first = (elem & 3) == 0
    near = [
        jnp.where(first, jnp.where(wall, flip * o, r), rolled(t, 1))
        for r, t, o in zip(from_below, load_face(ty_high), own_low)
    ]
    gap = jump_flux([n - o for n, o in zip(from_common(tab, near), low)], 1, 1.0)
    for i in range(8):
        out[node(i, 0), :] = out[node(i, 0), :] + scale * gap[i]
    near = [
        jnp.where((elem & 3) == 3, r, rolled(t, -1))
        for r, t in zip(from_above, own_low)
    ]
    gap = jump_flux([n - o for n, o in zip(from_common(tab, near), high)], 1, -1.0)
    gap = [scale * x for x in gap]
    for n in range(PMIN, NQ):
        w = row_of(tab, W_AT + n)
        for i in range(8):
            out[node(i, n), :] = out[node(i, n), :] - w * gap[i]
    scale = lift * metric[2]
    low, high = z_faces(q, tab)
    gap_low = jump_flux([h - o for h, o in zip(high, low)], 2, 1.0)
    gap_high = jump_flux([o - h for h, o in zip(high, low)], 2, -1.0)
    sub = lax.broadcasted_iota(jnp.int32, (8, LANES), 0)
    at_low = jnp.where(sub == 0, scale, 0.0)
    at_high = -scale * tab[pl.ds(W_AT, 8), :]
    for i in range(8):
        for j in range(8):
            pick = jnp.full((8, LANES), j, jnp.int32)
            lo = jnp.take_along_axis(gap_low[i], pick, axis=0)
            hi = jnp.take_along_axis(gap_high[i], pick, axis=0)
            out[node(i, j), :] = out[node(i, j), :] + at_low * lo + at_high * hi


def volume_terms(q, tab, metric, out):
    couplings = [coupling_of(d) for d in range(3)]

    def flux(x, d):
        source, has = couplings[d]
        y = metric[d] * x
        mixed = has * jnp.take_along_axis(y, source, axis=1)
        return mixed if mean_flow[d] == 0.0 else mean_flow[d] * y + mixed

    def along_x(j, carry):
        face = [q[node(i, j), :] for i in range(8)]
        for i, x in enumerate(along_first(tab, D_AT, face)):
            out[node(i, j), :] = -flux(x, 0)
        return carry

    lax.fori_loop(0, 8, along_x, 0)

    def along_yz(i, carry):
        face = [q[node(i, j), :] for j in range(8)]
        by_y = along_first(tab, D_AT, face)
        by_z = along_second(tab, DK_AT, face)
        for j in range(8):
            out[node(i, j), :] = out[node(i, j), :] - (flux(by_y[j], 1) + flux(by_z[j], 2))
        return carry

    lax.fori_loop(0, 8, along_yz, 0)


def all_metrics(metric_ref):
    return [spread(lambda x, y, d=d: metric_ref[d, x, y], jnp.float32) for d in range(3)]


def all_codes(turn_ref):
    return [spread(lambda x, y, s=s: turn_ref[s, x, y], jnp.int32) for s in range(2)]


def fetched(pairs, sems):
    copies = [pltpu.make_async_copy(a, b, sems.at[n]) for n, (a, b) in enumerate(pairs)]
    for copy in copies:
        copy.start()
    return copies


def first_kernel(fields_hbm, orders_hbm, turn_hbm, rows_hbm, core_ref, row_ref, q, tab, *rest):
    outs = rest[:8]
    flat, buf, fields, orders, turn, rows, sems = rest[8:]
    copies = fetched(
        [(orders_hbm, orders), (turn_hbm, turn), (rows_hbm, rows), (fields_hbm, fields)], sems
    )
    flat[pl.ds(80, 48), :] = jnp.zeros((48, 512), jnp.float32)
    copies[0].wait()
    copies[1].wait()
    order = spread(lambda x, y: orders[x, y], jnp.int32)
    level = lax.broadcasted_iota(jnp.int32, (LANES, LANES), 0) + PMIN
    one_hot = jnp.where(
        level == jnp.broadcast_to(order[0:1, :], (LANES, LANES)), 1.0, 0.0
    ).astype(jnp.float32)
    copies[2].wait()
    tab[...] = jnp.dot(
        rows[...], one_hot, precision=lax.Precision.HIGHEST, preferred_element_type=jnp.float32
    )
    copies[3].wait()
    for v in range(VARS):
        for x in range(4):
            flat[pl.ds(v * 16 + x * 4, 4), :] = fields[x, v]
    in_k = tab[pl.ds(A_AT, 8), :]
    for part in range(4):
        block = flat[:, pl.ds(part * LANES, LANES)].T
        for half in range(2):
            in_ik = in_k * row_of(tab, A_AT + part * 2 + half)
            for j in range(8):
                at = (half * 8 + j) * 8
                q[node(part * 2 + half, j), :] = (
                    block[at : at + 8] * in_ik * row_of(tab, A_AT + j)
                )
    code_low, code_high = all_codes(turn)
    make_traces(q, tab, code_low, code_high, places(core_ref, row_ref), outs, buf)


def second_kernel(q, tab, metric_hbm, turn_hbm, core_ref, row_ref, *rest):
    traces, arrived = rest[:4], rest[4:8]
    rate, middle = rest[8], rest[9]
    outs, buf, metric_ref, turn, sems = rest[10:18], *rest[18:]
    copies = fetched([(metric_hbm, metric_ref), (turn_hbm, turn)], sems)
    place = places(core_ref, row_ref)
    copies[0].wait()
    copies[1].wait()
    metric = all_metrics(metric_ref)
    lift = tab[pl.ds(LIFT_AT, 8), :]
    volume_terms(q, tab, metric, rate)
    gaps_to(
        q, tab, lift, traces, sorted_arrivals(arrived, place), row_ref[0] == 0, metric, rate
    )
    for n in range(64):
        at = pl.ds(8 * n, 8)
        middle[at, :] = q[at, :] + time_step * rate[at, :]
    code_low, code_high = all_codes(turn)
    make_traces(middle, tab, code_low, code_high, place, outs, buf)


def third_kernel(rate, middle, tab, metric_hbm, migration_hbm, core_ref, row_ref, *rest):
    traces, arrived = rest[:4], rest[4:8]
    outs = rest[8:12]
    second, flat, slots, count, metric_ref, migration, sems = rest[12:]
    copies = fetched([(metric_hbm, metric_ref), (migration_hbm, migration)], sems)
    place = places(core_ref, row_ref)
    copies[0].wait()
    copies[1].wait()
    metric = all_metrics(metric_ref)
    lift = tab[pl.ds(LIFT_AT, 8), :]
    volume_terms(middle, tab, metric, second)
    gaps_to(
        middle, tab, lift, traces, sorted_arrivals(arrived, place), row_ref[0] == 0, metric, second
    )
    for part in range(4):
        at = pl.ds(part * LANES, LANES)
        flat[:, 0, at] = ((0.5 * time_step) * (rate[at, :] + second[at, :])).T
    slots[...] = jnp.zeros_like(slots)
    for m in range(SPREAD):
        count[m] = 0
    for e in range(NB):
        m = migration[0, 0, 0, e]
        c = count[m]
        count[m] = c + 1
        slot = jnp.where(core_ref[0] == 0, m, SPREAD - 1 - m) * CAP + c
        for v in range(VARS):
            slots[slot, v] = flat[v * 16 + e]
    at = 0
    for out in outs:
        size = out.shape[0]
        out[...] = slots[pl.ds(at, size)]
        at += size


def last_kernel(far, own, near, core_ref, chip, relayed, out, sems):
    def put(groups):
        copies = [
            pltpu.make_async_copy(piece, out.at[pl.ds(m * CAP, CAP)], sems.at[m])
            for m, piece in enumerate(groups)
        ]
        for copy in copies:
            copy.start()
        for copy in copies:
            copy.wait()

    first = far.at[pl.ds(0, CAP)]

    @pl.when(core_ref[0] == 0)
    def _():
        put([first, chip.at[1], own, relayed.at[1, pl.ds(CAP, CAP)], near])

    @pl.when(core_ref[0] != 0)
    def _():
        put([near, relayed.at[0, pl.ds(CAP, CAP)], own, chip.at[0], first])


def f32(*shape):
    return jax.ShapeDtypeStruct(shape, jnp.float32)


VMEM = pl.BlockSpec(memory_space=pltpu.VMEM)
SMEM = pl.BlockSpec(memory_space=pltpu.SMEM)
HBM = pl.BlockSpec(memory_space=pltpu.HBM)
ANY = pl.BlockSpec(memory_space=pl.ANY)
PARAMS = pltpu.CompilerParams(vmem_limit_bytes=32 * 1024 * 1024)
FACE = f32(64, LANES)
VOLUME = f32(512, LANES)


def pairs_of(count, first):
    return [[n, n + 1] for n in range(first, count - 1, 2)]


def swapped(array, axis, wraps):
    count = lax.axis_size(axis)
    pairs = [(a, b) for a, b in pairs_of(count, 1)]
    if wraps:
        pairs.append((count - 1, 0))
    return lax.ppermute(array, axis, pairs + [(b, a) for a, b in pairs])


def paired(array, axis):
    return lax.all_gather(array, axis, axis_index_groups=pairs_of(lax.axis_size(axis), 0))


def exchanged(sends):
    chip, blk, pair, row = sends
    blk = swapped(blk, "blk", True)
    row = swapped(row, "row", False)
    return [paired(chip, "blk"), blk, paired(pair, "row"), row]


def hopped(array, outward):
    count = lax.axis_size("blk")
    step = [-2, 2] if outward else [2, -2]
    return lax.ppermute(array, "blk", [(n, (n + step[n % 2]) % count) for n in range(count)])


def vmem(*shape):
    return pltpu.VMEM(shape, jnp.float32)


def sems(count):
    return pltpu.SemaphoreType.DMA((count,))


def local(fields, orders, metric, face_turn, migration):
    by_var = jnp.transpose(fields, (0, 2, 1, 3))
    core = lax.rem(lax.axis_index("blk").astype(jnp.int32), 2).reshape(1)
    row = lax.axis_index("row").astype(jnp.int32).reshape(1)
    rows = jnp.asarray(table_rows())
    metric_at = pltpu.SMEM((3, 4, 4), jnp.float32)
    turn_at = pltpu.SMEM((2, 4, 4), jnp.int32)
    q, tab, *faces = pl.pallas_call(
        first_kernel,
        out_shape=[VOLUME, f32(TAB_ROWS, LANES)] + [FACE] * 8,
        in_specs=[HBM] * 4 + [SMEM] * 2,
        out_specs=[VMEM] * 10,
        scratch_shapes=[
            vmem(LANES, 512),
            vmem(64, LANES),
            vmem(4, VARS, 4, 512),
            pltpu.SMEM((4, 4), jnp.int32),
            turn_at,
            vmem(TAB_ROWS, LANES),
            sems(4),
        ],
        compiler_params=PARAMS,
    )(by_var, orders, face_turn, rows, core, row)
    arrived = exchanged(faces[4:])
    rate, middle, *next_faces = pl.pallas_call(
        second_kernel,
        out_shape=[VOLUME, VOLUME] + [FACE] * 8,
        in_specs=[VMEM] * 2 + [HBM] * 2 + [SMEM] * 2 + [VMEM] * 8,
        out_specs=[VMEM] * 10,
        scratch_shapes=[vmem(64, LANES), metric_at, turn_at, sems(2)],
        compiler_params=PARAMS,
    )(q, tab, metric, face_turn, core, row, *faces[:4], *arrived)
    arrived = exchanged(next_faces[4:])
    outward, own, same_chip, inward = pl.pallas_call(
        third_kernel,
        out_shape=[f32(n, VARS, 1, 512) for n in (2 * CAP, CAP, CAP, CAP)],
        in_specs=[VMEM] * 3 + [HBM] * 2 + [SMEM] * 2 + [VMEM] * 8,
        out_specs=[VMEM] * 4,
        scratch_shapes=[
            vmem(512, LANES),
            vmem(LANES, 1, 512),
            vmem(SPREAD * CAP, VARS, 1, 512),
            pltpu.SMEM((8,), jnp.int32),
            metric_at,
            pltpu.SMEM((1, 1, 1, NB), jnp.int32),
            sems(2),
        ],
        compiler_params=PARAMS,
    )(
        rate, middle, tab, metric, jnp.transpose(migration, (0, 1, 3, 2)), core, row,
        *next_faces[:4], *arrived,
    )
    far = hopped(outward, True)
    near = hopped(inward, False)
    chip = paired(same_chip, "blk")
    relayed = paired(far, "blk")
    moved = pl.pallas_call(
        last_kernel,
        out_shape=f32(SPREAD * CAP, VARS, 1, 512),
        in_specs=[ANY] * 3 + [SMEM] + [ANY] * 2,
        out_specs=HBM,
        scratch_shapes=[sems(SPREAD)],
        compiler_params=PARAMS,
    )(far, own, near, core, chip, relayed)
    return jnp.transpose(moved, (2, 0, 1, 3)).reshape(1, 1, SPREAD * CAP, VARS, 512)


def solution(mesh):
    placed = (
        P("blk", "row", None, None),
        P("blk", "row"),
        P(None, "blk", "row"),
        P(None, "blk", "row"),
        P("blk", "row", None, None),
    )
    return jax.shard_map(
        local,
        mesh=mesh,
        in_specs=placed,
        out_specs=P("blk", "row", None, None, None),
        check_vma=False,
    )
```

```python
import functools

import jax
import jax.numpy as jnp
import numpy as np
from jax import lax
from jax.experimental import pallas as pl
from jax.experimental.pallas import tpu as pltpu
from jax.sharding import PartitionSpec as P

PMAX = 7
PMIN = 3
VARS = 5
NQ = 8
NB = 16
SPREAD = 5
CAP = 5
LANES = 128

mean_flow = (0.4, 0.0, 0.2)
time_step = 0.008


def legendre_points(degree):
    point_count = degree + 1
    estimate = np.cos(np.pi * np.arange(point_count) / degree)
    for sweep_idx in range(40):
        values = np.zeros((point_count, point_count))
        values[:, 0] = 1.0
        values[:, 1] = estimate
        for order_idx in range(2, point_count):
            values[:, order_idx] = (
                (2 * order_idx - 1) * estimate * values[:, order_idx - 1]
                - (order_idx - 1) * values[:, order_idx - 2]
            ) / order_idx
        estimate = estimate - (estimate * values[:, degree] - values[:, degree - 1]) / (
            point_count * values[:, degree]
        )
    return np.sort(estimate)


def lagrange_matrix(points, targets):
    result = np.ones((len(targets), len(points)))
    for column in range(len(points)):
        for other_idx in range(len(points)):
            if other_idx != column:
                result[:, column] *= (targets - points[other_idx]) / (
                    points[column] - points[other_idx]
                )
    return result


def build_tables(lowest, highest):
    node_count = highest + 1
    level_count = highest - lowest + 1
    common = legendre_points(highest)
    derive = np.zeros((level_count, node_count, node_count))
    to_grid = np.zeros((level_count, node_count, node_count))
    from_grid = np.zeros((level_count, node_count, node_count))
    lifting = np.zeros((level_count,))
    last_node = np.zeros((level_count, node_count))
    active = np.zeros((level_count, node_count))
    for level_idx in range(level_count):
        degree = lowest + level_idx
        points = legendre_points(degree)
        filled = degree + 1
        weights = np.array(
            [
                1.0
                / np.prod(
                    [
                        points[column] - points[other_idx]
                        for other_idx in range(filled)
                        if other_idx != column
                    ]
                )
                for column in range(filled)
            ]
        )
        local_diff = np.zeros((filled, filled))
        for row_idx in range(filled):
            for column in range(filled):
                if column != row_idx:
                    local_diff[row_idx, column] = (
                        weights[column] / weights[row_idx] / (points[row_idx] - points[column])
                    )
            local_diff[row_idx, row_idx] = -np.sum(local_diff[row_idx])
        derive[level_idx, :filled, :filled] = local_diff
        to_grid[level_idx, :, :filled] = lagrange_matrix(points, common)
        from_grid[level_idx, :filled, :] = lagrange_matrix(common, points)
        lifting[level_idx] = degree * (degree + 1) / 2.0
        last_node[level_idx, degree] = 1.0
        active[level_idx, :filled] = 1.0
    return derive, to_grid, from_grid, lifting, last_node, active


D_AT, DK_AT, I_AT, IK_AT, B_AT, BK_AT, W_AT, A_AT, LIFT_AT, DLAST_AT = (
    0, 64, 128, 192, 256, 320, 384, 392, 400, 408)
TAB_ROWS = 416


def table_rows():
    derive, to_grid, from_grid, lifting, last_node, active = build_tables(PMIN, PMAX)
    rows = np.zeros((TAB_ROWS, LANES))
    for level in range(PMAX - PMIN + 1):
        for at, turned_at, mat in (
            (D_AT, DK_AT, derive[level]),
            (I_AT, IK_AT, to_grid[level]),
            (B_AT, BK_AT, from_grid[level]),
        ):
            rows[at : at + 64, level] = mat.reshape(-1)
            for turn in range(8):
                for a in range(8):
                    rows[turned_at + turn * 8 + a, level] = mat[a, (a + turn) % 8]
        rows[W_AT : W_AT + 8, level] = last_node[level]
        rows[A_AT : A_AT + 8, level] = active[level]
        rows[LIFT_AT : LIFT_AT + 8, level] = lifting[level]
        rows[DLAST_AT : DLAST_AT + 8, level] = derive[level][PMIN + level]
    return rows.astype(np.float32)


def lane_ids():
    lane = lax.broadcasted_iota(jnp.int32, (8, LANES), 1)
    return lane, lane & 15, lane >> 4


def spread(read, dtype):
    _, elem, _ = lane_ids()
    out = jnp.zeros((8, LANES), dtype)
    for e in range(NB):
        out = jnp.where(elem == e, read(e // 4, e % 4), out)
    return out


def rolled(x, by):
    return pltpu.roll(x, by % LANES, 1)


def subrolled(x, by):
    return x if by % 8 == 0 else pltpu.roll(x, by % 8, 0)


def row_of(ref, at):
    return jnp.broadcast_to(ref[pl.ds(at, 1), :], (8, LANES))


def along_first(tab, at, face):
    out = []
    for a in range(8):
        total = row_of(tab, at + a * 8) * face[0]
        for j in range(1, 8):
            total = total + row_of(tab, at + a * 8 + j) * face[j]
        out.append(total)
    return out


def along_second(tab, at, face):
    coefs = [tab[pl.ds(at + 8 * turn, 8), :] for turn in range(8)]
    out = []
    for x in face:
        total = coefs[0] * x
        for turn in range(1, 8):
            total = total + coefs[turn] * subrolled(x, -turn)
        out.append(total)
    return out


def to_common(tab, face):
    return along_second(tab, IK_AT, along_first(tab, I_AT, face))


def from_common(tab, face):
    return along_second(tab, BK_AT, along_first(tab, B_AT, face))


def turned(face, codes, buf):
    for a in range(8):
        buf[pl.ds(8 * a, 8), :] = face[a]
    back = lax.broadcasted_iota(jnp.int32, (8, LANES), 0) * -1 + 7
    out = []
    for a in range(8):
        x = jnp.where(codes == 1, face[7 - a], face[a])
        x = jnp.where(codes == 2, jnp.take_along_axis(face[a], back, axis=0), x)
        x = jnp.where(codes == 3, buf[pl.ds(a, 8, stride=8), :], x)
        out.append(x)
    return out


def coupling_of(direction):
    lane, elem, var = lane_ids()
    vel = elem + 16 * (1 + direction)
    source = jnp.where((var == 0) | (var == 4), vel, lane)
    source = jnp.where(var == 1 + direction, elem + 64, source)
    has = (var == 0) | (var == 4) | (var == 1 + direction)
    return source, jnp.where(has, 1.0, 0.0).astype(jnp.float32)


def jump_with(gap, coupling, factor):
    source, has = coupling
    half = 0.5 * has
    return [factor * x + half * jnp.take_along_axis(x, source, axis=1) for x in gap]


def jump_factor(direction, sign):
    return 0.5 * (mean_flow[direction] + sign * (abs(mean_flow[direction]) + 1.0))


def jump_flux(gap, direction, sign):
    return jump_with(gap, coupling_of(direction), jump_factor(direction, sign))


def load_face(ref):
    return [ref[pl.ds(8 * a, 8), :] for a in range(8)]


def store_face(ref, face):
    for a in range(8):
        ref[pl.ds(8 * a, 8), :] = face[a]


def picked(tab, read):
    out = None
    for n in range(PMIN, NQ):
        w = row_of(tab, W_AT + n)
        layer = [w * x for x in read(n)]
        out = layer if out is None else [s + x for s, x in zip(out, layer)]
    return out


def node(i, j):
    return pl.ds((i * 8 + j) * 8, 8)


def x_faces(q, tab):
    low = [q[node(0, j), :] for j in range(8)]
    high = picked(tab, lambda n: [q[node(n, j), :] for j in range(8)])
    return low, high


def y_faces(q, tab):
    low = [q[node(i, 0), :] for i in range(8)]
    high = picked(tab, lambda n: [q[node(i, n), :] for i in range(8)])
    return low, high


def z_faces(q, tab):
    low = [q[pl.ds(i * 64, 8, stride=8), :] for i in range(8)]
    high = picked(tab, lambda n: [q[pl.ds(i * 64 + n, 8, stride=8), :] for i in range(8)])
    return low, high


def end_rows(q, tab, read):
    low = high = None
    for n in range(NQ):
        first, last = row_of(tab, D_AT + n), row_of(tab, DLAST_AT + n)
        layer = read(n)
        by_low, by_high = [first * x for x in layer], [last * x for x in layer]
        low = by_low if low is None else [a + b for a, b in zip(low, by_low)]
        high = by_high if high is None else [a + b for a, b in zip(high, by_high)]
    return low, high


def packed(kinds, where, shifts):
    out = []
    for a in range(8):
        x = rolled(kinds[3][a], shifts[3])
        for kind in range(3):
            x = jnp.where(where == kind, rolled(kinds[kind][a], shifts[kind]), x)
        out.append(x)
    return out


def make_messages(q, tab, order, metric, codes, first_core, outs, buf):
    tx_low, tx_high, ty_low, ty_high, chip_send, blk_send, up, down = outs
    _, elem, _ = lane_ids()
    x_ends, y_ends = x_faces(q, tab), y_faces(q, tab)
    tx = [turned(to_common(tab, x_ends[side]), codes[side], buf) for side in range(2)]
    ty = [to_common(tab, y_ends[side]) for side in range(2)]
    for ref, face in zip((tx_low, tx_high, ty_low, ty_high), tx + ty):
        store_face(ref, face)
    x_rows = end_rows(q, tab, lambda n: [q[node(n, j), :] for j in range(8)])
    y_rows = end_rows(q, tab, lambda n: [q[node(i, n), :] for i in range(8)])
    params = [order.astype(jnp.float32)] + metric
    zero = jnp.zeros((8, LANES), jnp.float32)

    def along_x(side, shifts):
        edge = 7 * side
        lines = [ty[0][edge], ty[1][edge]] + params + [codes[side].astype(jnp.float32), zero]
        return packed([tx[side], x_ends[side], x_rows[side], lines], elem >> 2, shifts)

    def along_y(side, shifts):
        edge = 7 * side
        lines = [tx[0][edge], tx[1][edge]] + params + [zero, zero]
        return packed([ty[side], y_ends[side], y_rows[side], lines], elem & 3, shifts)

    left = along_x(0, (0, 4, 8, 12))
    right = along_x(1, (-12, -8, -4, 0))
    store_face(chip_send, [jnp.where(first_core, r, l) for l, r in zip(left, right)])
    store_face(blk_send, [jnp.where(first_core, l, r) for l, r in zip(left, right)])
    store_face(down, along_y(0, (0, 1, 2, 3)))
    store_face(up, along_y(1, (-3, -2, -1, 0)))


def sides_of(paired_ref, other_ref, first):
    pair = load_face(paired_ref.at[jnp.where(first, 1, 0)])
    other = load_face(other_ref)
    before = [jnp.where(first, o, p) for o, p in zip(other, pair)]
    after = [jnp.where(first, p, o) for o, p in zip(other, pair)]
    return before, after


def places(core_ref, row_ref):
    return core_ref[0] == 0, lax.rem(row_ref[0], 2) == 0


def halo_step(messages, traces, wall, rows, tab, q_buf):
    left, right, below, above = messages
    lane, elem, var = lane_ids()
    group, pos = elem >> 2, elem & 3
    base = lane - elem
    across_rows = group >= 2
    is_high = (group & 1) == 0

    def collected(block, kind):
        at = base + jnp.where(across_rows, pos * 4 + kind, kind * 4 + pos)
        out = jnp.take_along_axis(left[block], at, axis=1)
        for g, message in ((1, right), (2, below), (3, above)):
            out = jnp.where(group == g, jnp.take_along_axis(message[block], at, axis=1), out)
        return out

    order = collected(2, 3)
    level = lax.broadcasted_iota(jnp.int32, (LANES, LANES), 0) + PMIN
    one_hot = jnp.where(
        level.astype(jnp.float32) == jnp.broadcast_to(order[0:1, :], (LANES, LANES)), 1.0, 0.0
    ).astype(jnp.float32)
    tab[...] = jnp.dot(
        rows, one_hot, precision=lax.Precision.HIGHEST, preferred_element_type=jnp.float32
    )
    lift = tab[pl.ds(LIFT_AT, 8), :]
    metric_x, metric_y, metric_z = [collected(3 + d, 3) for d in range(3)]
    metric_n = jnp.where(across_rows, metric_y, metric_x)
    metric_t = jnp.where(across_rows, metric_x, metric_y)
    codes = jnp.where(across_rows, 0.0, collected(6, 3)).astype(jnp.int32)
    by_x, by_y, by_z = [coupling_of(d) for d in range(3)]

    def mixed(a, b):
        return tuple(jnp.where(across_rows, y, x) for x, y in zip(a, b))

    couple_n, couple_t = mixed(by_x, by_y), mixed(by_y, by_x)

    def factor(d, sign):
        return jnp.float32(jump_factor(d, sign))

    factor_n = jnp.where(
        across_rows,
        jnp.where(is_high, factor(1, -1.0), factor(1, 1.0)),
        jnp.where(is_high, factor(0, -1.0), factor(0, 1.0)),
    )
    factor_t = [
        jnp.where(across_rows, factor(0, sign), factor(1, sign)) for sign in (1.0, -1.0)
    ]
    flow_n = jnp.where(across_rows, mean_flow[1], mean_flow[0])
    flow_t = jnp.where(across_rows, mean_flow[0], mean_flow[1])

    def flux(x, flow, coupling):
        source, has = coupling
        return flow * x + has * jnp.take_along_axis(x, source, axis=1)

    face = [collected(a, 1) for a in range(8)]
    slope = [collected(a, 2) for a in range(8)]
    tx_low, tx_high, ty_low, ty_high = traces
    at = jnp.where(group == 0, pos, jnp.where(group == 1, 12 + pos, 4 * pos))
    at = base + jnp.where(group == 3, 4 * pos + 3, at)
    near = []
    for a in range(8):
        out = jnp.take_along_axis(tx_low[a], at, axis=1)
        for g, trace in ((1, tx_high), (2, ty_low), (3, ty_high)):
            out = jnp.where(group == g, jnp.take_along_axis(trace[a], at, axis=1), out)
        near.append(out)
    gap = [n - f for n, f in zip(from_common(tab, near), face)]
    gap = jump_with(gap, couple_n, factor_n)
    scale = metric_n * lift * jnp.where(is_high, -1.0, 1.0)
    rate = [
        scale * g - metric_n * flux(d, flow_n, couple_n) for g, d in zip(gap, slope)
    ]
    by_t = along_first(tab, D_AT, face)
    by_k = along_second(tab, DK_AT, face)
    scale_z = metric_z * lift
    sub = lax.broadcasted_iota(jnp.int32, (8, LANES), 0)
    weights = tab[pl.ds(W_AT, 8), :]
    at_low = jnp.where(sub == 0, scale_z, 0.0)
    at_high = -scale_z * weights

    def at_k(x, k):
        return jnp.take_along_axis(x, jnp.full((8, LANES), k, jnp.int32), axis=0)

    for a in range(8):
        low = at_k(face[a], 0)
        high = row_of(tab, W_AT + PMIN) * at_k(face[a], PMIN)
        for n in range(PMIN + 1, NQ):
            high = high + row_of(tab, W_AT + n) * at_k(face[a], n)
        gap_low = jump_flux([high - low], 2, 1.0)[0]
        gap_high = jump_flux([low - high], 2, -1.0)[0]
        rate[a] = (
            rate[a]
            - metric_t * flux(by_t[a], flow_t, couple_t)
            - metric_z * flux(by_k[a], mean_flow[2], by_z)
            + at_low * gap_low
            + at_high * gap_high
        )
    line_low, line_high = collected(0, 3), collected(1, 3)
    flip = jnp.where(var == 2, -1.0, 1.0).astype(jnp.float32)

    def corners(side, block_below, block_above):
        at = base + jnp.where(elem == (4 if side == 0 else 7), 15, 3)
        if side == 1:
            at = base + jnp.where(elem == 3, 3, 15)
        return (
            jnp.take_along_axis(below[block_below], at, axis=1),
            jnp.take_along_axis(above[block_above], at, axis=1),
        )

    from_below, _ = corners(0, 7, 7)
    at_wall = jnp.where(wall, flip * line_low, from_below)
    from_below, from_above = corners(0, 6, 6)
    corner = jnp.where(
        across_rows, jnp.where(group == 2, from_below, from_above), at_wall
    )
    near_low = jnp.where(pos == 0, corner, rolled(line_high, 1))
    _, beyond = corners(1, 7, 7)
    from_below, from_above = corners(1, 6, 6)
    corner = jnp.where(across_rows, jnp.where(group == 2, from_below, from_above), beyond)
    near_high = jnp.where(pos == 3, corner, rolled(line_low, -1))
    near_low, near_high = along_second(tab, BK_AT, [near_low, near_high])
    own_high = row_of(tab, W_AT + PMIN) * face[PMIN]
    for n in range(PMIN + 1, NQ):
        own_high = own_high + row_of(tab, W_AT + n) * face[n]
    scale = metric_t * lift
    gap_low = scale * jump_with([near_low - face[0]], couple_t, factor_t[0])[0]
    gap_high = scale * jump_with([near_high - own_high], couple_t, factor_t[1])[0]
    rate[0] = rate[0] + gap_low
    for n in range(PMIN, NQ):
        rate[n] = rate[n] - row_of(tab, W_AT + n) * gap_high
    middle = [f + time_step * r for f, r in zip(face, rate)]
    return turned(to_common(tab, middle), codes, q_buf)


def from_halo(face):
    lane, elem, _ = lane_ids()
    base = lane - elem
    at_below = base + 8 + (elem >> 2)
    at_above = base + 12 + (elem >> 2)
    return (
        face,
        [rolled(x, 8) for x in face],
        [jnp.take_along_axis(x, at_below, axis=1) for x in face],
        [jnp.take_along_axis(x, at_above, axis=1) for x in face],
    )


def gaps_to(q, tab, lift, traces, arrived, wall, metric, out):
    tx_low, tx_high, ty_low, ty_high = traces
    from_left, from_right, from_below, from_above = arrived
    _, elem, var = lane_ids()
    scale = lift * metric[0]
    low, high = x_faces(q, tab)
    near = [
        jnp.where(elem < 4, r, rolled(t, 4))
        for r, t in zip(from_left, tx_high)
    ]
    gap = jump_flux([n - o for n, o in zip(from_common(tab, near), low)], 0, 1.0)
    for j in range(8):
        out[node(0, j), :] = out[node(0, j), :] + scale * gap[j]
    near = [
        jnp.where(elem >= 12, r, rolled(t, -4))
        for r, t in zip(from_right, tx_low)
    ]
    gap = jump_flux([n - o for n, o in zip(from_common(tab, near), high)], 0, -1.0)
    gap = [scale * x for x in gap]
    for n in range(PMIN, NQ):
        w = row_of(tab, W_AT + n)
        for j in range(8):
            out[node(n, j), :] = out[node(n, j), :] - w * gap[j]
    scale = lift * metric[1]
    low, high = y_faces(q, tab)
    own_low = ty_low
    flip = jnp.where(var == 2, -1.0, 1.0).astype(jnp.float32)
    first = (elem & 3) == 0
    near = [
        jnp.where(first, jnp.where(wall, flip * o, r), rolled(t, 1))
        for r, t, o in zip(from_below, ty_high, own_low)
    ]
    gap = jump_flux([n - o for n, o in zip(from_common(tab, near), low)], 1, 1.0)
    for i in range(8):
        out[node(i, 0), :] = out[node(i, 0), :] + scale * gap[i]
    near = [
        jnp.where((elem & 3) == 3, r, rolled(t, -1))
        for r, t in zip(from_above, own_low)
    ]
    gap = jump_flux([n - o for n, o in zip(from_common(tab, near), high)], 1, -1.0)
    gap = [scale * x for x in gap]
    for n in range(PMIN, NQ):
        w = row_of(tab, W_AT + n)
        for i in range(8):
            out[node(i, n), :] = out[node(i, n), :] - w * gap[i]
    scale = lift * metric[2]
    low, high = z_faces(q, tab)
    gap_low = jump_flux([h - o for h, o in zip(high, low)], 2, 1.0)
    gap_high = jump_flux([o - h for h, o in zip(high, low)], 2, -1.0)
    sub = lax.broadcasted_iota(jnp.int32, (8, LANES), 0)
    at_low = jnp.where(sub == 0, scale, 0.0)
    at_high = -scale * tab[pl.ds(W_AT, 8), :]
    for i in range(8):
        for j in range(8):
            pick = jnp.full((8, LANES), j, jnp.int32)
            lo = jnp.take_along_axis(gap_low[i], pick, axis=0)
            hi = jnp.take_along_axis(gap_high[i], pick, axis=0)
            out[node(i, j), :] = out[node(i, j), :] + at_low * lo + at_high * hi


def volume_terms(q, tab, metric, out):
    couplings = [coupling_of(d) for d in range(3)]

    def flux(x, d):
        source, has = couplings[d]
        y = metric[d] * x
        mixed = has * jnp.take_along_axis(y, source, axis=1)
        return mixed if mean_flow[d] == 0.0 else mean_flow[d] * y + mixed

    def along_x(j, carry):
        face = [q[node(i, j), :] for i in range(8)]
        for i, x in enumerate(along_first(tab, D_AT, face)):
            out[node(i, j), :] = -flux(x, 0)
        return carry

    lax.fori_loop(0, 8, along_x, 0)

    def along_yz(i, carry):
        face = [q[node(i, j), :] for j in range(8)]
        by_y = along_first(tab, D_AT, face)
        by_z = along_second(tab, DK_AT, face)
        for j in range(8):
            out[node(i, j), :] = out[node(i, j), :] - (flux(by_y[j], 1) + flux(by_z[j], 2))
        return carry

    lax.fori_loop(0, 8, along_yz, 0)


def all_metrics(metric_ref):
    return [spread(lambda x, y, d=d: metric_ref[d, x, y], jnp.float32) for d in range(3)]


def all_codes(turn_ref):
    return [spread(lambda x, y, s=s: turn_ref[s, x, y], jnp.int32) for s in range(2)]


def fetched(pairs, sems):
    copies = [pltpu.make_async_copy(a, b, sems.at[n]) for n, (a, b) in enumerate(pairs)]
    for copy in copies:
        copy.start()
    return copies


def first_kernel(
    fields_hbm, orders_hbm, turn_hbm, metric_hbm, rows_hbm, core_ref, row_ref, q, tab, *rest
):
    outs = rest[:8]
    flat, buf, fields, orders, turn, metric_ref, rows, sems = rest[8:]
    copies = fetched(
        [
            (orders_hbm, orders),
            (turn_hbm, turn),
            (metric_hbm, metric_ref),
            (rows_hbm, rows),
            (fields_hbm, fields),
        ],
        sems,
    )
    flat[pl.ds(80, 48), :] = jnp.zeros((48, 512), jnp.float32)
    for n in range(3):
        copies[n].wait()
    order = spread(lambda x, y: orders[x, y], jnp.int32)
    level = lax.broadcasted_iota(jnp.int32, (LANES, LANES), 0) + PMIN
    one_hot = jnp.where(
        level == jnp.broadcast_to(order[0:1, :], (LANES, LANES)), 1.0, 0.0
    ).astype(jnp.float32)
    copies[3].wait()
    tab[...] = jnp.dot(
        rows[...], one_hot, precision=lax.Precision.HIGHEST, preferred_element_type=jnp.float32
    )
    copies[4].wait()
    for v in range(VARS):
        for x in range(4):
            flat[pl.ds(v * 16 + x * 4, 4), :] = fields[x, v]
    in_k = tab[pl.ds(A_AT, 8), :]
    for part in range(4):
        block = flat[:, pl.ds(part * LANES, LANES)].T
        for half in range(2):
            in_ik = in_k * row_of(tab, A_AT + part * 2 + half)
            for j in range(8):
                at = (half * 8 + j) * 8
                q[node(part * 2 + half, j), :] = (
                    block[at : at + 8] * in_ik * row_of(tab, A_AT + j)
                )
    first_core, _ = places(core_ref, row_ref)
    make_messages(
        q, tab, order, all_metrics(metric_ref), all_codes(turn), first_core, outs, buf
    )


def second_kernel(up, down, chip, blk, core_ref, row_ref, pair_send, row_send):
    first_core, even_row = places(core_ref, row_ref)
    left, right = sides_of(chip, blk, first_core)
    _, elem, _ = lane_ids()
    up, down = load_face(up), load_face(down)

    def with_corners(message, edge, y, line):
        at_left, at_right = elem == 3, elem == 15
        out = message[:6]
        out.append(
            jnp.where(
                at_left,
                rolled(left[edge], 3 - y),
                jnp.where(at_right, rolled(right[edge], 15 - y), message[6]),
            )
        )
        out.append(
            jnp.where(
                at_left,
                rolled(left[line], -9 - y),
                jnp.where(at_right, rolled(right[line], 3 - y), message[7]),
            )
        )
        return out

    up = with_corners(up, 7, 3, 1)
    down = with_corners(down, 0, 0, 0)
    store_face(pair_send, [jnp.where(even_row, u, d) for u, d in zip(up, down)])
    store_face(row_send, [jnp.where(even_row, d, u) for u, d in zip(up, down)])


def third_kernel(
    q, tab, metric_hbm, turn_hbm, migration_hbm, rows_hbm, core_ref, row_ref, *rest
):
    traces, arrived = rest[:4], rest[4:8]
    outs = rest[8:12]
    (
        rate, middle, second, flat, slots, count, metric_ref, turn, migration, rows, halo_tab,
        buf, sems,
    ) = rest[12:]
    copies = fetched(
        [
            (metric_hbm, metric_ref),
            (turn_hbm, turn),
            (migration_hbm, migration),
            (rows_hbm, rows),
        ],
        sems,
    )
    first_core, even_row = places(core_ref, row_ref)
    wall = row_ref[0] == 0
    for copy in copies:
        copy.wait()
    metric = all_metrics(metric_ref)
    lift = tab[pl.ds(LIFT_AT, 8), :]
    chip, blk, pair, row = arrived
    left, right = sides_of(chip, blk, first_core)
    below, above = sides_of(pair, row, even_row)
    own = [load_face(ref) for ref in traces]
    beside = halo_step((left, right, below, above), own, wall, rows[...], halo_tab, buf)
    near = (left, [rolled(x, 12) for x in right], below, [rolled(x, 3) for x in above])
    volume_terms(q, tab, metric, rate)
    gaps_to(q, tab, lift, own, near, wall, metric, rate)
    for n in range(64):
        at = pl.ds(8 * n, 8)
        middle[at, :] = q[at, :] + time_step * rate[at, :]
    codes = all_codes(turn)
    x_ends, y_ends = x_faces(middle, tab), y_faces(middle, tab)
    own = [turned(to_common(tab, x_ends[side]), codes[side], buf) for side in range(2)]
    own = own + [to_common(tab, y_ends[side]) for side in range(2)]
    volume_terms(middle, tab, metric, second)
    gaps_to(middle, tab, lift, own, from_halo(beside), wall, metric, second)
    for part in range(4):
        at = pl.ds(part * LANES, LANES)
        flat[:, 0, at] = ((0.5 * time_step) * (rate[at, :] + second[at, :])).T
    slots[...] = jnp.zeros_like(slots)
    for m in range(SPREAD):
        count[m] = 0
    for e in range(NB):
        m = migration[0, 0, 0, e]
        c = count[m]
        count[m] = c + 1
        slot = jnp.where(core_ref[0] == 0, m, SPREAD - 1 - m) * CAP + c
        for v in range(VARS):
            slots[slot, v] = flat[v * 16 + e]
    at = 0
    for out in outs:
        size = out.shape[0]
        out[...] = slots[pl.ds(at, size)]
        at += size


def last_kernel(far, own, near, core_ref, chip, relayed, out, sems):
    def put(groups):
        copies = [
            pltpu.make_async_copy(piece, out.at[pl.ds(m * CAP, CAP)], sems.at[m])
            for m, piece in enumerate(groups)
        ]
        for copy in copies:
            copy.start()
        for copy in copies:
            copy.wait()

    first = far.at[pl.ds(0, CAP)]

    @pl.when(core_ref[0] == 0)
    def _():
        put([first, chip.at[1], own, relayed.at[1, pl.ds(CAP, CAP)], near])

    @pl.when(core_ref[0] != 0)
    def _():
        put([near, relayed.at[0, pl.ds(CAP, CAP)], own, chip.at[0], first])


def f32(*shape):
    return jax.ShapeDtypeStruct(shape, jnp.float32)


VMEM = pl.BlockSpec(memory_space=pltpu.VMEM)
SMEM = pl.BlockSpec(memory_space=pltpu.SMEM)
HBM = pl.BlockSpec(memory_space=pltpu.HBM)
ANY = pl.BlockSpec(memory_space=pl.ANY)
PARAMS = pltpu.CompilerParams(vmem_limit_bytes=32 * 1024 * 1024)
FACE = f32(64, LANES)
VOLUME = f32(512, LANES)


def pairs_of(count, first):
    return [[n, n + 1] for n in range(first, count - 1, 2)]


def swapped(array, axis, wraps):
    count = lax.axis_size(axis)
    pairs = [(a, b) for a, b in pairs_of(count, 1)]
    if wraps:
        pairs.append((count - 1, 0))
    return lax.ppermute(array, axis, pairs + [(b, a) for a, b in pairs])


def paired(array, axis):
    return lax.all_gather(array, axis, axis_index_groups=pairs_of(lax.axis_size(axis), 0))


def hopped(array, outward):
    count = lax.axis_size("blk")
    step = [-2, 2] if outward else [2, -2]
    return lax.ppermute(array, "blk", [(n, (n + step[n % 2]) % count) for n in range(count)])


def vmem(*shape):
    return pltpu.VMEM(shape, jnp.float32)


def sems(count):
    return pltpu.SemaphoreType.DMA((count,))


def local(fields, orders, metric, face_turn, migration):
    by_var = jnp.transpose(fields, (0, 2, 1, 3))
    core = lax.rem(lax.axis_index("blk").astype(jnp.int32), 2).reshape(1)
    row = lax.axis_index("row").astype(jnp.int32).reshape(1)
    rows = jnp.asarray(table_rows())
    metric_at = pltpu.SMEM((3, 4, 4), jnp.float32)
    turn_at = pltpu.SMEM((2, 4, 4), jnp.int32)
    q, tab, *faces = pl.pallas_call(
        first_kernel,
        out_shape=[VOLUME, f32(TAB_ROWS, LANES)] + [FACE] * 8,
        in_specs=[HBM] * 5 + [SMEM] * 2,
        out_specs=[VMEM] * 10,
        scratch_shapes=[
            vmem(LANES, 512),
            vmem(64, LANES),
            vmem(4, VARS, 4, 512),
            pltpu.SMEM((4, 4), jnp.int32),
            turn_at,
            metric_at,
            vmem(TAB_ROWS, LANES),
            sems(5),
        ],
        compiler_params=PARAMS,
    )(by_var, orders, face_turn, metric, rows, core, row)
    chip_send, blk_send, up, down = faces[4:]
    blk = swapped(blk_send, "blk", True)
    chip = paired(chip_send, "blk")
    pair_send, row_send = pl.pallas_call(
        second_kernel,
        out_shape=[FACE] * 2,
        in_specs=[VMEM] * 4 + [SMEM] * 2,
        out_specs=[VMEM] * 2,
        compiler_params=PARAMS,
    )(up, down, chip, blk, core, row)
    beyond = swapped(row_send, "row", False)
    pair = paired(pair_send, "row")
    outward, own, same_chip, inward = pl.pallas_call(
        third_kernel,
        out_shape=[f32(n, VARS, 1, 512) for n in (2 * CAP, CAP, CAP, CAP)],
        in_specs=[VMEM] * 2 + [HBM] * 4 + [SMEM] * 2 + [VMEM] * 8,
        out_specs=[VMEM] * 4,
        scratch_shapes=[
            vmem(512, LANES),
            vmem(512, LANES),
            vmem(512, LANES),
            vmem(LANES, 1, 512),
            vmem(SPREAD * CAP, VARS, 1, 512),
            pltpu.SMEM((8,), jnp.int32),
            metric_at,
            turn_at,
            pltpu.SMEM((1, 1, 1, NB), jnp.int32),
            vmem(TAB_ROWS, LANES),
            vmem(TAB_ROWS, LANES),
            vmem(64, LANES),
            sems(4),
        ],
        compiler_params=PARAMS,
    )(
        q, tab, metric, face_turn, jnp.transpose(migration, (0, 1, 3, 2)), rows, core, row,
        *faces[:4], chip, blk, pair, beyond,
    )
    far = hopped(outward, True)
    near = hopped(inward, False)
    chip = paired(same_chip, "blk")
    relayed = paired(far, "blk")
    moved = pl.pallas_call(
        last_kernel,
        out_shape=f32(SPREAD * CAP, VARS, 1, 512),
        in_specs=[ANY] * 3 + [SMEM] + [ANY] * 2,
        out_specs=HBM,
        scratch_shapes=[sems(SPREAD)],
        compiler_params=PARAMS,
    )(far, own, near, core, chip, relayed)
    return jnp.transpose(moved, (2, 0, 1, 3)).reshape(1, 1, SPREAD * CAP, VARS, 512)


def solution(mesh):
    placed = (
        P("blk", "row", None, None),
        P("blk", "row"),
        P(None, "blk", "row"),
        P(None, "blk", "row"),
        P("blk", "row", None, None),
    )
    return jax.shard_map(
        local,
        mesh=mesh,
        in_specs=placed,
        out_specs=P("blk", "row", None, None, None),
        check_vma=False,
    )
```

```python
import jax
import jax.numpy as jnp
import ml_dtypes
import numpy as np
from jax import lax
from jax.experimental import pallas as pl
from jax.experimental.pallas import tpu as pltpu
from jax.sharding import PartitionSpec as P

PMAX = 7
PMIN = 3
VARS = 5
NQ = 8
NB = 16
SPREAD = 5
CAP = 5
LANES = 128

mean_flow = (0.4, 0.0, 0.2)
time_step = 0.008


def legendre_points(degree):
    point_count = degree + 1
    estimate = np.cos(np.pi * np.arange(point_count) / degree)
    for sweep_idx in range(40):
        values = np.zeros((point_count, point_count))
        values[:, 0] = 1.0
        values[:, 1] = estimate
        for order_idx in range(2, point_count):
            values[:, order_idx] = (
                (2 * order_idx - 1) * estimate * values[:, order_idx - 1]
                - (order_idx - 1) * values[:, order_idx - 2]
            ) / order_idx
        estimate = estimate - (estimate * values[:, degree] - values[:, degree - 1]) / (
            point_count * values[:, degree]
        )
    return np.sort(estimate)


def lagrange_matrix(points, targets):
    result = np.ones((len(targets), len(points)))
    for column in range(len(points)):
        for other_idx in range(len(points)):
            if other_idx != column:
                result[:, column] *= (targets - points[other_idx]) / (
                    points[column] - points[other_idx]
                )
    return result


def build_tables(lowest, highest):
    node_count = highest + 1
    level_count = highest - lowest + 1
    common = legendre_points(highest)
    derive = np.zeros((level_count, node_count, node_count))
    to_grid = np.zeros((level_count, node_count, node_count))
    from_grid = np.zeros((level_count, node_count, node_count))
    lifting = np.zeros((level_count,))
    last_node = np.zeros((level_count, node_count))
    active = np.zeros((level_count, node_count))
    for level_idx in range(level_count):
        degree = lowest + level_idx
        points = legendre_points(degree)
        filled = degree + 1
        weights = np.array(
            [
                1.0
                / np.prod(
                    [
                        points[column] - points[other_idx]
                        for other_idx in range(filled)
                        if other_idx != column
                    ]
                )
                for column in range(filled)
            ]
        )
        local_diff = np.zeros((filled, filled))
        for row_idx in range(filled):
            for column in range(filled):
                if column != row_idx:
                    local_diff[row_idx, column] = (
                        weights[column] / weights[row_idx] / (points[row_idx] - points[column])
                    )
            local_diff[row_idx, row_idx] = -np.sum(local_diff[row_idx])
        derive[level_idx, :filled, :filled] = local_diff
        to_grid[level_idx, :, :filled] = lagrange_matrix(points, common)
        from_grid[level_idx, :filled, :] = lagrange_matrix(common, points)
        lifting[level_idx] = degree * (degree + 1) / 2.0
        last_node[level_idx, degree] = 1.0
        active[level_idx, :filled] = 1.0
    return derive, to_grid, from_grid, lifting, last_node, active


D_AT, DK_AT, I_AT, IK_AT, B_AT, BK_AT, W_AT, A_AT, LIFT_AT, DLAST_AT = (
    0, 64, 128, 192, 256, 320, 384, 392, 400, 408)
TAB_ROWS = 416


def table_columns():
    derive, to_grid, from_grid, lifting, last_node, active = build_tables(PMIN, PMAX)
    rows = np.zeros((4 * LANES, 8))
    for level in range(PMAX - PMIN + 1):
        for at, turned_at, mat in (
            (D_AT, DK_AT, derive[level]),
            (I_AT, IK_AT, to_grid[level]),
            (B_AT, BK_AT, from_grid[level]),
        ):
            rows[at : at + 64, level] = mat.reshape(-1)
            for turn in range(8):
                for a in range(8):
                    rows[turned_at + turn * 8 + a, level] = mat[a, (a + turn) % 8]
        rows[W_AT : W_AT + 8, level] = last_node[level]
        rows[A_AT : A_AT + 8, level] = active[level]
        rows[LIFT_AT : LIFT_AT + 8, level] = lifting[level]
        rows[DLAST_AT : DLAST_AT + 8, level] = derive[level][PMIN + level]
    left, parts = rows.T.astype(np.float32), []
    for _ in range(3):
        parts.append(left.astype(ml_dtypes.bfloat16).astype(np.float32))
        left = left - parts[-1]
    return np.concatenate(parts)


def lane_ids():
    lane = lax.broadcasted_iota(jnp.int32, (8, LANES), 1)
    return lane, lane & 15, lane >> 4


def spread(read, dtype):
    _, elem, _ = lane_ids()
    out = jnp.zeros((8, LANES), dtype)
    for e in range(NB):
        out = jnp.where(elem == e, read(e // 4, e % 4), out)
    return out


def rolled(x, by):
    return pltpu.roll(x, by % LANES, 1)


def subrolled(x, by):
    return x if by % 8 == 0 else pltpu.roll(x, by % 8, 0)


def row_of(ref, at):
    return jnp.broadcast_to(ref[pl.ds(at, 1), :], (8, LANES))


def along_first(tab, at, face):
    out = []
    for a in range(8):
        total = row_of(tab, at + a * 8) * face[0]
        for j in range(1, 8):
            total = total + row_of(tab, at + a * 8 + j) * face[j]
        out.append(total)
    return out


def along_second(tab, at, face):
    coefs = [tab[pl.ds(at + 8 * turn, 8), :] for turn in range(8)]
    out = []
    for x in face:
        total = coefs[0] * x
        for turn in range(1, 8):
            total = total + coefs[turn] * subrolled(x, -turn)
        out.append(total)
    return out


def to_common(tab, face):
    return along_second(tab, IK_AT, along_first(tab, I_AT, face))


def from_common(tab, face):
    return along_second(tab, BK_AT, along_first(tab, B_AT, face))


def turned(face, codes, buf):
    for a in range(8):
        buf[pl.ds(8 * a, 8), :] = face[a]
    back = lax.broadcasted_iota(jnp.int32, (8, LANES), 0) * -1 + 7
    out = []
    for a in range(8):
        x = jnp.where(codes == 1, face[7 - a], face[a])
        x = jnp.where(codes == 2, jnp.take_along_axis(face[a], back, axis=0), x)
        x = jnp.where(codes == 3, buf[pl.ds(a, 8, stride=8), :], x)
        out.append(x)
    return out


def coupling_of(direction):
    lane, elem, var = lane_ids()
    vel = elem + 16 * (1 + direction)
    source = jnp.where((var == 0) | (var == 4), vel, lane)
    source = jnp.where(var == 1 + direction, elem + 64, source)
    has = (var == 0) | (var == 4) | (var == 1 + direction)
    return source, jnp.where(has, 1.0, 0.0).astype(jnp.float32)


def jump_with(gap, coupling, factor):
    source, has = coupling
    half = 0.5 * has
    return [factor * x + half * jnp.take_along_axis(x, source, axis=1) for x in gap]


def jump_factor(direction, sign):
    return 0.5 * (mean_flow[direction] + sign * (abs(mean_flow[direction]) + 1.0))


def jump_flux(gap, direction, sign):
    return jump_with(gap, coupling_of(direction), jump_factor(direction, sign))


def load_face(ref):
    return [ref[pl.ds(8 * a, 8), :] for a in range(8)]


def store_face(ref, face):
    for a in range(8):
        ref[pl.ds(8 * a, 8), :] = face[a]


def picked(tab, read):
    out = None
    for n in range(PMIN, NQ):
        w = row_of(tab, W_AT + n)
        layer = [w * x for x in read(n)]
        out = layer if out is None else [s + x for s, x in zip(out, layer)]
    return out


def node(i, j):
    return pl.ds((i * 8 + j) * 8, 8)


def x_faces(q, tab):
    low = [q[node(0, j), :] for j in range(8)]
    high = picked(tab, lambda n: [q[node(n, j), :] for j in range(8)])
    return low, high


def y_faces(q, tab):
    low = [q[node(i, 0), :] for i in range(8)]
    high = picked(tab, lambda n: [q[node(i, n), :] for i in range(8)])
    return low, high


def z_faces(q, tab):
    low = [q[pl.ds(i * 64, 8, stride=8), :] for i in range(8)]
    high = picked(tab, lambda n: [q[pl.ds(i * 64 + n, 8, stride=8), :] for i in range(8)])
    return low, high


def end_rows(q, tab, read):
    low = high = None
    for n in range(NQ):
        first, last = row_of(tab, D_AT + n), row_of(tab, DLAST_AT + n)
        layer = read(n)
        by_low, by_high = [first * x for x in layer], [last * x for x in layer]
        low = by_low if low is None else [a + b for a, b in zip(low, by_low)]
        high = by_high if high is None else [a + b for a, b in zip(high, by_high)]
    return low, high


def packed(kinds, where, shifts):
    out = []
    for a in range(8):
        x = rolled(kinds[3][a], shifts[3])
        for kind in range(3):
            x = jnp.where(where == kind, rolled(kinds[kind][a], shifts[kind]), x)
        out.append(x)
    return out


def make_messages(q, tab, order, metric, codes, first_core, outs, buf):
    tx_low, tx_high, ty_low, ty_high, chip_send, blk_send, up, down = outs
    _, elem, _ = lane_ids()
    x_ends, y_ends = x_faces(q, tab), y_faces(q, tab)
    tx = [turned(to_common(tab, x_ends[side]), codes[side], buf) for side in range(2)]
    ty = [to_common(tab, y_ends[side]) for side in range(2)]
    for ref, face in zip((tx_low, tx_high, ty_low, ty_high), tx + ty):
        store_face(ref, face)
    x_rows = end_rows(q, tab, lambda n: [q[node(n, j), :] for j in range(8)])
    y_rows = end_rows(q, tab, lambda n: [q[node(i, n), :] for i in range(8)])
    params = [order.astype(jnp.float32)] + metric
    zero = jnp.zeros((8, LANES), jnp.float32)

    def along_x(side, shifts):
        edge = 7 * side
        lines = [ty[0][edge], ty[1][edge]] + params + [codes[side].astype(jnp.float32), zero]
        return packed([tx[side], x_ends[side], x_rows[side], lines], elem >> 2, shifts)

    def along_y(side, shifts):
        edge = 7 * side
        lines = [tx[0][edge], tx[1][edge]] + params + [zero, zero]
        return packed([ty[side], y_ends[side], y_rows[side], lines], elem & 3, shifts)

    left = along_x(0, (0, 4, 8, 12))
    right = along_x(1, (-12, -8, -4, 0))
    store_face(chip_send, [jnp.where(first_core, r, l) for l, r in zip(left, right)])
    store_face(blk_send, [jnp.where(first_core, l, r) for l, r in zip(left, right)])
    store_face(down, along_y(0, (0, 1, 2, 3)))
    store_face(up, along_y(1, (-3, -2, -1, 0)))


def sides_of(paired_ref, other_ref, first):
    pair = load_face(paired_ref.at[jnp.where(first, 1, 0)])
    other = load_face(other_ref)
    before = [jnp.where(first, o, p) for o, p in zip(other, pair)]
    after = [jnp.where(first, p, o) for o, p in zip(other, pair)]
    return before, after


def places(core_ref, row_ref):
    return core_ref[0] == 0, lax.rem(row_ref[0], 2) == 0


def halo_step(messages, traces, wall, columns, tab, q_buf):
    left, right, below, above = messages
    lane, elem, var = lane_ids()
    group, pos = elem >> 2, elem & 3
    base = lane - elem
    across_rows = group >= 2
    is_high = (group & 1) == 0

    def collected(block, kind):
        at = base + jnp.where(across_rows, pos * 4 + kind, kind * 4 + pos)
        out = jnp.take_along_axis(left[block], at, axis=1)
        for g, message in ((1, right), (2, below), (3, above)):
            out = jnp.where(group == g, jnp.take_along_axis(message[block], at, axis=1), out)
        return out

    table_for(columns, collected(2, 3)[0:1, :], tab)
    lift = tab[pl.ds(LIFT_AT, 8), :]
    metric_x, metric_y, metric_z = [collected(3 + d, 3) for d in range(3)]
    metric_n = jnp.where(across_rows, metric_y, metric_x)
    metric_t = jnp.where(across_rows, metric_x, metric_y)
    codes = jnp.where(across_rows, 0.0, collected(6, 3)).astype(jnp.int32)
    by_x, by_y, by_z = [coupling_of(d) for d in range(3)]

    def mixed(a, b):
        return tuple(jnp.where(across_rows, y, x) for x, y in zip(a, b))

    couple_n, couple_t = mixed(by_x, by_y), mixed(by_y, by_x)

    def factor(d, sign):
        return jnp.float32(jump_factor(d, sign))

    factor_n = jnp.where(
        across_rows,
        jnp.where(is_high, factor(1, -1.0), factor(1, 1.0)),
        jnp.where(is_high, factor(0, -1.0), factor(0, 1.0)),
    )
    factor_t = [
        jnp.where(across_rows, factor(0, sign), factor(1, sign)) for sign in (1.0, -1.0)
    ]
    flow_n = jnp.where(across_rows, mean_flow[1], mean_flow[0])
    flow_t = jnp.where(across_rows, mean_flow[0], mean_flow[1])

    def flux(x, flow, coupling):
        source, has = coupling
        return flow * x + has * jnp.take_along_axis(x, source, axis=1)

    face = [collected(a, 1) for a in range(8)]
    slope = [collected(a, 2) for a in range(8)]
    tx_low, tx_high, ty_low, ty_high = traces
    at = jnp.where(group == 0, pos, jnp.where(group == 1, 12 + pos, 4 * pos))
    at = base + jnp.where(group == 3, 4 * pos + 3, at)
    near = []
    for a in range(8):
        out = jnp.take_along_axis(tx_low[a], at, axis=1)
        for g, trace in ((1, tx_high), (2, ty_low), (3, ty_high)):
            out = jnp.where(group == g, jnp.take_along_axis(trace[a], at, axis=1), out)
        near.append(out)
    gap = [n - f for n, f in zip(from_common(tab, near), face)]
    gap = jump_with(gap, couple_n, factor_n)
    scale = metric_n * lift * jnp.where(is_high, -1.0, 1.0)
    rate = [
        scale * g - metric_n * flux(d, flow_n, couple_n) for g, d in zip(gap, slope)
    ]
    by_t = along_first(tab, D_AT, face)
    by_k = along_second(tab, DK_AT, face)
    scale_z = metric_z * lift
    sub = lax.broadcasted_iota(jnp.int32, (8, LANES), 0)
    weights = tab[pl.ds(W_AT, 8), :]
    at_low = jnp.where(sub == 0, scale_z, 0.0)
    at_high = -scale_z * weights

    def at_k(x, k):
        return jnp.take_along_axis(x, jnp.full((8, LANES), k, jnp.int32), axis=0)

    for a in range(8):
        low = at_k(face[a], 0)
        high = row_of(tab, W_AT + PMIN) * at_k(face[a], PMIN)
        for n in range(PMIN + 1, NQ):
            high = high + row_of(tab, W_AT + n) * at_k(face[a], n)
        gap_low = jump_flux([high - low], 2, 1.0)[0]
        gap_high = jump_flux([low - high], 2, -1.0)[0]
        rate[a] = (
            rate[a]
            - metric_t * flux(by_t[a], flow_t, couple_t)
            - metric_z * flux(by_k[a], mean_flow[2], by_z)
            + at_low * gap_low
            + at_high * gap_high
        )
    line_low, line_high = collected(0, 3), collected(1, 3)
    flip = jnp.where(var == 2, -1.0, 1.0).astype(jnp.float32)

    def corners(side, block_below, block_above):
        at = base + jnp.where(elem == (4 if side == 0 else 7), 15, 3)
        if side == 1:
            at = base + jnp.where(elem == 3, 3, 15)
        return (
            jnp.take_along_axis(below[block_below], at, axis=1),
            jnp.take_along_axis(above[block_above], at, axis=1),
        )

    from_below, _ = corners(0, 7, 7)
    at_wall = jnp.where(wall, flip * line_low, from_below)
    from_below, from_above = corners(0, 6, 6)
    corner = jnp.where(
        across_rows, jnp.where(group == 2, from_below, from_above), at_wall
    )
    near_low = jnp.where(pos == 0, corner, rolled(line_high, 1))
    _, beyond = corners(1, 7, 7)
    from_below, from_above = corners(1, 6, 6)
    corner = jnp.where(across_rows, jnp.where(group == 2, from_below, from_above), beyond)
    near_high = jnp.where(pos == 3, corner, rolled(line_low, -1))
    near_low, near_high = along_second(tab, BK_AT, [near_low, near_high])
    own_high = row_of(tab, W_AT + PMIN) * face[PMIN]
    for n in range(PMIN + 1, NQ):
        own_high = own_high + row_of(tab, W_AT + n) * face[n]
    scale = metric_t * lift
    gap_low = scale * jump_with([near_low - face[0]], couple_t, factor_t[0])[0]
    gap_high = scale * jump_with([near_high - own_high], couple_t, factor_t[1])[0]
    rate[0] = rate[0] + gap_low
    for n in range(PMIN, NQ):
        rate[n] = rate[n] - row_of(tab, W_AT + n) * gap_high
    middle = [f + time_step * r for f, r in zip(face, rate)]
    return turned(to_common(tab, middle), codes, q_buf)


def from_halo(face):
    lane, elem, _ = lane_ids()
    base = lane - elem
    at_below = base + 8 + (elem >> 2)
    at_above = base + 12 + (elem >> 2)
    return (
        face,
        [rolled(x, 8) for x in face],
        [jnp.take_along_axis(x, at_below, axis=1) for x in face],
        [jnp.take_along_axis(x, at_above, axis=1) for x in face],
    )


def gaps_to(q, tab, lift, traces, arrived, wall, metric, out):
    tx_low, tx_high, ty_low, ty_high = traces
    from_left, from_right, from_below, from_above = arrived
    _, elem, var = lane_ids()
    scale = lift * metric[0]
    low, high = x_faces(q, tab)
    near = [
        jnp.where(elem < 4, r, rolled(t, 4))
        for r, t in zip(from_left, tx_high)
    ]
    gap = jump_flux([n - o for n, o in zip(from_common(tab, near), low)], 0, 1.0)
    for j in range(8):
        out[node(0, j), :] = out[node(0, j), :] + scale * gap[j]
    near = [
        jnp.where(elem >= 12, r, rolled(t, -4))
        for r, t in zip(from_right, tx_low)
    ]
    gap = jump_flux([n - o for n, o in zip(from_common(tab, near), high)], 0, -1.0)
    gap = [scale * x for x in gap]
    for n in range(PMIN, NQ):
        w = row_of(tab, W_AT + n)
        for j in range(8):
            out[node(n, j), :] = out[node(n, j), :] - w * gap[j]
    scale = lift * metric[1]
    low, high = y_faces(q, tab)
    own_low = ty_low
    flip = jnp.where(var == 2, -1.0, 1.0).astype(jnp.float32)
    first = (elem & 3) == 0
    near = [
        jnp.where(first, jnp.where(wall, flip * o, r), rolled(t, 1))
        for r, t, o in zip(from_below, ty_high, own_low)
    ]
    gap = jump_flux([n - o for n, o in zip(from_common(tab, near), low)], 1, 1.0)
    for i in range(8):
        out[node(i, 0), :] = out[node(i, 0), :] + scale * gap[i]
    near = [
        jnp.where((elem & 3) == 3, r, rolled(t, -1))
        for r, t in zip(from_above, own_low)
    ]
    gap = jump_flux([n - o for n, o in zip(from_common(tab, near), high)], 1, -1.0)
    gap = [scale * x for x in gap]
    for n in range(PMIN, NQ):
        w = row_of(tab, W_AT + n)
        for i in range(8):
            out[node(i, n), :] = out[node(i, n), :] - w * gap[i]


def span_terms(q, tab, lift, metric, out):
    scale = lift * metric[2]
    low, high = z_faces(q, tab)
    gap_low = jump_flux([h - o for h, o in zip(high, low)], 2, 1.0)
    gap_high = jump_flux([o - h for h, o in zip(high, low)], 2, -1.0)
    sub = lax.broadcasted_iota(jnp.int32, (8, LANES), 0)
    at_low = jnp.where(sub == 0, scale, 0.0)
    at_high = -scale * tab[pl.ds(W_AT, 8), :]
    for i in range(8):
        for j in range(8):
            pick = jnp.full((8, LANES), j, jnp.int32)
            lo = jnp.take_along_axis(gap_low[i], pick, axis=0)
            hi = jnp.take_along_axis(gap_high[i], pick, axis=0)
            out[node(i, j), :] = out[node(i, j), :] + at_low * lo + at_high * hi


def volume_terms(q, tab, metric, out):
    couplings = [coupling_of(d) for d in range(3)]

    def flux(x, d):
        source, has = couplings[d]
        y = metric[d] * x
        mixed = has * jnp.take_along_axis(y, source, axis=1)
        return mixed if mean_flow[d] == 0.0 else mean_flow[d] * y + mixed

    for j in range(8):
        face = [q[node(i, j), :] for i in range(8)]
        for i, x in enumerate(along_first(tab, D_AT, face)):
            out[node(i, j), :] = -flux(x, 0)
    for i in range(8):
        face = [q[node(i, j), :] for j in range(8)]
        by_y = along_first(tab, D_AT, face)
        by_z = along_second(tab, DK_AT, face)
        for j in range(8):
            out[node(i, j), :] = out[node(i, j), :] - (flux(by_y[j], 1) + flux(by_z[j], 2))


def all_metrics(metric_ref):
    return [spread(lambda x, y, d=d: metric_ref[d, x, y], jnp.float32) for d in range(3)]


def all_codes(turn_ref):
    return [spread(lambda x, y, s=s: turn_ref[s, x, y], jnp.int32) for s in range(2)]


def kept_metrics(params):
    return [params[pl.ds(8 * d, 8), :] for d in range(3)]


def kept_codes(params):
    return [params[pl.ds(24 + 8 * s, 8), :].astype(jnp.int32) for s in range(2)]


def table_for(columns, level_row, tab):
    level = (lax.broadcasted_iota(jnp.int32, (LANES, LANES), 0) & 7) + PMIN
    one_hot = jnp.where(
        level.astype(jnp.float32) == jnp.broadcast_to(level_row, (LANES, LANES)), 1.0, 0.0
    ).astype(jnp.bfloat16)
    pad = jnp.zeros((LANES - 24, LANES), jnp.float32)
    for part in range(4):
        at = part * LANES
        size = min(LANES, TAB_ROWS - at)
        block = jnp.concatenate([columns[:, pl.ds(at, LANES)], pad], axis=0).T
        tab[pl.ds(at, size), :] = jnp.dot(
            block.astype(jnp.bfloat16), one_hot, preferred_element_type=jnp.float32
        )[:size]


def fetched(pairs, sems):
    copies = [pltpu.make_async_copy(a, b, sems.at[n]) for n, (a, b) in enumerate(pairs)]
    for copy in copies:
        copy.start()
    return copies


def first_kernel(
    fields, columns, orders_hbm, turn_hbm, metric_hbm, core_ref, row_ref, q, tab, params, *rest
):
    outs = rest[:8]
    flat, buf, orders, turn, metric_ref, sems = rest[8:]
    copies = fetched(
        [(orders_hbm, orders), (turn_hbm, turn), (metric_hbm, metric_ref)], sems
    )
    flat[pl.ds(80, 48), :] = jnp.zeros((48, 512), jnp.float32)
    for v in range(VARS):
        for x in range(4):
            flat[pl.ds(v * 16 + x * 4, 4), :] = fields[x, v]
    for copy in copies:
        copy.wait()
    order = spread(lambda x, y: orders[x, y].astype(jnp.float32), jnp.float32)
    metric, codes = all_metrics(metric_ref), all_codes(turn)
    for n, x in enumerate(metric + codes):
        params[pl.ds(8 * n, 8), :] = x.astype(jnp.float32)
    table_for(columns, order[0:1, :], tab)
    in_k = tab[pl.ds(A_AT, 8), :]
    for part in range(4):
        block = flat[:, pl.ds(part * LANES, LANES)].T
        for half in range(2):
            in_ik = in_k * row_of(tab, A_AT + part * 2 + half)
            for j in range(8):
                at = (half * 8 + j) * 8
                q[node(part * 2 + half, j), :] = (
                    block[at : at + 8] * in_ik * row_of(tab, A_AT + j)
                )
    first_core, _ = places(core_ref, row_ref)
    make_messages(q, tab, order, metric, codes, first_core, outs, buf)


def inner_kernel(q, tab, params, rate):
    metric = kept_metrics(params)
    volume_terms(q, tab, metric, rate)
    span_terms(q, tab, tab[pl.ds(LIFT_AT, 8), :], metric, rate)


def second_kernel(up, down, chip, blk, inner, core_ref, row_ref, pair_send, row_send):
    first_core, even_row = places(core_ref, row_ref)
    left, right = sides_of(chip, blk, first_core)
    _, elem, _ = lane_ids()
    up, down = load_face(up), load_face(down)

    def with_corners(message, edge, y, line):
        at_left, at_right = elem == 3, elem == 15
        out = message[:6]
        out.append(
            jnp.where(
                at_left,
                rolled(left[edge], 3 - y),
                jnp.where(at_right, rolled(right[edge], 15 - y), message[6]),
            )
        )
        out.append(
            jnp.where(
                at_left,
                rolled(left[line], -9 - y),
                jnp.where(at_right, rolled(right[line], 3 - y), message[7]),
            )
        )
        return out

    up = with_corners(up, 7, 3, 1)
    down = with_corners(down, 0, 0, 0)
    store_face(pair_send, [jnp.where(even_row, u, d) for u, d in zip(up, down)])
    store_face(row_send, [jnp.where(even_row, d, u) for u, d in zip(up, down)])


def third_kernel(q, tab, params, inner, columns, migration_hbm, core_ref, row_ref, *rest):
    traces, arrived = rest[:4], rest[4:8]
    outs = rest[8:12]
    rate, middle, second, flat, slots, count, migration, halo_tab, buf, sems = rest[12:]
    copies = fetched([(migration_hbm, migration)], sems)
    first_core, even_row = places(core_ref, row_ref)
    wall = row_ref[0] == 0
    metric, codes = kept_metrics(params), kept_codes(params)
    lift = tab[pl.ds(LIFT_AT, 8), :]
    chip, blk, pair, row = arrived
    left, right = sides_of(chip, blk, first_core)
    below, above = sides_of(pair, row, even_row)
    own = [load_face(ref) for ref in traces]
    beside = halo_step((left, right, below, above), own, wall, columns, halo_tab, buf)
    near = (left, [rolled(x, 12) for x in right], below, [rolled(x, 3) for x in above])
    rate[...] = inner[...]
    gaps_to(q, tab, lift, own, near, wall, metric, rate)
    for n in range(64):
        at = pl.ds(8 * n, 8)
        middle[at, :] = q[at, :] + time_step * rate[at, :]
    x_ends, y_ends = x_faces(middle, tab), y_faces(middle, tab)
    own = [turned(to_common(tab, x_ends[side]), codes[side], buf) for side in range(2)]
    own = own + [to_common(tab, y_ends[side]) for side in range(2)]
    volume_terms(middle, tab, metric, second)
    span_terms(middle, tab, lift, metric, second)
    gaps_to(middle, tab, lift, own, from_halo(beside), wall, metric, second)
    copies[0].wait()
    for part in range(4):
        at = pl.ds(part * LANES, LANES)
        flat[:, 0, at] = ((0.5 * time_step) * (rate[at, :] + second[at, :])).T
    slots[...] = jnp.zeros_like(slots)
    for m in range(SPREAD):
        count[m] = 0
    for e in range(NB):
        m = migration[0, 0, 0, e]
        c = count[m]
        count[m] = c + 1
        slot = jnp.where(core_ref[0] == 0, m, SPREAD - 1 - m) * CAP + c
        for v in range(VARS):
            slots[slot, v] = flat[v * 16 + e]
    at = 0
    for out in outs:
        size = out.shape[0]
        out[...] = slots[pl.ds(at, size)]
        at += size


def last_kernel(far, own, near, core_ref, chip, relayed, out, sems):
    def put(groups):
        copies = [
            pltpu.make_async_copy(piece, out.at[pl.ds(m * CAP, CAP)], sems.at[m])
            for m, piece in enumerate(groups)
        ]
        for copy in copies:
            copy.start()
        for copy in copies:
            copy.wait()

    first = far.at[pl.ds(0, CAP)]

    @pl.when(core_ref[0] == 0)
    def _():
        put([first, chip.at[1], own, relayed.at[1, pl.ds(CAP, CAP)], near])

    @pl.when(core_ref[0] != 0)
    def _():
        put([near, relayed.at[0, pl.ds(CAP, CAP)], own, chip.at[0], first])


def f32(*shape):
    return jax.ShapeDtypeStruct(shape, jnp.float32)


VMEM = pl.BlockSpec(memory_space=pltpu.VMEM)
SMEM = pl.BlockSpec(memory_space=pltpu.SMEM)
HBM = pl.BlockSpec(memory_space=pltpu.HBM)
ANY = pl.BlockSpec(memory_space=pl.ANY)
PARAMS = pltpu.CompilerParams(vmem_limit_bytes=32 * 1024 * 1024)
FACE = f32(64, LANES)
VOLUME = f32(512, LANES)


def pairs_of(count, first):
    return [[n, n + 1] for n in range(first, count - 1, 2)]


def swapped(array, axis, wraps):
    count = lax.axis_size(axis)
    pairs = [(a, b) for a, b in pairs_of(count, 1)]
    if wraps:
        pairs.append((count - 1, 0))
    return lax.ppermute(array, axis, pairs + [(b, a) for a, b in pairs])


def paired(array, axis):
    return lax.all_gather(array, axis, axis_index_groups=pairs_of(lax.axis_size(axis), 0))


def hopped(array, outward):
    count = lax.axis_size("blk")
    step = [-2, 2] if outward else [2, -2]
    return lax.ppermute(array, "blk", [(n, (n + step[n % 2]) % count) for n in range(count)])


def vmem(*shape):
    return pltpu.VMEM(shape, jnp.float32)


def sems(count):
    return pltpu.SemaphoreType.DMA((count,))


def local(fields, orders, metric, face_turn, migration):
    by_var = jnp.transpose(fields, (0, 2, 1, 3))
    core = lax.rem(lax.axis_index("blk").astype(jnp.int32), 2).reshape(1)
    row = lax.axis_index("row").astype(jnp.int32).reshape(1)
    columns = jnp.asarray(table_columns())
    q, tab, params, *faces = pl.pallas_call(
        first_kernel,
        out_shape=[VOLUME, f32(TAB_ROWS, LANES), f32(40, LANES)] + [FACE] * 8,
        in_specs=[VMEM] * 2 + [HBM] * 3 + [SMEM] * 2,
        out_specs=[VMEM] * 11,
        scratch_shapes=[
            vmem(LANES, 512),
            vmem(64, LANES),
            pltpu.SMEM((4, 4), jnp.int32),
            pltpu.SMEM((2, 4, 4), jnp.int32),
            pltpu.SMEM((3, 4, 4), jnp.float32),
            sems(3),
        ],
        compiler_params=PARAMS,
    )(by_var, columns, orders, face_turn, metric, core, row)
    chip_send, blk_send, up, down = faces[4:]
    blk = swapped(blk_send, "blk", True)
    chip = paired(chip_send, "blk")
    inner = pl.pallas_call(
        inner_kernel,
        out_shape=VOLUME,
        in_specs=[VMEM] * 3,
        out_specs=VMEM,
        compiler_params=PARAMS,
        cost_estimate=pl.CostEstimate(
            flops=40_000_000, bytes_accessed=6_000_000, transcendentals=0
        ),
    )(q, tab, params)
    pair_send, row_send = pl.pallas_call(
        second_kernel,
        out_shape=[FACE] * 2,
        in_specs=[VMEM] * 4 + [ANY] + [SMEM] * 2,
        out_specs=[VMEM] * 2,
        compiler_params=PARAMS,
    )(up, down, chip, blk, inner, core, row)
    beyond = swapped(row_send, "row", False)
    pair = paired(pair_send, "row")
    outward, own, same_chip, inward = pl.pallas_call(
        third_kernel,
        out_shape=[f32(n, VARS, 1, 512) for n in (2 * CAP, CAP, CAP, CAP)],
        in_specs=[VMEM] * 5 + [HBM] + [SMEM] * 2 + [VMEM] * 8,
        out_specs=[VMEM] * 4,
        scratch_shapes=[
            vmem(512, LANES),
            vmem(512, LANES),
            vmem(512, LANES),
            vmem(LANES, 1, 512),
            vmem(SPREAD * CAP, VARS, 1, 512),
            pltpu.SMEM((8,), jnp.int32),
            pltpu.SMEM((1, 1, 1, NB), jnp.int32),
            vmem(TAB_ROWS, LANES),
            vmem(64, LANES),
            sems(1),
        ],
        compiler_params=PARAMS,
    )(
        q, tab, params, inner, columns, jnp.transpose(migration, (0, 1, 3, 2)), core, row,
        *faces[:4], chip, blk, pair, beyond,
    )
    far = hopped(outward, True)
    near = hopped(inward, False)
    chip = paired(same_chip, "blk")
    relayed = paired(far, "blk")
    moved = pl.pallas_call(
        last_kernel,
        out_shape=f32(SPREAD * CAP, VARS, 1, 512),
        in_specs=[ANY] * 3 + [SMEM] + [ANY] * 2,
        out_specs=HBM,
        scratch_shapes=[sems(SPREAD)],
        compiler_params=PARAMS,
    )(far, own, near, core, chip, relayed)
    return jnp.transpose(moved, (2, 0, 1, 3)).reshape(1, 1, SPREAD * CAP, VARS, 512)


def solution(mesh):
    placed = (
        P("blk", "row", None, None),
        P("blk", "row"),
        P(None, "blk", "row"),
        P(None, "blk", "row"),
        P("blk", "row", None, None),
    )
    return jax.shard_map(
        local,
        mesh=mesh,
        in_specs=placed,
        out_specs=P("blk", "row", None, None, None),
        check_vma=False,
    )
```

```python
import jax
import jax.numpy as jnp
import ml_dtypes
import numpy as np
from jax import lax
from jax.experimental import pallas as pl
from jax.experimental.pallas import tpu as pltpu
from jax.sharding import PartitionSpec as P

PMAX = 7
PMIN = 3
VARS = 5
NQ = 8
NB = 16
SPREAD = 5
CAP = 5
LANES = 128

mean_flow = (0.4, 0.0, 0.2)
time_step = 0.008


def legendre_points(degree):
    point_count = degree + 1
    estimate = np.cos(np.pi * np.arange(point_count) / degree)
    for sweep_idx in range(40):
        values = np.zeros((point_count, point_count))
        values[:, 0] = 1.0
        values[:, 1] = estimate
        for order_idx in range(2, point_count):
            values[:, order_idx] = (
                (2 * order_idx - 1) * estimate * values[:, order_idx - 1]
                - (order_idx - 1) * values[:, order_idx - 2]
            ) / order_idx
        estimate = estimate - (estimate * values[:, degree] - values[:, degree - 1]) / (
            point_count * values[:, degree]
        )
    return np.sort(estimate)


def lagrange_matrix(points, targets):
    result = np.ones((len(targets), len(points)))
    for column in range(len(points)):
        for other_idx in range(len(points)):
            if other_idx != column:
                result[:, column] *= (targets - points[other_idx]) / (
                    points[column] - points[other_idx]
                )
    return result


def build_tables(lowest, highest):
    node_count = highest + 1
    level_count = highest - lowest + 1
    common = legendre_points(highest)
    derive = np.zeros((level_count, node_count, node_count))
    to_grid = np.zeros((level_count, node_count, node_count))
    from_grid = np.zeros((level_count, node_count, node_count))
    lifting = np.zeros((level_count,))
    last_node = np.zeros((level_count, node_count))
    active = np.zeros((level_count, node_count))
    for level_idx in range(level_count):
        degree = lowest + level_idx
        points = legendre_points(degree)
        filled = degree + 1
        weights = np.array(
            [
                1.0
                / np.prod(
                    [
                        points[column] - points[other_idx]
                        for other_idx in range(filled)
                        if other_idx != column
                    ]
                )
                for column in range(filled)
            ]
        )
        local_diff = np.zeros((filled, filled))
        for row_idx in range(filled):
            for column in range(filled):
                if column != row_idx:
                    local_diff[row_idx, column] = (
                        weights[column] / weights[row_idx] / (points[row_idx] - points[column])
                    )
            local_diff[row_idx, row_idx] = -np.sum(local_diff[row_idx])
        derive[level_idx, :filled, :filled] = local_diff
        to_grid[level_idx, :, :filled] = lagrange_matrix(points, common)
        from_grid[level_idx, :filled, :] = lagrange_matrix(common, points)
        lifting[level_idx] = degree * (degree + 1) / 2.0
        last_node[level_idx, degree] = 1.0
        active[level_idx, :filled] = 1.0
    return derive, to_grid, from_grid, lifting, last_node, active


D_AT, DK_AT, I_AT, IK_AT, B_AT, BK_AT, W_AT, A_AT, LIFT_AT, DLAST_AT = (
    0, 64, 128, 192, 256, 320, 384, 392, 400, 408)
TAB_ROWS = 416


def table_columns():
    derive, to_grid, from_grid, lifting, last_node, active = build_tables(PMIN, PMAX)
    rows = np.zeros((4 * LANES, 8))
    for level in range(PMAX - PMIN + 1):
        for at, turned_at, mat in (
            (D_AT, DK_AT, derive[level]),
            (I_AT, IK_AT, to_grid[level]),
            (B_AT, BK_AT, from_grid[level]),
        ):
            rows[at : at + 64, level] = mat.reshape(-1)
            for turn in range(8):
                for a in range(8):
                    rows[turned_at + turn * 8 + a, level] = mat[a, (a + turn) % 8]
        rows[W_AT : W_AT + 8, level] = last_node[level]
        rows[A_AT : A_AT + 8, level] = active[level]
        rows[LIFT_AT : LIFT_AT + 8, level] = lifting[level]
        rows[DLAST_AT : DLAST_AT + 8, level] = derive[level][PMIN + level]
    left, parts = rows.T.astype(np.float32), []
    for _ in range(3):
        parts.append(left.astype(ml_dtypes.bfloat16).astype(np.float32))
        left = left - parts[-1]
    return np.concatenate(parts)


def lane_ids():
    lane = lax.broadcasted_iota(jnp.int32, (8, LANES), 1)
    return lane, lane & 15, lane >> 4


def spread(read, dtype):
    _, elem, _ = lane_ids()
    out = jnp.zeros((8, LANES), dtype)
    for e in range(NB):
        out = jnp.where(elem == e, read(e // 4, e % 4), out)
    return out


def rolled(x, by):
    return pltpu.roll(x, by % LANES, 1)


def subrolled(x, by):
    return x if by % 8 == 0 else pltpu.roll(x, by % 8, 0)


def row_of(ref, at):
    return jnp.broadcast_to(ref[pl.ds(at, 1), :], (8, LANES))


def along_first(tab, at, face):
    out = []
    for a in range(8):
        total = row_of(tab, at + a * 8) * face[0]
        for j in range(1, 8):
            total = total + row_of(tab, at + a * 8 + j) * face[j]
        out.append(total)
    return out


def along_second(tab, at, face):
    coefs = [tab[pl.ds(at + 8 * turn, 8), :] for turn in range(8)]
    out = []
    for x in face:
        total = coefs[0] * x
        for turn in range(1, 8):
            total = total + coefs[turn] * subrolled(x, -turn)
        out.append(total)
    return out


def to_common(tab, face):
    return along_second(tab, IK_AT, along_first(tab, I_AT, face))


def from_common(tab, face):
    return along_second(tab, BK_AT, along_first(tab, B_AT, face))


def turned(face, codes, buf):
    for a in range(8):
        buf[pl.ds(8 * a, 8), :] = face[a]
    back = lax.broadcasted_iota(jnp.int32, (8, LANES), 0) * -1 + 7
    out = []
    for a in range(8):
        x = jnp.where(codes == 1, face[7 - a], face[a])
        x = jnp.where(codes == 2, jnp.take_along_axis(face[a], back, axis=0), x)
        x = jnp.where(codes == 3, buf[pl.ds(a, 8, stride=8), :], x)
        out.append(x)
    return out


def coupling_of(direction):
    lane, elem, var = lane_ids()
    vel = elem + 16 * (1 + direction)
    source = jnp.where((var == 0) | (var == 4), vel, lane)
    source = jnp.where(var == 1 + direction, elem + 64, source)
    has = (var == 0) | (var == 4) | (var == 1 + direction)
    return source, jnp.where(has, 1.0, 0.0).astype(jnp.float32)


def jump_with(gap, coupling, factor):
    source, has = coupling
    half = 0.5 * has
    return [factor * x + half * jnp.take_along_axis(x, source, axis=1) for x in gap]


def jump_factor(direction, sign):
    return 0.5 * (mean_flow[direction] + sign * (abs(mean_flow[direction]) + 1.0))


def jump_flux(gap, direction, sign):
    return jump_with(gap, coupling_of(direction), jump_factor(direction, sign))


def load_face(ref):
    return [ref[pl.ds(8 * a, 8), :] for a in range(8)]


def store_face(ref, face):
    for a in range(8):
        ref[pl.ds(8 * a, 8), :] = face[a]


def picked(tab, read):
    out = None
    for n in range(PMIN, NQ):
        w = row_of(tab, W_AT + n)
        layer = [w * x for x in read(n)]
        out = layer if out is None else [s + x for s, x in zip(out, layer)]
    return out


def node(i, j):
    return pl.ds((i * 8 + j) * 8, 8)


def x_faces(q, tab):
    low = [q[node(0, j), :] for j in range(8)]
    high = picked(tab, lambda n: [q[node(n, j), :] for j in range(8)])
    return low, high


def y_faces(q, tab):
    low = [q[node(i, 0), :] for i in range(8)]
    high = picked(tab, lambda n: [q[node(i, n), :] for i in range(8)])
    return low, high


def z_faces(q, tab):
    low = [q[pl.ds(i * 64, 8, stride=8), :] for i in range(8)]
    high = picked(tab, lambda n: [q[pl.ds(i * 64 + n, 8, stride=8), :] for i in range(8)])
    return low, high


def end_rows(q, tab, read):
    low = high = None
    for n in range(NQ):
        first, last = row_of(tab, D_AT + n), row_of(tab, DLAST_AT + n)
        layer = read(n)
        by_low, by_high = [first * x for x in layer], [last * x for x in layer]
        low = by_low if low is None else [a + b for a, b in zip(low, by_low)]
        high = by_high if high is None else [a + b for a, b in zip(high, by_high)]
    return low, high


def packed(kinds, where, shifts):
    out = []
    for a in range(8):
        x = rolled(kinds[3][a], shifts[3])
        for kind in range(3):
            x = jnp.where(where == kind, rolled(kinds[kind][a], shifts[kind]), x)
        out.append(x)
    return out


def make_messages(q, tab, order, metric, codes, first_core, outs, buf):
    tx_low, tx_high, ty_low, ty_high, chip_send, blk_send, up, down = outs
    _, elem, _ = lane_ids()
    x_ends, y_ends = x_faces(q, tab), y_faces(q, tab)
    tx = [turned(to_common(tab, x_ends[side]), codes[side], buf) for side in range(2)]
    ty = [to_common(tab, y_ends[side]) for side in range(2)]
    for ref, face in zip((tx_low, tx_high, ty_low, ty_high), tx + ty):
        store_face(ref, face)
    x_rows = end_rows(q, tab, lambda n: [q[node(n, j), :] for j in range(8)])
    y_rows = end_rows(q, tab, lambda n: [q[node(i, n), :] for i in range(8)])
    params = [order.astype(jnp.float32)] + metric
    zero = jnp.zeros((8, LANES), jnp.float32)

    def along_x(side, shifts):
        edge = 7 * side
        lines = [ty[0][edge], ty[1][edge]] + params + [codes[side].astype(jnp.float32), zero]
        return packed([tx[side], x_ends[side], x_rows[side], lines], elem >> 2, shifts)

    def along_y(side, shifts):
        edge = 7 * side
        lines = [tx[0][edge], tx[1][edge]] + params + [zero, zero]
        return packed([ty[side], y_ends[side], y_rows[side], lines], elem & 3, shifts)

    left = along_x(0, (0, 4, 8, 12))
    right = along_x(1, (-12, -8, -4, 0))
    store_face(chip_send, [jnp.where(first_core, r, l) for l, r in zip(left, right)])
    store_face(blk_send, [jnp.where(first_core, l, r) for l, r in zip(left, right)])
    store_face(down, along_y(0, (0, 1, 2, 3)))
    store_face(up, along_y(1, (-3, -2, -1, 0)))


def sides_of(paired_ref, other_ref, first):
    pair = load_face(paired_ref.at[jnp.where(first, 1, 0)])
    other = load_face(other_ref)
    before = [jnp.where(first, o, p) for o, p in zip(other, pair)]
    after = [jnp.where(first, p, o) for o, p in zip(other, pair)]
    return before, after


def places(core_ref, row_ref):
    return core_ref[0] == 0, lax.rem(row_ref[0], 2) == 0


def halo_step(messages, traces, wall, columns, tab, q_buf):
    left, right, below, above = messages
    lane, elem, var = lane_ids()
    group, pos = elem >> 2, elem & 3
    base = lane - elem
    across_rows = group >= 2
    is_high = (group & 1) == 0

    def collected(block, kind):
        at = base + jnp.where(across_rows, pos * 4 + kind, kind * 4 + pos)
        out = jnp.take_along_axis(left[block], at, axis=1)
        for g, message in ((1, right), (2, below), (3, above)):
            out = jnp.where(group == g, jnp.take_along_axis(message[block], at, axis=1), out)
        return out

    table_for(columns, collected(2, 3)[0:1, :], tab)
    lift = tab[pl.ds(LIFT_AT, 8), :]
    metric_x, metric_y, metric_z = [collected(3 + d, 3) for d in range(3)]
    metric_n = jnp.where(across_rows, metric_y, metric_x)
    metric_t = jnp.where(across_rows, metric_x, metric_y)
    codes = jnp.where(across_rows, 0.0, collected(6, 3)).astype(jnp.int32)
    by_x, by_y, by_z = [coupling_of(d) for d in range(3)]

    def mixed(a, b):
        return tuple(jnp.where(across_rows, y, x) for x, y in zip(a, b))

    couple_n, couple_t = mixed(by_x, by_y), mixed(by_y, by_x)

    def factor(d, sign):
        return jnp.float32(jump_factor(d, sign))

    factor_n = jnp.where(
        across_rows,
        jnp.where(is_high, factor(1, -1.0), factor(1, 1.0)),
        jnp.where(is_high, factor(0, -1.0), factor(0, 1.0)),
    )
    factor_t = [
        jnp.where(across_rows, factor(0, sign), factor(1, sign)) for sign in (1.0, -1.0)
    ]
    flow_n = jnp.where(across_rows, mean_flow[1], mean_flow[0])
    flow_t = jnp.where(across_rows, mean_flow[0], mean_flow[1])

    def flux(x, flow, coupling):
        source, has = coupling
        return flow * x + has * jnp.take_along_axis(x, source, axis=1)

    face = [collected(a, 1) for a in range(8)]
    slope = [collected(a, 2) for a in range(8)]
    tx_low, tx_high, ty_low, ty_high = traces
    at = jnp.where(group == 0, pos, jnp.where(group == 1, 12 + pos, 4 * pos))
    at = base + jnp.where(group == 3, 4 * pos + 3, at)
    near = []
    for a in range(8):
        out = jnp.take_along_axis(tx_low[a], at, axis=1)
        for g, trace in ((1, tx_high), (2, ty_low), (3, ty_high)):
            out = jnp.where(group == g, jnp.take_along_axis(trace[a], at, axis=1), out)
        near.append(out)
    gap = [n - f for n, f in zip(from_common(tab, near), face)]
    gap = jump_with(gap, couple_n, factor_n)
    scale = metric_n * lift * jnp.where(is_high, -1.0, 1.0)
    rate = [
        scale * g - metric_n * flux(d, flow_n, couple_n) for g, d in zip(gap, slope)
    ]
    by_t = along_first(tab, D_AT, face)
    by_k = along_second(tab, DK_AT, face)
    scale_z = metric_z * lift
    sub = lax.broadcasted_iota(jnp.int32, (8, LANES), 0)
    weights = tab[pl.ds(W_AT, 8), :]
    at_low = jnp.where(sub == 0, scale_z, 0.0)
    at_high = -scale_z * weights

    def at_k(x, k):
        return jnp.take_along_axis(x, jnp.full((8, LANES), k, jnp.int32), axis=0)

    for a in range(8):
        low = at_k(face[a], 0)
        high = row_of(tab, W_AT + PMIN) * at_k(face[a], PMIN)
        for n in range(PMIN + 1, NQ):
            high = high + row_of(tab, W_AT + n) * at_k(face[a], n)
        gap_low = jump_flux([high - low], 2, 1.0)[0]
        gap_high = jump_flux([low - high], 2, -1.0)[0]
        rate[a] = (
            rate[a]
            - metric_t * flux(by_t[a], flow_t, couple_t)
            - metric_z * flux(by_k[a], mean_flow[2], by_z)
            + at_low * gap_low
            + at_high * gap_high
        )
    line_low, line_high = collected(0, 3), collected(1, 3)
    flip = jnp.where(var == 2, -1.0, 1.0).astype(jnp.float32)

    def corners(side, block_below, block_above):
        at = base + jnp.where(elem == (4 if side == 0 else 7), 15, 3)
        if side == 1:
            at = base + jnp.where(elem == 3, 3, 15)
        return (
            jnp.take_along_axis(below[block_below], at, axis=1),
            jnp.take_along_axis(above[block_above], at, axis=1),
        )

    from_below, _ = corners(0, 7, 7)
    at_wall = jnp.where(wall, flip * line_low, from_below)
    from_below, from_above = corners(0, 6, 6)
    corner = jnp.where(
        across_rows, jnp.where(group == 2, from_below, from_above), at_wall
    )
    near_low = jnp.where(pos == 0, corner, rolled(line_high, 1))
    _, beyond = corners(1, 7, 7)
    from_below, from_above = corners(1, 6, 6)
    corner = jnp.where(across_rows, jnp.where(group == 2, from_below, from_above), beyond)
    near_high = jnp.where(pos == 3, corner, rolled(line_low, -1))
    near_low, near_high = along_second(tab, BK_AT, [near_low, near_high])
    own_high = row_of(tab, W_AT + PMIN) * face[PMIN]
    for n in range(PMIN + 1, NQ):
        own_high = own_high + row_of(tab, W_AT + n) * face[n]
    scale = metric_t * lift
    gap_low = scale * jump_with([near_low - face[0]], couple_t, factor_t[0])[0]
    gap_high = scale * jump_with([near_high - own_high], couple_t, factor_t[1])[0]
    rate[0] = rate[0] + gap_low
    for n in range(PMIN, NQ):
        rate[n] = rate[n] - row_of(tab, W_AT + n) * gap_high
    middle = [f + time_step * r for f, r in zip(face, rate)]
    return turned(to_common(tab, middle), codes, q_buf)


def from_halo(face):
    lane, elem, _ = lane_ids()
    base = lane - elem
    at_below = base + 8 + (elem >> 2)
    at_above = base + 12 + (elem >> 2)
    return (
        face,
        [rolled(x, 8) for x in face],
        [jnp.take_along_axis(x, at_below, axis=1) for x in face],
        [jnp.take_along_axis(x, at_above, axis=1) for x in face],
    )


def gaps_to(q, tab, lift, traces, arrived, wall, metric, out):
    tx_low, tx_high, ty_low, ty_high = traces
    from_left, from_right, from_below, from_above = arrived
    _, elem, var = lane_ids()
    scale = lift * metric[0]
    low, high = x_faces(q, tab)
    near = [
        jnp.where(elem < 4, r, rolled(t, 4))
        for r, t in zip(from_left, tx_high)
    ]
    gap = jump_flux([n - o for n, o in zip(from_common(tab, near), low)], 0, 1.0)
    for j in range(8):
        out[node(0, j), :] = out[node(0, j), :] + scale * gap[j]
    near = [
        jnp.where(elem >= 12, r, rolled(t, -4))
        for r, t in zip(from_right, tx_low)
    ]
    gap = jump_flux([n - o for n, o in zip(from_common(tab, near), high)], 0, -1.0)
    gap = [scale * x for x in gap]
    for n in range(PMIN, NQ):
        w = row_of(tab, W_AT + n)
        for j in range(8):
            out[node(n, j), :] = out[node(n, j), :] - w * gap[j]
    scale = lift * metric[1]
    low, high = y_faces(q, tab)
    own_low = ty_low
    flip = jnp.where(var == 2, -1.0, 1.0).astype(jnp.float32)
    first = (elem & 3) == 0
    near = [
        jnp.where(first, jnp.where(wall, flip * o, r), rolled(t, 1))
        for r, t, o in zip(from_below, ty_high, own_low)
    ]
    gap = jump_flux([n - o for n, o in zip(from_common(tab, near), low)], 1, 1.0)
    for i in range(8):
        out[node(i, 0), :] = out[node(i, 0), :] + scale * gap[i]
    near = [
        jnp.where((elem & 3) == 3, r, rolled(t, -1))
        for r, t in zip(from_above, own_low)
    ]
    gap = jump_flux([n - o for n, o in zip(from_common(tab, near), high)], 1, -1.0)
    gap = [scale * x for x in gap]
    for n in range(PMIN, NQ):
        w = row_of(tab, W_AT + n)
        for i in range(8):
            out[node(i, n), :] = out[node(i, n), :] - w * gap[i]


def span_terms(q, tab, lift, metric, out):
    scale = lift * metric[2]
    low, high = z_faces(q, tab)
    gap_low = jump_flux([h - o for h, o in zip(high, low)], 2, 1.0)
    gap_high = jump_flux([o - h for h, o in zip(high, low)], 2, -1.0)
    sub = lax.broadcasted_iota(jnp.int32, (8, LANES), 0)
    at_low = jnp.where(sub == 0, scale, 0.0)
    at_high = -scale * tab[pl.ds(W_AT, 8), :]
    for i in range(8):
        for j in range(8):
            pick = jnp.full((8, LANES), j, jnp.int32)
            lo = jnp.take_along_axis(gap_low[i], pick, axis=0)
            hi = jnp.take_along_axis(gap_high[i], pick, axis=0)
            out[node(i, j), :] = out[node(i, j), :] + at_low * lo + at_high * hi


def volume_terms(q, tab, metric, out):
    couplings = [coupling_of(d) for d in range(3)]

    def flux(x, d):
        source, has = couplings[d]
        y = metric[d] * x
        mixed = has * jnp.take_along_axis(y, source, axis=1)
        return mixed if mean_flow[d] == 0.0 else mean_flow[d] * y + mixed

    for j in range(8):
        face = [q[node(i, j), :] for i in range(8)]
        for i, x in enumerate(along_first(tab, D_AT, face)):
            out[node(i, j), :] = -flux(x, 0)
    for i in range(8):
        face = [q[node(i, j), :] for j in range(8)]
        by_y = along_first(tab, D_AT, face)
        by_z = along_second(tab, DK_AT, face)
        for j in range(8):
            out[node(i, j), :] = out[node(i, j), :] - (flux(by_y[j], 1) + flux(by_z[j], 2))


def all_metrics(metric_ref):
    return [spread(lambda x, y, d=d: metric_ref[d, x, y], jnp.float32) for d in range(3)]


def all_codes(turn_ref):
    return [spread(lambda x, y, s=s: turn_ref[s, x, y], jnp.int32) for s in range(2)]


def kept_metrics(params):
    return [params[pl.ds(8 * d, 8), :] for d in range(3)]


def kept_codes(params):
    return [params[pl.ds(24 + 8 * s, 8), :].astype(jnp.int32) for s in range(2)]


def table_for(columns, level_row, tab):
    level = (lax.broadcasted_iota(jnp.int32, (LANES, LANES), 0) & 7) + PMIN
    one_hot = jnp.where(
        level.astype(jnp.float32) == jnp.broadcast_to(level_row, (LANES, LANES)), 1.0, 0.0
    ).astype(jnp.bfloat16)
    pad = jnp.zeros((LANES - 24, LANES), jnp.float32)
    for part in range(4):
        at = part * LANES
        size = min(LANES, TAB_ROWS - at)
        block = jnp.concatenate([columns[:, pl.ds(at, LANES)], pad], axis=0).T
        tab[pl.ds(at, size), :] = jnp.dot(
            block.astype(jnp.bfloat16), one_hot, preferred_element_type=jnp.float32
        )[:size]


def fetched(pairs, sems):
    copies = [pltpu.make_async_copy(a, b, sems.at[n]) for n, (a, b) in enumerate(pairs)]
    for copy in copies:
        copy.start()
    return copies


def table_kernel(columns, orders_hbm, turn_hbm, metric_hbm, _, tab, params, *rest):
    orders, turn, metric_ref, sems = rest
    copies = fetched(
        [(orders_hbm, orders), (turn_hbm, turn), (metric_hbm, metric_ref)], sems
    )
    for copy in copies:
        copy.wait()
    order = spread(lambda x, y: orders[x, y].astype(jnp.float32), jnp.float32)
    for n, x in enumerate(all_metrics(metric_ref) + all_codes(turn) + [order]):
        params[pl.ds(8 * n, 8), :] = x.astype(jnp.float32)
    table_for(columns, order[0:1, :], tab)


def first_kernel(fields, tab, params, core_ref, row_ref, q, *rest):
    outs = rest[:8]
    flat, buf = rest[8:]
    flat[pl.ds(80, 48), :] = jnp.zeros((48, 512), jnp.float32)
    for v in range(VARS):
        for x in range(4):
            flat[pl.ds(v * 16 + x * 4, 4), :] = fields[x, v]
    in_k = tab[pl.ds(A_AT, 8), :]
    for part in range(4):
        block = flat[:, pl.ds(part * LANES, LANES)].T
        for half in range(2):
            in_ik = in_k * row_of(tab, A_AT + part * 2 + half)
            for j in range(8):
                at = (half * 8 + j) * 8
                q[node(part * 2 + half, j), :] = (
                    block[at : at + 8] * in_ik * row_of(tab, A_AT + j)
                )
    first_core, _ = places(core_ref, row_ref)
    order = params[pl.ds(40, 8), :]
    make_messages(
        q, tab, order, kept_metrics(params), kept_codes(params), first_core, outs, buf
    )


def inner_kernel(q, tab, params, rate):
    metric = kept_metrics(params)
    volume_terms(q, tab, metric, rate)
    span_terms(q, tab, tab[pl.ds(LIFT_AT, 8), :], metric, rate)


def second_kernel(up, down, chip, blk, inner, core_ref, row_ref, pair_send, row_send):
    first_core, even_row = places(core_ref, row_ref)
    left, right = sides_of(chip, blk, first_core)
    _, elem, _ = lane_ids()
    up, down = load_face(up), load_face(down)

    def with_corners(message, edge, y, line):
        at_left, at_right = elem == 3, elem == 15
        out = message[:6]
        out.append(
            jnp.where(
                at_left,
                rolled(left[edge], 3 - y),
                jnp.where(at_right, rolled(right[edge], 15 - y), message[6]),
            )
        )
        out.append(
            jnp.where(
                at_left,
                rolled(left[line], -9 - y),
                jnp.where(at_right, rolled(right[line], 3 - y), message[7]),
            )
        )
        return out

    up = with_corners(up, 7, 3, 1)
    down = with_corners(down, 0, 0, 0)
    store_face(pair_send, [jnp.where(even_row, u, d) for u, d in zip(up, down)])
    store_face(row_send, [jnp.where(even_row, d, u) for u, d in zip(up, down)])


def third_kernel(q, tab, params, inner, columns, migration_hbm, core_ref, row_ref, *rest):
    traces, arrived = rest[:4], rest[4:8]
    outs = rest[8:12]
    rate, middle, second, flat, slots, count, migration, halo_tab, buf, sems = rest[12:]
    copies = fetched([(migration_hbm, migration)], sems)
    first_core, even_row = places(core_ref, row_ref)
    wall = row_ref[0] == 0
    metric, codes = kept_metrics(params), kept_codes(params)
    lift = tab[pl.ds(LIFT_AT, 8), :]
    chip, blk, pair, row = arrived
    left, right = sides_of(chip, blk, first_core)
    below, above = sides_of(pair, row, even_row)
    own = [load_face(ref) for ref in traces]
    beside = halo_step((left, right, below, above), own, wall, columns, halo_tab, buf)
    near = (left, [rolled(x, 12) for x in right], below, [rolled(x, 3) for x in above])
    rate[...] = inner[...]
    gaps_to(q, tab, lift, own, near, wall, metric, rate)
    for n in range(64):
        at = pl.ds(8 * n, 8)
        middle[at, :] = q[at, :] + time_step * rate[at, :]
    x_ends, y_ends = x_faces(middle, tab), y_faces(middle, tab)
    own = [turned(to_common(tab, x_ends[side]), codes[side], buf) for side in range(2)]
    own = own + [to_common(tab, y_ends[side]) for side in range(2)]
    volume_terms(middle, tab, metric, second)
    span_terms(middle, tab, lift, metric, second)
    gaps_to(middle, tab, lift, own, from_halo(beside), wall, metric, second)
    copies[0].wait()
    for part in range(4):
        at = pl.ds(part * LANES, LANES)
        flat[:, 0, at] = ((0.5 * time_step) * (rate[at, :] + second[at, :])).T
    slots[...] = jnp.zeros_like(slots)
    for m in range(SPREAD):
        count[m] = 0
    for e in range(NB):
        m = migration[0, 0, 0, e]
        c = count[m]
        count[m] = c + 1
        slot = jnp.where(core_ref[0] == 0, m, SPREAD - 1 - m) * CAP + c
        for v in range(VARS):
            slots[slot, v] = flat[v * 16 + e]
    at = 0
    for out in outs:
        size = out.shape[0]
        out[...] = slots[pl.ds(at, size)]
        at += size


def last_kernel(far, own, near, core_ref, chip, relayed, out, sems):
    def put(groups):
        copies = [
            pltpu.make_async_copy(piece, out.at[pl.ds(m * CAP, CAP)], sems.at[m])
            for m, piece in enumerate(groups)
        ]
        for copy in copies:
            copy.start()
        for copy in copies:
            copy.wait()

    first = far.at[pl.ds(0, CAP)]

    @pl.when(core_ref[0] == 0)
    def _():
        put([first, chip.at[1], own, relayed.at[1, pl.ds(CAP, CAP)], near])

    @pl.when(core_ref[0] != 0)
    def _():
        put([near, relayed.at[0, pl.ds(CAP, CAP)], own, chip.at[0], first])


def f32(*shape):
    return jax.ShapeDtypeStruct(shape, jnp.float32)


VMEM = pl.BlockSpec(memory_space=pltpu.VMEM)
SMEM = pl.BlockSpec(memory_space=pltpu.SMEM)
HBM = pl.BlockSpec(memory_space=pltpu.HBM)
ANY = pl.BlockSpec(memory_space=pl.ANY)
PARAMS = pltpu.CompilerParams(vmem_limit_bytes=32 * 1024 * 1024)
FACE = f32(64, LANES)
VOLUME = f32(512, LANES)


def pairs_of(count, first):
    return [[n, n + 1] for n in range(first, count - 1, 2)]


def swapped(array, axis, wraps):
    count = lax.axis_size(axis)
    pairs = [(a, b) for a, b in pairs_of(count, 1)]
    if wraps:
        pairs.append((count - 1, 0))
    return lax.ppermute(array, axis, pairs + [(b, a) for a, b in pairs])


def paired(array, axis):
    return lax.all_gather(array, axis, axis_index_groups=pairs_of(lax.axis_size(axis), 0))


def hopped(array, outward):
    count = lax.axis_size("blk")
    step = [-2, 2] if outward else [2, -2]
    return lax.ppermute(array, "blk", [(n, (n + step[n % 2]) % count) for n in range(count)])


def vmem(*shape):
    return pltpu.VMEM(shape, jnp.float32)


def sems(count):
    return pltpu.SemaphoreType.DMA((count,))


def local(fields, orders, metric, face_turn, migration):
    by_var = jnp.transpose(fields, (0, 2, 1, 3))
    core = lax.rem(lax.axis_index("blk").astype(jnp.int32), 2).reshape(1)
    row = lax.axis_index("row").astype(jnp.int32).reshape(1)
    columns = jnp.asarray(table_columns())
    targets = jnp.transpose(migration, (0, 1, 3, 2))
    tab, params = pl.pallas_call(
        table_kernel,
        out_shape=[f32(TAB_ROWS, LANES), f32(48, LANES)],
        in_specs=[VMEM] + [HBM] * 3 + [ANY],
        out_specs=[VMEM] * 2,
        scratch_shapes=[
            pltpu.SMEM((4, 4), jnp.int32),
            pltpu.SMEM((2, 4, 4), jnp.int32),
            pltpu.SMEM((3, 4, 4), jnp.float32),
            sems(3),
        ],
        compiler_params=PARAMS,
    )(columns, orders, face_turn, metric, targets)
    q, *faces = pl.pallas_call(
        first_kernel,
        out_shape=[VOLUME] + [FACE] * 8,
        in_specs=[VMEM] * 3 + [SMEM] * 2,
        out_specs=[VMEM] * 9,
        scratch_shapes=[vmem(LANES, 512), vmem(64, LANES)],
        compiler_params=PARAMS,
    )(by_var, tab, params, core, row)
    chip_send, blk_send, up, down = faces[4:]
    blk = swapped(blk_send, "blk", True)
    chip = paired(chip_send, "blk")
    inner = pl.pallas_call(
        inner_kernel,
        out_shape=VOLUME,
        in_specs=[VMEM] * 3,
        out_specs=VMEM,
        compiler_params=PARAMS,
        cost_estimate=pl.CostEstimate(
            flops=40_000_000, bytes_accessed=6_000_000, transcendentals=0
        ),
    )(q, tab, params)
    pair_send, row_send = pl.pallas_call(
        second_kernel,
        out_shape=[FACE] * 2,
        in_specs=[VMEM] * 4 + [ANY] + [SMEM] * 2,
        out_specs=[VMEM] * 2,
        compiler_params=PARAMS,
    )(up, down, chip, blk, inner, core, row)
    beyond = swapped(row_send, "row", False)
    pair = paired(pair_send, "row")
    outward, own, same_chip, inward = pl.pallas_call(
        third_kernel,
        out_shape=[f32(n, VARS, 1, 512) for n in (2 * CAP, CAP, CAP, CAP)],
        in_specs=[VMEM] * 5 + [HBM] + [SMEM] * 2 + [VMEM] * 8,
        out_specs=[VMEM] * 4,
        scratch_shapes=[
            vmem(512, LANES),
            vmem(512, LANES),
            vmem(512, LANES),
            vmem(LANES, 1, 512),
            vmem(SPREAD * CAP, VARS, 1, 512),
            pltpu.SMEM((8,), jnp.int32),
            pltpu.SMEM((1, 1, 1, NB), jnp.int32),
            vmem(TAB_ROWS, LANES),
            vmem(64, LANES),
            sems(1),
        ],
        compiler_params=PARAMS,
    )(
        q, tab, params, inner, columns, targets, core, row,
        *faces[:4], chip, blk, pair, beyond,
    )
    far = hopped(outward, True)
    near = hopped(inward, False)
    chip = paired(same_chip, "blk")
    relayed = paired(far, "blk")
    moved = pl.pallas_call(
        last_kernel,
        out_shape=f32(SPREAD * CAP, VARS, 1, 512),
        in_specs=[ANY] * 3 + [SMEM] + [ANY] * 2,
        out_specs=HBM,
        scratch_shapes=[sems(SPREAD)],
        compiler_params=PARAMS,
    )(far, own, near, core, chip, relayed)
    return jnp.transpose(moved, (2, 0, 1, 3)).reshape(1, 1, SPREAD * CAP, VARS, 512)


def solution(mesh):
    placed = (
        P("blk", "row", None, None),
        P("blk", "row"),
        P(None, "blk", "row"),
        P(None, "blk", "row"),
        P("blk", "row", None, None),
    )
    return jax.shard_map(
        local,
        mesh=mesh,
        in_specs=placed,
        out_specs=P("blk", "row", None, None, None),
        check_vma=False,
    )
```

```python
import jax
import jax.numpy as jnp
import ml_dtypes
import numpy as np
from jax import lax
from jax.experimental import pallas as pl
from jax.experimental.pallas import tpu as pltpu
from jax.sharding import PartitionSpec as P

PMAX = 7
PMIN = 3
VARS = 5
NQ = 8
NB = 16
SPREAD = 5
CAP = 5
LANES = 128

mean_flow = (0.4, 0.0, 0.2)
time_step = 0.008


def legendre_points(degree):
    point_count = degree + 1
    estimate = np.cos(np.pi * np.arange(point_count) / degree)
    for sweep_idx in range(40):
        values = np.zeros((point_count, point_count))
        values[:, 0] = 1.0
        values[:, 1] = estimate
        for order_idx in range(2, point_count):
            values[:, order_idx] = (
                (2 * order_idx - 1) * estimate * values[:, order_idx - 1]
                - (order_idx - 1) * values[:, order_idx - 2]
            ) / order_idx
        estimate = estimate - (estimate * values[:, degree] - values[:, degree - 1]) / (
            point_count * values[:, degree]
        )
    return np.sort(estimate)


def lagrange_matrix(points, targets):
    result = np.ones((len(targets), len(points)))
    for column in range(len(points)):
        for other_idx in range(len(points)):
            if other_idx != column:
                result[:, column] *= (targets - points[other_idx]) / (
                    points[column] - points[other_idx]
                )
    return result


def build_tables(lowest, highest):
    node_count = highest + 1
    level_count = highest - lowest + 1
    common = legendre_points(highest)
    derive = np.zeros((level_count, node_count, node_count))
    to_grid = np.zeros((level_count, node_count, node_count))
    from_grid = np.zeros((level_count, node_count, node_count))
    lifting = np.zeros((level_count,))
    last_node = np.zeros((level_count, node_count))
    active = np.zeros((level_count, node_count))
    for level_idx in range(level_count):
        degree = lowest + level_idx
        points = legendre_points(degree)
        filled = degree + 1
        weights = np.array(
            [
                1.0
                / np.prod(
                    [
                        points[column] - points[other_idx]
                        for other_idx in range(filled)
                        if other_idx != column
                    ]
                )
                for column in range(filled)
            ]
        )
        local_diff = np.zeros((filled, filled))
        for row_idx in range(filled):
            for column in range(filled):
                if column != row_idx:
                    local_diff[row_idx, column] = (
                        weights[column] / weights[row_idx] / (points[row_idx] - points[column])
                    )
            local_diff[row_idx, row_idx] = -np.sum(local_diff[row_idx])
        derive[level_idx, :filled, :filled] = local_diff
        to_grid[level_idx, :, :filled] = lagrange_matrix(points, common)
        from_grid[level_idx, :filled, :] = lagrange_matrix(common, points)
        lifting[level_idx] = degree * (degree + 1) / 2.0
        last_node[level_idx, degree] = 1.0
        active[level_idx, :filled] = 1.0
    return derive, to_grid, from_grid, lifting, last_node, active


D_AT, DK_AT, I_AT, IK_AT, B_AT, BK_AT, W_AT, A_AT, LIFT_AT, DLAST_AT = (
    0, 64, 128, 192, 256, 320, 384, 392, 400, 408)
TAB_ROWS = 416


def table_columns():
    derive, to_grid, from_grid, lifting, last_node, active = build_tables(PMIN, PMAX)
    rows = np.zeros((4 * LANES, 8))
    for level in range(PMAX - PMIN + 1):
        for at, turned_at, mat in (
            (D_AT, DK_AT, derive[level]),
            (I_AT, IK_AT, to_grid[level]),
            (B_AT, BK_AT, from_grid[level]),
        ):
            rows[at : at + 64, level] = mat.reshape(-1)
            for turn in range(8):
                for a in range(8):
                    rows[turned_at + turn * 8 + a, level] = mat[a, (a + turn) % 8]
        rows[W_AT : W_AT + 8, level] = last_node[level]
        rows[A_AT : A_AT + 8, level] = active[level]
        rows[LIFT_AT : LIFT_AT + 8, level] = lifting[level]
        rows[DLAST_AT : DLAST_AT + 8, level] = derive[level][PMIN + level]
    left, parts = rows.T.astype(np.float32), []
    for _ in range(3):
        parts.append(left.astype(ml_dtypes.bfloat16).astype(np.float32))
        left = left - parts[-1]
    return np.concatenate(parts)


def lane_ids():
    lane = lax.broadcasted_iota(jnp.int32, (8, LANES), 1)
    return lane, lane & 15, lane >> 4


def spread(read, dtype):
    _, elem, _ = lane_ids()
    out = jnp.zeros((8, LANES), dtype)
    for e in range(NB):
        out = jnp.where(elem == e, read(e // 4, e % 4), out)
    return out


def rolled(x, by):
    return pltpu.roll(x, by % LANES, 1)


def subrolled(x, by):
    return x if by % 8 == 0 else pltpu.roll(x, by % 8, 0)


def row_of(ref, at):
    return jnp.broadcast_to(ref[pl.ds(at, 1), :], (8, LANES))


def along_first(tab, at, face):
    out = []
    for a in range(8):
        total = row_of(tab, at + a * 8) * face[0]
        for j in range(1, 8):
            total = total + row_of(tab, at + a * 8 + j) * face[j]
        out.append(total)
    return out


def along_second(tab, at, face):
    coefs = [tab[pl.ds(at + 8 * turn, 8), :] for turn in range(8)]
    out = []
    for x in face:
        total = coefs[0] * x
        for turn in range(1, 8):
            total = total + coefs[turn] * subrolled(x, -turn)
        out.append(total)
    return out


def to_common(tab, face):
    return along_second(tab, IK_AT, along_first(tab, I_AT, face))


def from_common(tab, face):
    return along_second(tab, BK_AT, along_first(tab, B_AT, face))


def turned(face, codes, buf):
    for a in range(8):
        buf[pl.ds(8 * a, 8), :] = face[a]
    back = lax.broadcasted_iota(jnp.int32, (8, LANES), 0) * -1 + 7
    out = []
    for a in range(8):
        x = jnp.where(codes == 1, face[7 - a], face[a])
        x = jnp.where(codes == 2, jnp.take_along_axis(face[a], back, axis=0), x)
        x = jnp.where(codes == 3, buf[pl.ds(a, 8, stride=8), :], x)
        out.append(x)
    return out


def coupling_of(direction):
    lane, elem, var = lane_ids()
    vel = elem + 16 * (1 + direction)
    source = jnp.where((var == 0) | (var == 4), vel, lane)
    source = jnp.where(var == 1 + direction, elem + 64, source)
    has = (var == 0) | (var == 4) | (var == 1 + direction)
    return source, jnp.where(has, 1.0, 0.0).astype(jnp.float32)


def jump_with(gap, coupling, factor):
    source, has = coupling
    half = 0.5 * has
    return [factor * x + half * jnp.take_along_axis(x, source, axis=1) for x in gap]


def jump_factor(direction, sign):
    return 0.5 * (mean_flow[direction] + sign * (abs(mean_flow[direction]) + 1.0))


def jump_flux(gap, direction, sign):
    return jump_with(gap, coupling_of(direction), jump_factor(direction, sign))


def load_face(ref):
    return [ref[pl.ds(8 * a, 8), :] for a in range(8)]


def store_face(ref, face):
    for a in range(8):
        ref[pl.ds(8 * a, 8), :] = face[a]


def picked(tab, read):
    out = None
    for n in range(PMIN, NQ):
        w = row_of(tab, W_AT + n)
        layer = [w * x for x in read(n)]
        out = layer if out is None else [s + x for s, x in zip(out, layer)]
    return out


def node(i, j):
    return pl.ds((i * 8 + j) * 8, 8)


def x_faces(q, tab):
    low = [q[node(0, j), :] for j in range(8)]
    high = picked(tab, lambda n: [q[node(n, j), :] for j in range(8)])
    return low, high


def y_faces(q, tab):
    low = [q[node(i, 0), :] for i in range(8)]
    high = picked(tab, lambda n: [q[node(i, n), :] for i in range(8)])
    return low, high


def z_faces(q, tab):
    low = [q[pl.ds(i * 64, 8, stride=8), :] for i in range(8)]
    high = picked(tab, lambda n: [q[pl.ds(i * 64 + n, 8, stride=8), :] for i in range(8)])
    return low, high


def end_rows(q, tab, read):
    low = high = None
    for n in range(NQ):
        first, last = row_of(tab, D_AT + n), row_of(tab, DLAST_AT + n)
        layer = read(n)
        by_low, by_high = [first * x for x in layer], [last * x for x in layer]
        low = by_low if low is None else [a + b for a, b in zip(low, by_low)]
        high = by_high if high is None else [a + b for a, b in zip(high, by_high)]
    return low, high


def packed(kinds, where, shifts):
    out = []
    for a in range(8):
        x = rolled(kinds[3][a], shifts[3])
        for kind in range(3):
            x = jnp.where(where == kind, rolled(kinds[kind][a], shifts[kind]), x)
        out.append(x)
    return out


def make_messages(q, tab, order, metric, codes, first_core, outs, buf):
    tx_low, tx_high, ty_low, ty_high, chip_send, blk_send, up, down = outs
    _, elem, _ = lane_ids()
    x_ends, y_ends = x_faces(q, tab), y_faces(q, tab)
    tx = [turned(to_common(tab, x_ends[side]), codes[side], buf) for side in range(2)]
    ty = [to_common(tab, y_ends[side]) for side in range(2)]
    for ref, face in zip((tx_low, tx_high, ty_low, ty_high), tx + ty):
        store_face(ref, face)
    x_rows = end_rows(q, tab, lambda n: [q[node(n, j), :] for j in range(8)])
    y_rows = end_rows(q, tab, lambda n: [q[node(i, n), :] for i in range(8)])
    params = [order.astype(jnp.float32)] + metric
    zero = jnp.zeros((8, LANES), jnp.float32)

    def along_x(side, shifts):
        edge = 7 * side
        lines = [ty[0][edge], ty[1][edge]] + params + [codes[side].astype(jnp.float32), zero]
        return packed([tx[side], x_ends[side], x_rows[side], lines], elem >> 2, shifts)

    def along_y(side, shifts):
        edge = 7 * side
        lines = [tx[0][edge], tx[1][edge]] + params + [zero, zero]
        return packed([ty[side], y_ends[side], y_rows[side], lines], elem & 3, shifts)

    left = along_x(0, (0, 4, 8, 12))
    right = along_x(1, (-12, -8, -4, 0))
    store_face(chip_send, [jnp.where(first_core, r, l) for l, r in zip(left, right)])
    store_face(blk_send, [jnp.where(first_core, l, r) for l, r in zip(left, right)])
    store_face(down, along_y(0, (0, 1, 2, 3)))
    store_face(up, along_y(1, (-3, -2, -1, 0)))


def sides_of(paired_ref, other_ref, first):
    pair = load_face(paired_ref.at[jnp.where(first, 1, 0)])
    other = load_face(other_ref)
    before = [jnp.where(first, o, p) for o, p in zip(other, pair)]
    after = [jnp.where(first, p, o) for o, p in zip(other, pair)]
    return before, after


def places(core_ref, row_ref):
    return core_ref[0] == 0, lax.rem(row_ref[0], 2) == 0


def halo_step(messages, traces, wall, columns, tab, q_buf):
    left, right, below, above = messages
    lane, elem, var = lane_ids()
    group, pos = elem >> 2, elem & 3
    base = lane - elem
    across_rows = group >= 2
    is_high = (group & 1) == 0

    def collected(block, kind):
        at = base + jnp.where(across_rows, pos * 4 + kind, kind * 4 + pos)
        out = jnp.take_along_axis(left[block], at, axis=1)
        for g, message in ((1, right), (2, below), (3, above)):
            out = jnp.where(group == g, jnp.take_along_axis(message[block], at, axis=1), out)
        return out

    table_for(columns, collected(2, 3)[0:1, :], tab)
    lift = tab[pl.ds(LIFT_AT, 8), :]
    metric_x, metric_y, metric_z = [collected(3 + d, 3) for d in range(3)]
    metric_n = jnp.where(across_rows, metric_y, metric_x)
    metric_t = jnp.where(across_rows, metric_x, metric_y)
    codes = jnp.where(across_rows, 0.0, collected(6, 3)).astype(jnp.int32)
    by_x, by_y, by_z = [coupling_of(d) for d in range(3)]

    def mixed(a, b):
        return tuple(jnp.where(across_rows, y, x) for x, y in zip(a, b))

    couple_n, couple_t = mixed(by_x, by_y), mixed(by_y, by_x)

    def factor(d, sign):
        return jnp.float32(jump_factor(d, sign))

    factor_n = jnp.where(
        across_rows,
        jnp.where(is_high, factor(1, -1.0), factor(1, 1.0)),
        jnp.where(is_high, factor(0, -1.0), factor(0, 1.0)),
    )
    factor_t = [
        jnp.where(across_rows, factor(0, sign), factor(1, sign)) for sign in (1.0, -1.0)
    ]
    flow_n = jnp.where(across_rows, mean_flow[1], mean_flow[0])
    flow_t = jnp.where(across_rows, mean_flow[0], mean_flow[1])

    def flux(x, flow, coupling):
        source, has = coupling
        return flow * x + has * jnp.take_along_axis(x, source, axis=1)

    face = [collected(a, 1) for a in range(8)]
    slope = [collected(a, 2) for a in range(8)]
    tx_low, tx_high, ty_low, ty_high = traces
    at = jnp.where(group == 0, pos, jnp.where(group == 1, 12 + pos, 4 * pos))
    at = base + jnp.where(group == 3, 4 * pos + 3, at)
    near = []
    for a in range(8):
        out = jnp.take_along_axis(tx_low[a], at, axis=1)
        for g, trace in ((1, tx_high), (2, ty_low), (3, ty_high)):
            out = jnp.where(group == g, jnp.take_along_axis(trace[a], at, axis=1), out)
        near.append(out)
    gap = [n - f for n, f in zip(from_common(tab, near), face)]
    gap = jump_with(gap, couple_n, factor_n)
    scale = metric_n * lift * jnp.where(is_high, -1.0, 1.0)
    rate = [
        scale * g - metric_n * flux(d, flow_n, couple_n) for g, d in zip(gap, slope)
    ]
    by_t = along_first(tab, D_AT, face)
    by_k = along_second(tab, DK_AT, face)
    scale_z = metric_z * lift
    sub = lax.broadcasted_iota(jnp.int32, (8, LANES), 0)
    weights = tab[pl.ds(W_AT, 8), :]
    at_low = jnp.where(sub == 0, scale_z, 0.0)
    at_high = -scale_z * weights

    def at_k(x, k):
        return jnp.take_along_axis(x, jnp.full((8, LANES), k, jnp.int32), axis=0)

    for a in range(8):
        low = at_k(face[a], 0)
        high = row_of(tab, W_AT + PMIN) * at_k(face[a], PMIN)
        for n in range(PMIN + 1, NQ):
            high = high + row_of(tab, W_AT + n) * at_k(face[a], n)
        gap_low = jump_flux([high - low], 2, 1.0)[0]
        gap_high = jump_flux([low - high], 2, -1.0)[0]
        rate[a] = (
            rate[a]
            - metric_t * flux(by_t[a], flow_t, couple_t)
            - metric_z * flux(by_k[a], mean_flow[2], by_z)
            + at_low * gap_low
            + at_high * gap_high
        )
    line_low, line_high = collected(0, 3), collected(1, 3)
    flip = jnp.where(var == 2, -1.0, 1.0).astype(jnp.float32)

    def corners(side, block_below, block_above):
        at = base + jnp.where(elem == (4 if side == 0 else 7), 15, 3)
        if side == 1:
            at = base + jnp.where(elem == 3, 3, 15)
        return (
            jnp.take_along_axis(below[block_below], at, axis=1),
            jnp.take_along_axis(above[block_above], at, axis=1),
        )

    from_below, _ = corners(0, 7, 7)
    at_wall = jnp.where(wall, flip * line_low, from_below)
    from_below, from_above = corners(0, 6, 6)
    corner = jnp.where(
        across_rows, jnp.where(group == 2, from_below, from_above), at_wall
    )
    near_low = jnp.where(pos == 0, corner, rolled(line_high, 1))
    _, beyond = corners(1, 7, 7)
    from_below, from_above = corners(1, 6, 6)
    corner = jnp.where(across_rows, jnp.where(group == 2, from_below, from_above), beyond)
    near_high = jnp.where(pos == 3, corner, rolled(line_low, -1))
    near_low, near_high = along_second(tab, BK_AT, [near_low, near_high])
    own_high = row_of(tab, W_AT + PMIN) * face[PMIN]
    for n in range(PMIN + 1, NQ):
        own_high = own_high + row_of(tab, W_AT + n) * face[n]
    scale = metric_t * lift
    gap_low = scale * jump_with([near_low - face[0]], couple_t, factor_t[0])[0]
    gap_high = scale * jump_with([near_high - own_high], couple_t, factor_t[1])[0]
    rate[0] = rate[0] + gap_low
    for n in range(PMIN, NQ):
        rate[n] = rate[n] - row_of(tab, W_AT + n) * gap_high
    middle = [f + time_step * r for f, r in zip(face, rate)]
    return turned(to_common(tab, middle), codes, q_buf)


def from_halo(face):
    lane, elem, _ = lane_ids()
    base = lane - elem
    at_below = base + 8 + (elem >> 2)
    at_above = base + 12 + (elem >> 2)
    return (
        face,
        [rolled(x, 8) for x in face],
        [jnp.take_along_axis(x, at_below, axis=1) for x in face],
        [jnp.take_along_axis(x, at_above, axis=1) for x in face],
    )


def gaps_to(q, tab, lift, traces, arrived, wall, metric, out):
    tx_low, tx_high, ty_low, ty_high = traces
    from_left, from_right, from_below, from_above = arrived
    _, elem, var = lane_ids()
    scale = lift * metric[0]
    low, high = x_faces(q, tab)
    near = [
        jnp.where(elem < 4, r, rolled(t, 4))
        for r, t in zip(from_left, tx_high)
    ]
    gap = jump_flux([n - o for n, o in zip(from_common(tab, near), low)], 0, 1.0)
    for j in range(8):
        out[node(0, j), :] = out[node(0, j), :] + scale * gap[j]
    near = [
        jnp.where(elem >= 12, r, rolled(t, -4))
        for r, t in zip(from_right, tx_low)
    ]
    gap = jump_flux([n - o for n, o in zip(from_common(tab, near), high)], 0, -1.0)
    gap = [scale * x for x in gap]
    for n in range(PMIN, NQ):
        w = row_of(tab, W_AT + n)
        for j in range(8):
            out[node(n, j), :] = out[node(n, j), :] - w * gap[j]
    scale = lift * metric[1]
    low, high = y_faces(q, tab)
    own_low = ty_low
    flip = jnp.where(var == 2, -1.0, 1.0).astype(jnp.float32)
    first = (elem & 3) == 0
    near = [
        jnp.where(first, jnp.where(wall, flip * o, r), rolled(t, 1))
        for r, t, o in zip(from_below, ty_high, own_low)
    ]
    gap = jump_flux([n - o for n, o in zip(from_common(tab, near), low)], 1, 1.0)
    for i in range(8):
        out[node(i, 0), :] = out[node(i, 0), :] + scale * gap[i]
    near = [
        jnp.where((elem & 3) == 3, r, rolled(t, -1))
        for r, t in zip(from_above, own_low)
    ]
    gap = jump_flux([n - o for n, o in zip(from_common(tab, near), high)], 1, -1.0)
    gap = [scale * x for x in gap]
    for n in range(PMIN, NQ):
        w = row_of(tab, W_AT + n)
        for i in range(8):
            out[node(i, n), :] = out[node(i, n), :] - w * gap[i]


def span_terms(q, tab, lift, metric, out):
    scale = lift * metric[2]
    low, high = z_faces(q, tab)
    gap_low = jump_flux([h - o for h, o in zip(high, low)], 2, 1.0)
    gap_high = jump_flux([o - h for h, o in zip(high, low)], 2, -1.0)
    sub = lax.broadcasted_iota(jnp.int32, (8, LANES), 0)
    at_low = jnp.where(sub == 0, scale, 0.0)
    at_high = -scale * tab[pl.ds(W_AT, 8), :]
    for i in range(8):
        for j in range(8):
            pick = jnp.full((8, LANES), j, jnp.int32)
            lo = jnp.take_along_axis(gap_low[i], pick, axis=0)
            hi = jnp.take_along_axis(gap_high[i], pick, axis=0)
            out[node(i, j), :] = out[node(i, j), :] + at_low * lo + at_high * hi


def volume_terms(q, tab, metric, out):
    couplings = [coupling_of(d) for d in range(3)]

    def flux(x, d):
        source, has = couplings[d]
        y = metric[d] * x
        mixed = has * jnp.take_along_axis(y, source, axis=1)
        return mixed if mean_flow[d] == 0.0 else mean_flow[d] * y + mixed

    for j in range(8):
        face = [q[node(i, j), :] for i in range(8)]
        for i, x in enumerate(along_first(tab, D_AT, face)):
            out[node(i, j), :] = -flux(x, 0)
    for i in range(8):
        face = [q[node(i, j), :] for j in range(8)]
        by_y = along_first(tab, D_AT, face)
        by_z = along_second(tab, DK_AT, face)
        for j in range(8):
            out[node(i, j), :] = out[node(i, j), :] - (flux(by_y[j], 1) + flux(by_z[j], 2))


def all_metrics(metric_ref):
    return [spread(lambda x, y, d=d: metric_ref[d, x, y], jnp.float32) for d in range(3)]


def all_codes(turn_ref):
    return [spread(lambda x, y, s=s: turn_ref[s, x, y], jnp.int32) for s in range(2)]


def kept_metrics(params):
    return [params[pl.ds(8 * d, 8), :] for d in range(3)]


def kept_codes(params):
    return [params[pl.ds(24 + 8 * s, 8), :].astype(jnp.int32) for s in range(2)]


def table_for(columns, level_row, tab):
    level = (lax.broadcasted_iota(jnp.int32, (LANES, LANES), 0) & 7) + PMIN
    one_hot = jnp.where(
        level.astype(jnp.float32) == jnp.broadcast_to(level_row, (LANES, LANES)), 1.0, 0.0
    ).astype(jnp.bfloat16)
    pad = jnp.zeros((LANES - 24, LANES), jnp.float32)
    for part in range(4):
        at = part * LANES
        size = min(LANES, TAB_ROWS - at)
        block = jnp.concatenate([columns[:, pl.ds(at, LANES)], pad], axis=0).T
        tab[pl.ds(at, size), :] = jnp.dot(
            block.astype(jnp.bfloat16), one_hot, preferred_element_type=jnp.float32
        )[:size]


def fetched(pairs, sems):
    copies = [pltpu.make_async_copy(a, b, sems.at[n]) for n, (a, b) in enumerate(pairs)]
    for copy in copies:
        copy.start()
    return copies


def first_kernel(
    fields, columns, orders_hbm, turn_hbm, metric_hbm, _, core_ref, row_ref, q, tab, params, *rest
):
    outs = rest[:8]
    flat, buf, orders, turn, metric_ref, sems = rest[8:]
    copies = fetched(
        [(orders_hbm, orders), (turn_hbm, turn), (metric_hbm, metric_ref)], sems
    )
    flat[pl.ds(80, 48), :] = jnp.zeros((48, 512), jnp.float32)
    for v in range(VARS):
        for x in range(4):
            flat[pl.ds(v * 16 + x * 4, 4), :] = fields[x, v]
    for copy in copies:
        copy.wait()
    order = spread(lambda x, y: orders[x, y].astype(jnp.float32), jnp.float32)
    metric, codes = all_metrics(metric_ref), all_codes(turn)
    for n, x in enumerate(metric + codes):
        params[pl.ds(8 * n, 8), :] = x.astype(jnp.float32)
    table_for(columns, order[0:1, :], tab)
    in_k = tab[pl.ds(A_AT, 8), :]
    for part in range(4):
        block = flat[:, pl.ds(part * LANES, LANES)].T
        for half in range(2):
            in_ik = in_k * row_of(tab, A_AT + part * 2 + half)
            for j in range(8):
                at = (half * 8 + j) * 8
                q[node(part * 2 + half, j), :] = (
                    block[at : at + 8] * in_ik * row_of(tab, A_AT + j)
                )
    first_core, _ = places(core_ref, row_ref)
    make_messages(q, tab, order, metric, codes, first_core, outs, buf)


def inner_kernel(q, tab, params, rate):
    metric = kept_metrics(params)
    volume_terms(q, tab, metric, rate)
    span_terms(q, tab, tab[pl.ds(LIFT_AT, 8), :], metric, rate)


def second_kernel(up, down, chip, blk, inner, core_ref, row_ref, pair_send, row_send):
    first_core, even_row = places(core_ref, row_ref)
    left, right = sides_of(chip, blk, first_core)
    _, elem, _ = lane_ids()
    up, down = load_face(up), load_face(down)

    def with_corners(message, edge, y, line):
        at_left, at_right = elem == 3, elem == 15
        out = message[:6]
        out.append(
            jnp.where(
                at_left,
                rolled(left[edge], 3 - y),
                jnp.where(at_right, rolled(right[edge], 15 - y), message[6]),
            )
        )
        out.append(
            jnp.where(
                at_left,
                rolled(left[line], -9 - y),
                jnp.where(at_right, rolled(right[line], 3 - y), message[7]),
            )
        )
        return out

    up = with_corners(up, 7, 3, 1)
    down = with_corners(down, 0, 0, 0)
    store_face(pair_send, [jnp.where(even_row, u, d) for u, d in zip(up, down)])
    store_face(row_send, [jnp.where(even_row, d, u) for u, d in zip(up, down)])


def third_kernel(q, tab, params, inner, columns, migration_hbm, core_ref, row_ref, *rest):
    traces, arrived = rest[:4], rest[4:8]
    outs = rest[8:12]
    rate, middle, second, flat, slots, count, migration, halo_tab, buf, sems = rest[12:]
    copies = fetched([(migration_hbm, migration)], sems)
    first_core, even_row = places(core_ref, row_ref)
    wall = row_ref[0] == 0
    metric, codes = kept_metrics(params), kept_codes(params)
    lift = tab[pl.ds(LIFT_AT, 8), :]
    chip, blk, pair, row = arrived
    left, right = sides_of(chip, blk, first_core)
    below, above = sides_of(pair, row, even_row)
    own = [load_face(ref) for ref in traces]
    beside = halo_step((left, right, below, above), own, wall, columns, halo_tab, buf)
    near = (left, [rolled(x, 12) for x in right], below, [rolled(x, 3) for x in above])
    rate[...] = inner[...]
    gaps_to(q, tab, lift, own, near, wall, metric, rate)
    for n in range(64):
        at = pl.ds(8 * n, 8)
        middle[at, :] = q[at, :] + time_step * rate[at, :]
    x_ends, y_ends = x_faces(middle, tab), y_faces(middle, tab)
    own = [turned(to_common(tab, x_ends[side]), codes[side], buf) for side in range(2)]
    own = own + [to_common(tab, y_ends[side]) for side in range(2)]
    volume_terms(middle, tab, metric, second)
    span_terms(middle, tab, lift, metric, second)
    gaps_to(middle, tab, lift, own, from_halo(beside), wall, metric, second)
    copies[0].wait()
    for part in range(4):
        at = pl.ds(part * LANES, LANES)
        flat[:, 0, at] = ((0.5 * time_step) * (rate[at, :] + second[at, :])).T
    slots[...] = jnp.zeros_like(slots)
    for m in range(SPREAD):
        count[m] = 0
    for e in range(NB):
        m = migration[0, 0, 0, e]
        c = count[m]
        count[m] = c + 1
        slot = jnp.where(core_ref[0] == 0, m, SPREAD - 1 - m) * CAP + c
        for v in range(VARS):
            slots[slot, v] = flat[v * 16 + e]
    at = 0
    for out in outs:
        size = out.shape[0]
        out[...] = slots[pl.ds(at, size)]
        at += size


def last_kernel(far, own, near, core_ref, chip, relayed, out, sems):
    def put(groups):
        copies = [
            pltpu.make_async_copy(piece, out.at[pl.ds(m * CAP, CAP)], sems.at[m])
            for m, piece in enumerate(groups)
        ]
        for copy in copies:
            copy.start()
        for copy in copies:
            copy.wait()

    first = far.at[pl.ds(0, CAP)]

    @pl.when(core_ref[0] == 0)
    def _():
        put([first, chip.at[1], own, relayed.at[1, pl.ds(CAP, CAP)], near])

    @pl.when(core_ref[0] != 0)
    def _():
        put([near, relayed.at[0, pl.ds(CAP, CAP)], own, chip.at[0], first])


def f32(*shape):
    return jax.ShapeDtypeStruct(shape, jnp.float32)


VMEM = pl.BlockSpec(memory_space=pltpu.VMEM)
SMEM = pl.BlockSpec(memory_space=pltpu.SMEM)
HBM = pl.BlockSpec(memory_space=pltpu.HBM)
ANY = pl.BlockSpec(memory_space=pl.ANY)
PARAMS = pltpu.CompilerParams(vmem_limit_bytes=32 * 1024 * 1024)
FACE = f32(64, LANES)
VOLUME = f32(512, LANES)


def pairs_of(count, first):
    return [[n, n + 1] for n in range(first, count - 1, 2)]


def swapped(array, axis, wraps):
    count = lax.axis_size(axis)
    pairs = [(a, b) for a, b in pairs_of(count, 1)]
    if wraps:
        pairs.append((count - 1, 0))
    return lax.ppermute(array, axis, pairs + [(b, a) for a, b in pairs])


def paired(array, axis):
    return lax.all_gather(array, axis, axis_index_groups=pairs_of(lax.axis_size(axis), 0))


def hopped(array, outward):
    count = lax.axis_size("blk")
    step = [-2, 2] if outward else [2, -2]
    return lax.ppermute(array, "blk", [(n, (n + step[n % 2]) % count) for n in range(count)])


def vmem(*shape):
    return pltpu.VMEM(shape, jnp.float32)


def sems(count):
    return pltpu.SemaphoreType.DMA((count,))


def local(fields, orders, metric, face_turn, migration):
    by_var = jnp.transpose(fields, (0, 2, 1, 3))
    core = lax.rem(lax.axis_index("blk").astype(jnp.int32), 2).reshape(1)
    row = lax.axis_index("row").astype(jnp.int32).reshape(1)
    columns = jnp.asarray(table_columns())
    targets = jnp.transpose(migration, (0, 1, 3, 2))
    q, tab, params, *faces = pl.pallas_call(
        first_kernel,
        out_shape=[VOLUME, f32(TAB_ROWS, LANES), f32(40, LANES)] + [FACE] * 8,
        in_specs=[VMEM] * 2 + [HBM] * 3 + [ANY] + [SMEM] * 2,
        out_specs=[VMEM] * 11,
        scratch_shapes=[
            vmem(LANES, 512),
            vmem(64, LANES),
            pltpu.SMEM((4, 4), jnp.int32),
            pltpu.SMEM((2, 4, 4), jnp.int32),
            pltpu.SMEM((3, 4, 4), jnp.float32),
            sems(3),
        ],
        compiler_params=PARAMS,
    )(by_var, columns, orders, face_turn, metric, targets, core, row)
    chip_send, blk_send, up, down = faces[4:]
    blk = swapped(blk_send, "blk", True)
    chip = paired(chip_send, "blk")
    inner = pl.pallas_call(
        inner_kernel,
        out_shape=VOLUME,
        in_specs=[VMEM] * 3,
        out_specs=VMEM,
        compiler_params=PARAMS,
        cost_estimate=pl.CostEstimate(
            flops=40_000_000, bytes_accessed=6_000_000, transcendentals=0
        ),
    )(q, tab, params)
    pair_send, row_send = pl.pallas_call(
        second_kernel,
        out_shape=[FACE] * 2,
        in_specs=[VMEM] * 4 + [ANY] + [SMEM] * 2,
        out_specs=[VMEM] * 2,
        compiler_params=PARAMS,
    )(up, down, chip, blk, inner, core, row)
    beyond = swapped(row_send, "row", False)
    pair = paired(pair_send, "row")
    outward, own, same_chip, inward = pl.pallas_call(
        third_kernel,
        out_shape=[f32(n, VARS, 1, 512) for n in (2 * CAP, CAP, CAP, CAP)],
        in_specs=[VMEM] * 5 + [HBM] + [SMEM] * 2 + [VMEM] * 8,
        out_specs=[VMEM] * 4,
        scratch_shapes=[
            vmem(512, LANES),
            vmem(512, LANES),
            vmem(512, LANES),
            vmem(LANES, 1, 512),
            vmem(SPREAD * CAP, VARS, 1, 512),
            pltpu.SMEM((8,), jnp.int32),
            pltpu.SMEM((1, 1, 1, NB), jnp.int32),
            vmem(TAB_ROWS, LANES),
            vmem(64, LANES),
            sems(1),
        ],
        compiler_params=PARAMS,
    )(
        q, tab, params, inner, columns, targets, core, row,
        *faces[:4], chip, blk, pair, beyond,
    )
    far = hopped(outward, True)
    near = hopped(inward, False)
    chip = paired(same_chip, "blk")
    relayed = paired(far, "blk")
    moved = pl.pallas_call(
        last_kernel,
        out_shape=f32(SPREAD * CAP, VARS, 1, 512),
        in_specs=[ANY] * 3 + [SMEM] + [ANY] * 2,
        out_specs=HBM,
        scratch_shapes=[sems(SPREAD)],
        compiler_params=PARAMS,
    )(far, own, near, core, chip, relayed)
    return jnp.transpose(moved, (2, 0, 1, 3)).reshape(1, 1, SPREAD * CAP, VARS, 512)


def solution(mesh):
    placed = (
        P("blk", "row", None, None),
        P("blk", "row"),
        P(None, "blk", "row"),
        P(None, "blk", "row"),
        P("blk", "row", None, None),
    )
    return jax.shard_map(
        local,
        mesh=mesh,
        in_specs=placed,
        out_specs=P("blk", "row", None, None, None),
        check_vma=False,
    )
```

```python
import jax
import jax.numpy as jnp
import numpy as np
from jax import lax
from jax.experimental import pallas as pl
from jax.experimental.pallas import tpu as pltpu
from jax.sharding import PartitionSpec as P

PMAX = 7
PMIN = 3
VARS = 5
NQ = 8
NB = 16
SPREAD = 5
CAP = 5
LANES = 128

mean_flow = (0.4, 0.0, 0.2)
time_step = 0.008


def legendre_points(degree):
    point_count = degree + 1
    estimate = np.cos(np.pi * np.arange(point_count) / degree)
    for sweep_idx in range(40):
        values = np.zeros((point_count, point_count))
        values[:, 0] = 1.0
        values[:, 1] = estimate
        for order_idx in range(2, point_count):
            values[:, order_idx] = (
                (2 * order_idx - 1) * estimate * values[:, order_idx - 1]
                - (order_idx - 1) * values[:, order_idx - 2]
            ) / order_idx
        estimate = estimate - (estimate * values[:, degree] - values[:, degree - 1]) / (
            point_count * values[:, degree]
        )
    return np.sort(estimate)


def lagrange_matrix(points, targets):
    result = np.ones((len(targets), len(points)))
    for column in range(len(points)):
        for other_idx in range(len(points)):
            if other_idx != column:
                result[:, column] *= (targets - points[other_idx]) / (
                    points[column] - points[other_idx]
                )
    return result


def build_tables(lowest, highest):
    node_count = highest + 1
    level_count = highest - lowest + 1
    common = legendre_points(highest)
    derive = np.zeros((level_count, node_count, node_count))
    to_grid = np.zeros((level_count, node_count, node_count))
    from_grid = np.zeros((level_count, node_count, node_count))
    lifting = np.zeros((level_count,))
    last_node = np.zeros((level_count, node_count))
    active = np.zeros((level_count, node_count))
    for level_idx in range(level_count):
        degree = lowest + level_idx
        points = legendre_points(degree)
        filled = degree + 1
        weights = np.array(
            [
                1.0
                / np.prod(
                    [
                        points[column] - points[other_idx]
                        for other_idx in range(filled)
                        if other_idx != column
                    ]
                )
                for column in range(filled)
            ]
        )
        local_diff = np.zeros((filled, filled))
        for row_idx in range(filled):
            for column in range(filled):
                if column != row_idx:
                    local_diff[row_idx, column] = (
                        weights[column] / weights[row_idx] / (points[row_idx] - points[column])
                    )
            local_diff[row_idx, row_idx] = -np.sum(local_diff[row_idx])
        derive[level_idx, :filled, :filled] = local_diff
        to_grid[level_idx, :, :filled] = lagrange_matrix(points, common)
        from_grid[level_idx, :filled, :] = lagrange_matrix(common, points)
        lifting[level_idx] = degree * (degree + 1) / 2.0
        last_node[level_idx, degree] = 1.0
        active[level_idx, :filled] = 1.0
    return derive, to_grid, from_grid, lifting, last_node, active


D_AT, DK_AT, I_AT, IK_AT, B_AT, BK_AT, W_AT, A_AT, LIFT_AT, DLAST_AT = (
    0, 64, 128, 192, 256, 320, 384, 392, 400, 408)
TAB_ROWS = 416


def table_columns():
    derive, to_grid, from_grid, lifting, last_node, active = build_tables(PMIN, PMAX)
    rows = np.zeros((4 * LANES, 8))
    for level in range(PMAX - PMIN + 1):
        for at, turned_at, mat in (
            (D_AT, DK_AT, derive[level]),
            (I_AT, IK_AT, to_grid[level]),
            (B_AT, BK_AT, from_grid[level]),
        ):
            rows[at : at + 64, level] = mat.reshape(-1)
            for turn in range(8):
                for a in range(8):
                    rows[turned_at + turn * 8 + a, level] = mat[a, (a + turn) % 8]
        rows[W_AT : W_AT + 8, level] = last_node[level]
        rows[A_AT : A_AT + 8, level] = active[level]
        rows[LIFT_AT : LIFT_AT + 8, level] = lifting[level]
        rows[DLAST_AT : DLAST_AT + 8, level] = derive[level][PMIN + level]
    return np.ascontiguousarray(rows.T).astype(np.float32)


def lane_ids():
    lane = lax.broadcasted_iota(jnp.int32, (8, LANES), 1)
    return lane, lane & 15, lane >> 4


def spread(read, dtype):
    _, elem, _ = lane_ids()
    out = jnp.zeros((8, LANES), dtype)
    for e in range(NB):
        out = jnp.where(elem == e, read(e // 4, e % 4), out)
    return out


def rolled(x, by):
    return pltpu.roll(x, by % LANES, 1)


def subrolled(x, by):
    return x if by % 8 == 0 else pltpu.roll(x, by % 8, 0)


def row_of(ref, at):
    return jnp.broadcast_to(ref[pl.ds(at, 1), :], (8, LANES))


def along_first(tab, at, face):
    out = []
    for a in range(8):
        total = row_of(tab, at + a * 8) * face[0]
        for j in range(1, 8):
            total = total + row_of(tab, at + a * 8 + j) * face[j]
        out.append(total)
    return out


def along_second(tab, at, face):
    coefs = [tab[pl.ds(at + 8 * turn, 8), :] for turn in range(8)]
    out = []
    for x in face:
        total = coefs[0] * x
        for turn in range(1, 8):
            total = total + coefs[turn] * subrolled(x, -turn)
        out.append(total)
    return out


def to_common(tab, face):
    return along_second(tab, IK_AT, along_first(tab, I_AT, face))


def from_common(tab, face):
    return along_second(tab, BK_AT, along_first(tab, B_AT, face))


def turned(face, codes, buf):
    for a in range(8):
        buf[pl.ds(8 * a, 8), :] = face[a]
    back = lax.broadcasted_iota(jnp.int32, (8, LANES), 0) * -1 + 7
    out = []
    for a in range(8):
        x = jnp.where(codes == 1, face[7 - a], face[a])
        x = jnp.where(codes == 2, jnp.take_along_axis(face[a], back, axis=0), x)
        x = jnp.where(codes == 3, buf[pl.ds(a, 8, stride=8), :], x)
        out.append(x)
    return out


def coupling_of(direction):
    lane, elem, var = lane_ids()
    vel = elem + 16 * (1 + direction)
    source = jnp.where((var == 0) | (var == 4), vel, lane)
    source = jnp.where(var == 1 + direction, elem + 64, source)
    has = (var == 0) | (var == 4) | (var == 1 + direction)
    return source, jnp.where(has, 1.0, 0.0).astype(jnp.float32)


def jump_with(gap, coupling, factor):
    source, has = coupling
    half = 0.5 * has
    return [factor * x + half * jnp.take_along_axis(x, source, axis=1) for x in gap]


def jump_factor(direction, sign):
    return 0.5 * (mean_flow[direction] + sign * (abs(mean_flow[direction]) + 1.0))


def jump_flux(gap, direction, sign):
    return jump_with(gap, coupling_of(direction), jump_factor(direction, sign))


def load_face(ref):
    return [ref[pl.ds(8 * a, 8), :] for a in range(8)]


def store_face(ref, face):
    for a in range(8):
        ref[pl.ds(8 * a, 8), :] = face[a]


def picked(tab, read):
    out = None
    for n in range(PMIN, NQ):
        w = row_of(tab, W_AT + n)
        layer = [w * x for x in read(n)]
        out = layer if out is None else [s + x for s, x in zip(out, layer)]
    return out


def node(i, j):
    return pl.ds((i * 8 + j) * 8, 8)


def x_faces(q, tab):
    low = [q[node(0, j), :] for j in range(8)]
    high = picked(tab, lambda n: [q[node(n, j), :] for j in range(8)])
    return low, high


def y_faces(q, tab):
    low = [q[node(i, 0), :] for i in range(8)]
    high = picked(tab, lambda n: [q[node(i, n), :] for i in range(8)])
    return low, high


def z_faces(q, tab):
    low = [q[pl.ds(i * 64, 8, stride=8), :] for i in range(8)]
    high = picked(tab, lambda n: [q[pl.ds(i * 64 + n, 8, stride=8), :] for i in range(8)])
    return low, high


def end_rows(q, tab, read):
    low = high = None
    for n in range(NQ):
        first, last = row_of(tab, D_AT + n), row_of(tab, DLAST_AT + n)
        layer = read(n)
        by_low, by_high = [first * x for x in layer], [last * x for x in layer]
        low = by_low if low is None else [a + b for a, b in zip(low, by_low)]
        high = by_high if high is None else [a + b for a, b in zip(high, by_high)]
    return low, high


def packed(kinds, where, shifts):
    out = []
    for a in range(8):
        x = rolled(kinds[3][a], shifts[3])
        for kind in range(3):
            x = jnp.where(where == kind, rolled(kinds[kind][a], shifts[kind]), x)
        out.append(x)
    return out


def make_messages(q, tab, order, metric, codes, first_core, outs, buf):
    tx_low, tx_high, ty_low, ty_high, chip_send, blk_send, up, down = outs
    _, elem, _ = lane_ids()
    x_ends, y_ends = x_faces(q, tab), y_faces(q, tab)
    tx = [turned(to_common(tab, x_ends[side]), codes[side], buf) for side in range(2)]
    ty = [to_common(tab, y_ends[side]) for side in range(2)]
    for ref, face in zip((tx_low, tx_high, ty_low, ty_high), tx + ty):
        store_face(ref, face)
    x_rows = end_rows(q, tab, lambda n: [q[node(n, j), :] for j in range(8)])
    y_rows = end_rows(q, tab, lambda n: [q[node(i, n), :] for i in range(8)])
    params = [order.astype(jnp.float32)] + metric
    zero = jnp.zeros((8, LANES), jnp.float32)

    def along_x(side, shifts):
        edge = 7 * side
        lines = [ty[0][edge], ty[1][edge]] + params + [codes[side].astype(jnp.float32), zero]
        return packed([tx[side], x_ends[side], x_rows[side], lines], elem >> 2, shifts)

    def along_y(side, shifts):
        edge = 7 * side
        lines = [tx[0][edge], tx[1][edge]] + params + [zero, zero]
        return packed([ty[side], y_ends[side], y_rows[side], lines], elem & 3, shifts)

    left = along_x(0, (0, 4, 8, 12))
    right = along_x(1, (-12, -8, -4, 0))
    store_face(chip_send, [jnp.where(first_core, r, l) for l, r in zip(left, right)])
    store_face(blk_send, [jnp.where(first_core, l, r) for l, r in zip(left, right)])
    store_face(down, along_y(0, (0, 1, 2, 3)))
    store_face(up, along_y(1, (-3, -2, -1, 0)))


def sides_of(paired_ref, other_ref, first):
    pair = load_face(paired_ref.at[jnp.where(first, 1, 0)])
    other = load_face(other_ref)
    before = [jnp.where(first, o, p) for o, p in zip(other, pair)]
    after = [jnp.where(first, p, o) for o, p in zip(other, pair)]
    return before, after


def places(core_ref, row_ref):
    return core_ref[0] == 0, lax.rem(row_ref[0], 2) == 0


def halo_step(messages, traces, wall, columns, tab, q_buf):
    left, right, below, above = messages
    lane, elem, var = lane_ids()
    group, pos = elem >> 2, elem & 3
    base = lane - elem
    across_rows = group >= 2
    is_high = (group & 1) == 0

    def collected(block, kind):
        at = base + jnp.where(across_rows, pos * 4 + kind, kind * 4 + pos)
        out = jnp.take_along_axis(left[block], at, axis=1)
        for g, message in ((1, right), (2, below), (3, above)):
            out = jnp.where(group == g, jnp.take_along_axis(message[block], at, axis=1), out)
        return out

    table_for(columns, collected(2, 3)[0:1, :], tab)
    lift = tab[pl.ds(LIFT_AT, 8), :]
    metric_x, metric_y, metric_z = [collected(3 + d, 3) for d in range(3)]
    metric_n = jnp.where(across_rows, metric_y, metric_x)
    metric_t = jnp.where(across_rows, metric_x, metric_y)
    codes = jnp.where(across_rows, 0.0, collected(6, 3)).astype(jnp.int32)
    by_x, by_y, by_z = [coupling_of(d) for d in range(3)]

    def mixed(a, b):
        return tuple(jnp.where(across_rows, y, x) for x, y in zip(a, b))

    couple_n, couple_t = mixed(by_x, by_y), mixed(by_y, by_x)

    def factor(d, sign):
        return jnp.float32(jump_factor(d, sign))

    factor_n = jnp.where(
        across_rows,
        jnp.where(is_high, factor(1, -1.0), factor(1, 1.0)),
        jnp.where(is_high, factor(0, -1.0), factor(0, 1.0)),
    )
    factor_t = [
        jnp.where(across_rows, factor(0, sign), factor(1, sign)) for sign in (1.0, -1.0)
    ]
    flow_n = jnp.where(across_rows, mean_flow[1], mean_flow[0])
    flow_t = jnp.where(across_rows, mean_flow[0], mean_flow[1])

    def flux(x, flow, coupling):
        source, has = coupling
        return flow * x + has * jnp.take_along_axis(x, source, axis=1)

    face = [collected(a, 1) for a in range(8)]
    slope = [collected(a, 2) for a in range(8)]
    tx_low, tx_high, ty_low, ty_high = traces
    at = jnp.where(group == 0, pos, jnp.where(group == 1, 12 + pos, 4 * pos))
    at = base + jnp.where(group == 3, 4 * pos + 3, at)
    near = []
    for a in range(8):
        out = jnp.take_along_axis(tx_low[a], at, axis=1)
        for g, trace in ((1, tx_high), (2, ty_low), (3, ty_high)):
            out = jnp.where(group == g, jnp.take_along_axis(trace[a], at, axis=1), out)
        near.append(out)
    gap = [n - f for n, f in zip(from_common(tab, near), face)]
    gap = jump_with(gap, couple_n, factor_n)
    scale = metric_n * lift * jnp.where(is_high, -1.0, 1.0)
    rate = [
        scale * g - metric_n * flux(d, flow_n, couple_n) for g, d in zip(gap, slope)
    ]
    by_t = along_first(tab, D_AT, face)
    by_k = along_second(tab, DK_AT, face)
    scale_z = metric_z * lift
    sub = lax.broadcasted_iota(jnp.int32, (8, LANES), 0)
    weights = tab[pl.ds(W_AT, 8), :]
    at_low = jnp.where(sub == 0, scale_z, 0.0)
    at_high = -scale_z * weights

    def at_k(x, k):
        return jnp.take_along_axis(x, jnp.full((8, LANES), k, jnp.int32), axis=0)

    for a in range(8):
        low = at_k(face[a], 0)
        high = row_of(tab, W_AT + PMIN) * at_k(face[a], PMIN)
        for n in range(PMIN + 1, NQ):
            high = high + row_of(tab, W_AT + n) * at_k(face[a], n)
        gap_low = jump_flux([high - low], 2, 1.0)[0]
        gap_high = jump_flux([low - high], 2, -1.0)[0]
        rate[a] = (
            rate[a]
            - metric_t * flux(by_t[a], flow_t, couple_t)
            - metric_z * flux(by_k[a], mean_flow[2], by_z)
            + at_low * gap_low
            + at_high * gap_high
        )
    line_low, line_high = collected(0, 3), collected(1, 3)
    flip = jnp.where(var == 2, -1.0, 1.0).astype(jnp.float32)

    def corners(side, block_below, block_above):
        at = base + jnp.where(elem == (4 if side == 0 else 7), 15, 3)
        if side == 1:
            at = base + jnp.where(elem == 3, 3, 15)
        return (
            jnp.take_along_axis(below[block_below], at, axis=1),
            jnp.take_along_axis(above[block_above], at, axis=1),
        )

    from_below, _ = corners(0, 7, 7)
    at_wall = jnp.where(wall, flip * line_low, from_below)
    from_below, from_above = corners(0, 6, 6)
    corner = jnp.where(
        across_rows, jnp.where(group == 2, from_below, from_above), at_wall
    )
    near_low = jnp.where(pos == 0, corner, rolled(line_high, 1))
    _, beyond = corners(1, 7, 7)
    from_below, from_above = corners(1, 6, 6)
    corner = jnp.where(across_rows, jnp.where(group == 2, from_below, from_above), beyond)
    near_high = jnp.where(pos == 3, corner, rolled(line_low, -1))
    near_low, near_high = along_second(tab, BK_AT, [near_low, near_high])
    own_high = row_of(tab, W_AT + PMIN) * face[PMIN]
    for n in range(PMIN + 1, NQ):
        own_high = own_high + row_of(tab, W_AT + n) * face[n]
    scale = metric_t * lift
    gap_low = scale * jump_with([near_low - face[0]], couple_t, factor_t[0])[0]
    gap_high = scale * jump_with([near_high - own_high], couple_t, factor_t[1])[0]
    rate[0] = rate[0] + gap_low
    for n in range(PMIN, NQ):
        rate[n] = rate[n] - row_of(tab, W_AT + n) * gap_high
    middle = [f + time_step * r for f, r in zip(face, rate)]
    return turned(to_common(tab, middle), codes, q_buf)


def from_halo(face):
    lane, elem, _ = lane_ids()
    base = lane - elem
    at_below = base + 8 + (elem >> 2)
    at_above = base + 12 + (elem >> 2)
    return (
        face,
        [rolled(x, 8) for x in face],
        [jnp.take_along_axis(x, at_below, axis=1) for x in face],
        [jnp.take_along_axis(x, at_above, axis=1) for x in face],
    )


def gaps_to(q, tab, lift, traces, arrived, wall, metric, out):
    tx_low, tx_high, ty_low, ty_high = traces
    from_left, from_right, from_below, from_above = arrived
    _, elem, var = lane_ids()
    scale = lift * metric[0]
    low, high = x_faces(q, tab)
    near = [
        jnp.where(elem < 4, r, rolled(t, 4))
        for r, t in zip(from_left, tx_high)
    ]
    gap = jump_flux([n - o for n, o in zip(from_common(tab, near), low)], 0, 1.0)
    for j in range(8):
        out[node(0, j), :] = out[node(0, j), :] + scale * gap[j]
    near = [
        jnp.where(elem >= 12, r, rolled(t, -4))
        for r, t in zip(from_right, tx_low)
    ]
    gap = jump_flux([n - o for n, o in zip(from_common(tab, near), high)], 0, -1.0)
    gap = [scale * x for x in gap]
    for n in range(PMIN, NQ):
        w = row_of(tab, W_AT + n)
        for j in range(8):
            out[node(n, j), :] = out[node(n, j), :] - w * gap[j]
    scale = lift * metric[1]
    low, high = y_faces(q, tab)
    own_low = ty_low
    flip = jnp.where(var == 2, -1.0, 1.0).astype(jnp.float32)
    first = (elem & 3) == 0
    near = [
        jnp.where(first, jnp.where(wall, flip * o, r), rolled(t, 1))
        for r, t, o in zip(from_below, ty_high, own_low)
    ]
    gap = jump_flux([n - o for n, o in zip(from_common(tab, near), low)], 1, 1.0)
    for i in range(8):
        out[node(i, 0), :] = out[node(i, 0), :] + scale * gap[i]
    near = [
        jnp.where((elem & 3) == 3, r, rolled(t, -1))
        for r, t in zip(from_above, own_low)
    ]
    gap = jump_flux([n - o for n, o in zip(from_common(tab, near), high)], 1, -1.0)
    gap = [scale * x for x in gap]
    for n in range(PMIN, NQ):
        w = row_of(tab, W_AT + n)
        for i in range(8):
            out[node(i, n), :] = out[node(i, n), :] - w * gap[i]


def span_terms(q, tab, lift, metric, out):
    scale = lift * metric[2]
    low, high = z_faces(q, tab)
    gap_low = jump_flux([h - o for h, o in zip(high, low)], 2, 1.0)
    gap_high = jump_flux([o - h for h, o in zip(high, low)], 2, -1.0)
    sub = lax.broadcasted_iota(jnp.int32, (8, LANES), 0)
    at_low = jnp.where(sub == 0, scale, 0.0)
    at_high = -scale * tab[pl.ds(W_AT, 8), :]
    for i in range(8):
        for j in range(8):
            pick = jnp.full((8, LANES), j, jnp.int32)
            lo = jnp.take_along_axis(gap_low[i], pick, axis=0)
            hi = jnp.take_along_axis(gap_high[i], pick, axis=0)
            out[node(i, j), :] = out[node(i, j), :] + at_low * lo + at_high * hi


def volume_terms(q, tab, metric, out):
    couplings = [coupling_of(d) for d in range(3)]

    def flux(x, d):
        source, has = couplings[d]
        y = metric[d] * x
        mixed = has * jnp.take_along_axis(y, source, axis=1)
        return mixed if mean_flow[d] == 0.0 else mean_flow[d] * y + mixed

    for j in range(8):
        face = [q[node(i, j), :] for i in range(8)]
        for i, x in enumerate(along_first(tab, D_AT, face)):
            out[node(i, j), :] = -flux(x, 0)
    for i in range(8):
        face = [q[node(i, j), :] for j in range(8)]
        by_y = along_first(tab, D_AT, face)
        by_z = along_second(tab, DK_AT, face)
        for j in range(8):
            out[node(i, j), :] = out[node(i, j), :] - (flux(by_y[j], 1) + flux(by_z[j], 2))


def all_metrics(metric_ref):
    return [spread(lambda x, y, d=d: metric_ref[d, x, y], jnp.float32) for d in range(3)]


def all_codes(turn_ref):
    return [spread(lambda x, y, s=s: turn_ref[s, x, y], jnp.int32) for s in range(2)]


def kept_metrics(params):
    return [params[pl.ds(8 * d, 8), :] for d in range(3)]


def kept_codes(params):
    return [params[pl.ds(24 + 8 * s, 8), :].astype(jnp.int32) for s in range(2)]


def table_for(columns, level_row, tab):
    level = (lax.broadcasted_iota(jnp.int32, (LANES, LANES), 0) & 7) + PMIN
    one_hot = jnp.where(
        level.astype(jnp.float32) == jnp.broadcast_to(level_row, (LANES, LANES)), 1.0, 0.0
    ).astype(jnp.bfloat16)
    pad = jnp.zeros((LANES - 24, LANES), jnp.float32)
    for part in range(4):
        at = part * LANES
        size = min(LANES, TAB_ROWS - at)
        left = jnp.concatenate([columns[:, pl.ds(at, LANES)], pad[:8]], axis=0)
        cut = []
        for _ in range(3):
            cut.append(left.astype(jnp.bfloat16).astype(jnp.float32))
            left = left - cut[-1]
        block = jnp.concatenate([x[:8] for x in cut] + [pad], axis=0).T
        tab[pl.ds(at, size), :] = jnp.dot(
            block.astype(jnp.bfloat16), one_hot, preferred_element_type=jnp.float32
        )[:size]


def fetched(pairs, sems):
    copies = [pltpu.make_async_copy(a, b, sems.at[n]) for n, (a, b) in enumerate(pairs)]
    for copy in copies:
        copy.start()
    return copies


def first_kernel(
    fields, columns, orders_hbm, turn_hbm, metric_hbm, _, core_ref, row_ref, q, tab, params, *rest
):
    outs = rest[:8]
    flat, buf, orders, turn, metric_ref, sems = rest[8:]
    copies = fetched(
        [(orders_hbm, orders), (turn_hbm, turn), (metric_hbm, metric_ref)], sems
    )
    flat[pl.ds(80, 48), :] = jnp.zeros((48, 512), jnp.float32)
    for v in range(VARS):
        for x in range(4):
            flat[pl.ds(v * 16 + x * 4, 4), :] = fields[x, v]
    for copy in copies:
        copy.wait()
    order = spread(lambda x, y: orders[x, y].astype(jnp.float32), jnp.float32)
    metric, codes = all_metrics(metric_ref), all_codes(turn)
    for n, x in enumerate(metric + codes):
        params[pl.ds(8 * n, 8), :] = x.astype(jnp.float32)
    table_for(columns, order[0:1, :], tab)
    in_k = tab[pl.ds(A_AT, 8), :]
    for part in range(4):
        block = flat[:, pl.ds(part * LANES, LANES)].T
        for half in range(2):
            in_ik = in_k * row_of(tab, A_AT + part * 2 + half)
            for j in range(8):
                at = (half * 8 + j) * 8
                q[node(part * 2 + half, j), :] = (
                    block[at : at + 8] * in_ik * row_of(tab, A_AT + j)
                )
    first_core, _ = places(core_ref, row_ref)
    make_messages(q, tab, order, metric, codes, first_core, outs, buf)


def inner_kernel(q, tab, params, rate):
    metric = kept_metrics(params)
    volume_terms(q, tab, metric, rate)
    span_terms(q, tab, tab[pl.ds(LIFT_AT, 8), :], metric, rate)


def second_kernel(up, down, chip, blk, inner, core_ref, row_ref, pair_send, row_send):
    first_core, even_row = places(core_ref, row_ref)
    left, right = sides_of(chip, blk, first_core)
    _, elem, _ = lane_ids()
    up, down = load_face(up), load_face(down)

    def with_corners(message, edge, y, line):
        at_left, at_right = elem == 3, elem == 15
        out = message[:6]
        out.append(
            jnp.where(
                at_left,
                rolled(left[edge], 3 - y),
                jnp.where(at_right, rolled(right[edge], 15 - y), message[6]),
            )
        )
        out.append(
            jnp.where(
                at_left,
                rolled(left[line], -9 - y),
                jnp.where(at_right, rolled(right[line], 3 - y), message[7]),
            )
        )
        return out

    up = with_corners(up, 7, 3, 1)
    down = with_corners(down, 0, 0, 0)
    store_face(pair_send, [jnp.where(even_row, u, d) for u, d in zip(up, down)])
    store_face(row_send, [jnp.where(even_row, d, u) for u, d in zip(up, down)])


def third_kernel(q, tab, params, inner, columns, migration_hbm, core_ref, row_ref, *rest):
    traces, arrived = rest[:4], rest[4:8]
    outs = rest[8:12]
    rate, middle, second, flat, slots, count, migration, halo_tab, buf, sems = rest[12:]
    copies = fetched([(migration_hbm, migration)], sems)
    first_core, even_row = places(core_ref, row_ref)
    wall = row_ref[0] == 0
    metric, codes = kept_metrics(params), kept_codes(params)
    lift = tab[pl.ds(LIFT_AT, 8), :]
    chip, blk, pair, row = arrived
    left, right = sides_of(chip, blk, first_core)
    below, above = sides_of(pair, row, even_row)
    own = [load_face(ref) for ref in traces]
    beside = halo_step((left, right, below, above), own, wall, columns, halo_tab, buf)
    near = (left, [rolled(x, 12) for x in right], below, [rolled(x, 3) for x in above])
    rate[...] = inner[...]
    gaps_to(q, tab, lift, own, near, wall, metric, rate)
    for n in range(64):
        at = pl.ds(8 * n, 8)
        middle[at, :] = q[at, :] + time_step * rate[at, :]
    x_ends, y_ends = x_faces(middle, tab), y_faces(middle, tab)
    own = [turned(to_common(tab, x_ends[side]), codes[side], buf) for side in range(2)]
    own = own + [to_common(tab, y_ends[side]) for side in range(2)]
    volume_terms(middle, tab, metric, second)
    span_terms(middle, tab, lift, metric, second)
    gaps_to(middle, tab, lift, own, from_halo(beside), wall, metric, second)
    copies[0].wait()
    for part in range(4):
        at = pl.ds(part * LANES, LANES)
        flat[:, 0, at] = ((0.5 * time_step) * (rate[at, :] + second[at, :])).T
    slots[...] = jnp.zeros_like(slots)
    for m in range(SPREAD):
        count[m] = 0
    for e in range(NB):
        m = migration[0, 0, 0, e]
        c = count[m]
        count[m] = c + 1
        slot = jnp.where(core_ref[0] == 0, m, SPREAD - 1 - m) * CAP + c
        for v in range(VARS):
            slots[slot, v] = flat[v * 16 + e]
    at = 0
    for out in outs:
        size = out.shape[0]
        out[...] = slots[pl.ds(at, size)]
        at += size


def last_kernel(far, own, near, core_ref, chip, relayed, out, sems):
    def put(groups):
        copies = [
            pltpu.make_async_copy(piece, out.at[pl.ds(m * CAP, CAP)], sems.at[m])
            for m, piece in enumerate(groups)
        ]
        for copy in copies:
            copy.start()
        for copy in copies:
            copy.wait()

    first = far.at[pl.ds(0, CAP)]

    @pl.when(core_ref[0] == 0)
    def _():
        put([first, chip.at[1], own, relayed.at[1, pl.ds(CAP, CAP)], near])

    @pl.when(core_ref[0] != 0)
    def _():
        put([near, relayed.at[0, pl.ds(CAP, CAP)], own, chip.at[0], first])


def f32(*shape):
    return jax.ShapeDtypeStruct(shape, jnp.float32)


VMEM = pl.BlockSpec(memory_space=pltpu.VMEM)
SMEM = pl.BlockSpec(memory_space=pltpu.SMEM)
HBM = pl.BlockSpec(memory_space=pltpu.HBM)
ANY = pl.BlockSpec(memory_space=pl.ANY)
PARAMS = pltpu.CompilerParams(vmem_limit_bytes=32 * 1024 * 1024)
FACE = f32(64, LANES)
VOLUME = f32(512, LANES)


def pairs_of(count, first):
    return [[n, n + 1] for n in range(first, count - 1, 2)]


def swapped(array, axis, wraps):
    count = lax.axis_size(axis)
    pairs = [(a, b) for a, b in pairs_of(count, 1)]
    if wraps:
        pairs.append((count - 1, 0))
    return lax.ppermute(array, axis, pairs + [(b, a) for a, b in pairs])


def paired(array, axis):
    return lax.all_gather(array, axis, axis_index_groups=pairs_of(lax.axis_size(axis), 0))


def hopped(array, outward):
    count = lax.axis_size("blk")
    step = [-2, 2] if outward else [2, -2]
    return lax.ppermute(array, "blk", [(n, (n + step[n % 2]) % count) for n in range(count)])


def vmem(*shape):
    return pltpu.VMEM(shape, jnp.float32)


def sems(count):
    return pltpu.SemaphoreType.DMA((count,))


def local(fields, orders, metric, face_turn, migration):
    by_var = jnp.transpose(fields, (0, 2, 1, 3))
    core = lax.rem(lax.axis_index("blk").astype(jnp.int32), 2).reshape(1)
    row = lax.axis_index("row").astype(jnp.int32).reshape(1)
    columns = jnp.asarray(table_columns())
    targets = jnp.transpose(migration, (0, 1, 3, 2))
    q, tab, params, *faces = pl.pallas_call(
        first_kernel,
        out_shape=[VOLUME, f32(TAB_ROWS, LANES), f32(40, LANES)] + [FACE] * 8,
        in_specs=[VMEM] * 2 + [HBM] * 3 + [ANY] + [SMEM] * 2,
        out_specs=[VMEM] * 11,
        scratch_shapes=[
            vmem(LANES, 512),
            vmem(64, LANES),
            pltpu.SMEM((4, 4), jnp.int32),
            pltpu.SMEM((2, 4, 4), jnp.int32),
            pltpu.SMEM((3, 4, 4), jnp.float32),
            sems(3),
        ],
        compiler_params=PARAMS,
    )(by_var, columns, orders, face_turn, metric, targets, core, row)
    chip_send, blk_send, up, down = faces[4:]
    blk = swapped(blk_send, "blk", True)
    chip = paired(chip_send, "blk")
    inner = pl.pallas_call(
        inner_kernel,
        out_shape=VOLUME,
        in_specs=[VMEM] * 3,
        out_specs=VMEM,
        compiler_params=PARAMS,
        cost_estimate=pl.CostEstimate(
            flops=40_000_000, bytes_accessed=6_000_000, transcendentals=0
        ),
    )(q, tab, params)
    pair_send, row_send = pl.pallas_call(
        second_kernel,
        out_shape=[FACE] * 2,
        in_specs=[VMEM] * 4 + [ANY] + [SMEM] * 2,
        out_specs=[VMEM] * 2,
        compiler_params=PARAMS,
    )(up, down, chip, blk, inner, core, row)
    beyond = swapped(row_send, "row", False)
    pair = paired(pair_send, "row")
    outward, own, same_chip, inward = pl.pallas_call(
        third_kernel,
        out_shape=[f32(n, VARS, 1, 512) for n in (2 * CAP, CAP, CAP, CAP)],
        in_specs=[VMEM] * 5 + [HBM] + [SMEM] * 2 + [VMEM] * 8,
        out_specs=[VMEM] * 4,
        scratch_shapes=[
            vmem(512, LANES),
            vmem(512, LANES),
            vmem(512, LANES),
            vmem(LANES, 1, 512),
            vmem(SPREAD * CAP, VARS, 1, 512),
            pltpu.SMEM((8,), jnp.int32),
            pltpu.SMEM((1, 1, 1, NB), jnp.int32),
            vmem(TAB_ROWS, LANES),
            vmem(64, LANES),
            sems(1),
        ],
        compiler_params=PARAMS,
    )(
        q, tab, params, inner, columns, targets, core, row,
        *faces[:4], chip, blk, pair, beyond,
    )
    far = hopped(outward, True)
    near = hopped(inward, False)
    chip = paired(same_chip, "blk")
    relayed = paired(far, "blk")
    moved = pl.pallas_call(
        last_kernel,
        out_shape=f32(SPREAD * CAP, VARS, 1, 512),
        in_specs=[ANY] * 3 + [SMEM] + [ANY] * 2,
        out_specs=HBM,
        scratch_shapes=[sems(SPREAD)],
        compiler_params=PARAMS,
    )(far, own, near, core, chip, relayed)
    return jnp.transpose(moved, (2, 0, 1, 3)).reshape(1, 1, SPREAD * CAP, VARS, 512)


def solution(mesh):
    placed = (
        P("blk", "row", None, None),
        P("blk", "row"),
        P(None, "blk", "row"),
        P(None, "blk", "row"),
        P("blk", "row", None, None),
    )
    return jax.shard_map(
        local,
        mesh=mesh,
        in_specs=placed,
        out_specs=P("blk", "row", None, None, None),
        check_vma=False,
    )
```

```python
import jax
import jax.numpy as jnp
import numpy as np
from jax import lax
from jax.experimental import pallas as pl
from jax.experimental.pallas import tpu as pltpu
from jax.sharding import PartitionSpec as P

PMAX = 7
PMIN = 3
VARS = 5
NQ = 8
NB = 16
SPREAD = 5
CAP = 5
LANES = 128

mean_flow = (0.4, 0.0, 0.2)
time_step = 0.008


def legendre_points(degree):
    point_count = degree + 1
    estimate = np.cos(np.pi * np.arange(point_count) / degree)
    for sweep_idx in range(40):
        values = np.zeros((point_count, point_count))
        values[:, 0] = 1.0
        values[:, 1] = estimate
        for order_idx in range(2, point_count):
            values[:, order_idx] = (
                (2 * order_idx - 1) * estimate * values[:, order_idx - 1]
                - (order_idx - 1) * values[:, order_idx - 2]
            ) / order_idx
        estimate = estimate - (estimate * values[:, degree] - values[:, degree - 1]) / (
            point_count * values[:, degree]
        )
    return np.sort(estimate)


def lagrange_matrix(points, targets):
    result = np.ones((len(targets), len(points)))
    for column in range(len(points)):
        for other_idx in range(len(points)):
            if other_idx != column:
                result[:, column] *= (targets - points[other_idx]) / (
                    points[column] - points[other_idx]
                )
    return result


def build_tables(lowest, highest):
    node_count = highest + 1
    level_count = highest - lowest + 1
    common = legendre_points(highest)
    derive = np.zeros((level_count, node_count, node_count))
    to_grid = np.zeros((level_count, node_count, node_count))
    from_grid = np.zeros((level_count, node_count, node_count))
    lifting = np.zeros((level_count,))
    last_node = np.zeros((level_count, node_count))
    active = np.zeros((level_count, node_count))
    for level_idx in range(level_count):
        degree = lowest + level_idx
        points = legendre_points(degree)
        filled = degree + 1
        weights = np.array(
            [
                1.0
                / np.prod(
                    [
                        points[column] - points[other_idx]
                        for other_idx in range(filled)
                        if other_idx != column
                    ]
                )
                for column in range(filled)
            ]
        )
        local_diff = np.zeros((filled, filled))
        for row_idx in range(filled):
            for column in range(filled):
                if column != row_idx:
                    local_diff[row_idx, column] = (
                        weights[column] / weights[row_idx] / (points[row_idx] - points[column])
                    )
            local_diff[row_idx, row_idx] = -np.sum(local_diff[row_idx])
        derive[level_idx, :filled, :filled] = local_diff
        to_grid[level_idx, :, :filled] = lagrange_matrix(points, common)
        from_grid[level_idx, :filled, :] = lagrange_matrix(common, points)
        lifting[level_idx] = degree * (degree + 1) / 2.0
        last_node[level_idx, degree] = 1.0
        active[level_idx, :filled] = 1.0
    return derive, to_grid, from_grid, lifting, last_node, active


D_AT, DK_AT, I_AT, IK_AT, B_AT, BK_AT, W_AT, A_AT, LIFT_AT, DLAST_AT = (
    0, 64, 128, 192, 256, 320, 384, 392, 400, 408)
TAB_ROWS = 416


def table_columns():
    derive, to_grid, from_grid, lifting, last_node, active = build_tables(PMIN, PMAX)
    rows = np.zeros((4 * LANES, 8))
    for level in range(PMAX - PMIN + 1):
        for at, turned_at, mat in (
            (D_AT, DK_AT, derive[level]),
            (I_AT, IK_AT, to_grid[level]),
            (B_AT, BK_AT, from_grid[level]),
        ):
            rows[at : at + 64, level] = mat.reshape(-1)
            for turn in range(8):
                for a in range(8):
                    rows[turned_at + turn * 8 + a, level] = mat[a, (a + turn) % 8]
        rows[W_AT : W_AT + 8, level] = last_node[level]
        rows[A_AT : A_AT + 8, level] = active[level]
        rows[LIFT_AT : LIFT_AT + 8, level] = lifting[level]
        rows[DLAST_AT : DLAST_AT + 8, level] = derive[level][PMIN + level]
    return np.ascontiguousarray(rows.T).astype(np.float32)


def lane_ids():
    lane = lax.broadcasted_iota(jnp.int32, (8, LANES), 1)
    return lane, lane & 15, lane >> 4


def spread(read, dtype):
    _, elem, _ = lane_ids()
    out = jnp.zeros((8, LANES), dtype)
    for e in range(NB):
        out = jnp.where(elem == e, read(e // 4, e % 4), out)
    return out


def rolled(x, by):
    return pltpu.roll(x, by % LANES, 1)


def subrolled(x, by):
    return x if by % 8 == 0 else pltpu.roll(x, by % 8, 0)


def row_of(ref, at):
    return jnp.broadcast_to(ref[pl.ds(at, 1), :], (8, LANES))


def along_first(tab, at, face):
    out = []
    for a in range(8):
        total = row_of(tab, at + a * 8) * face[0]
        for j in range(1, 8):
            total = total + row_of(tab, at + a * 8 + j) * face[j]
        out.append(total)
    return out


def along_second(tab, at, face):
    coefs = [tab[pl.ds(at + 8 * turn, 8), :] for turn in range(8)]
    out = []
    for x in face:
        total = coefs[0] * x
        for turn in range(1, 8):
            total = total + coefs[turn] * subrolled(x, -turn)
        out.append(total)
    return out


def to_common(tab, face):
    return along_second(tab, IK_AT, along_first(tab, I_AT, face))


def from_common(tab, face):
    return along_second(tab, BK_AT, along_first(tab, B_AT, face))


def turned(face, codes, buf):
    for a in range(8):
        buf[pl.ds(8 * a, 8), :] = face[a]
    back = lax.broadcasted_iota(jnp.int32, (8, LANES), 0) * -1 + 7
    out = []
    for a in range(8):
        x = jnp.where(codes == 1, face[7 - a], face[a])
        x = jnp.where(codes == 2, jnp.take_along_axis(face[a], back, axis=0), x)
        x = jnp.where(codes == 3, buf[pl.ds(a, 8, stride=8), :], x)
        out.append(x)
    return out


def coupling_of(direction):
    lane, elem, var = lane_ids()
    vel = elem + 16 * (1 + direction)
    source = jnp.where((var == 0) | (var == 4), vel, lane)
    source = jnp.where(var == 1 + direction, elem + 64, source)
    has = (var == 0) | (var == 4) | (var == 1 + direction)
    return source, jnp.where(has, 1.0, 0.0).astype(jnp.float32)


def jump_with(gap, coupling, factor):
    source, has = coupling
    half = 0.5 * has
    return [factor * x + half * jnp.take_along_axis(x, source, axis=1) for x in gap]


def jump_factor(direction, sign):
    return 0.5 * (mean_flow[direction] + sign * (abs(mean_flow[direction]) + 1.0))


def jump_flux(gap, direction, sign):
    return jump_with(gap, coupling_of(direction), jump_factor(direction, sign))


def load_face(ref):
    return [ref[pl.ds(8 * a, 8), :] for a in range(8)]


def store_face(ref, face):
    for a in range(8):
        ref[pl.ds(8 * a, 8), :] = face[a]


def picked(tab, read):
    out = None
    for n in range(PMIN, NQ):
        w = row_of(tab, W_AT + n)
        layer = [w * x for x in read(n)]
        out = layer if out is None else [s + x for s, x in zip(out, layer)]
    return out


def node(i, j):
    return pl.ds((i * 8 + j) * 8, 8)


def x_faces(q, tab):
    low = [q[node(0, j), :] for j in range(8)]
    high = picked(tab, lambda n: [q[node(n, j), :] for j in range(8)])
    return low, high


def y_faces(q, tab):
    low = [q[node(i, 0), :] for i in range(8)]
    high = picked(tab, lambda n: [q[node(i, n), :] for i in range(8)])
    return low, high


def z_faces(q, tab):
    low = [q[pl.ds(i * 64, 8, stride=8), :] for i in range(8)]
    high = picked(tab, lambda n: [q[pl.ds(i * 64 + n, 8, stride=8), :] for i in range(8)])
    return low, high


def end_rows(q, tab, read):
    low = high = None
    for n in range(NQ):
        first, last = row_of(tab, D_AT + n), row_of(tab, DLAST_AT + n)
        layer = read(n)
        by_low, by_high = [first * x for x in layer], [last * x for x in layer]
        low = by_low if low is None else [a + b for a, b in zip(low, by_low)]
        high = by_high if high is None else [a + b for a, b in zip(high, by_high)]
    return low, high


def packed(kinds, where, shifts):
    out = []
    for a in range(8):
        x = rolled(kinds[3][a], shifts[3])
        for kind in range(3):
            x = jnp.where(where == kind, rolled(kinds[kind][a], shifts[kind]), x)
        out.append(x)
    return out


def make_messages(q, tab, order, metric, codes, first_core, outs, buf):
    tx_low, tx_high, ty_low, ty_high, chip_send, blk_send = outs
    _, elem, _ = lane_ids()
    x_ends, y_ends = x_faces(q, tab), y_faces(q, tab)
    tx = [turned(to_common(tab, x_ends[side]), codes[side], buf) for side in range(2)]
    ty = [to_common(tab, y_ends[side]) for side in range(2)]
    for ref, face in zip((tx_low, tx_high, ty_low, ty_high), tx + ty):
        store_face(ref, face)
    x_rows = end_rows(q, tab, lambda n: [q[node(n, j), :] for j in range(8)])
    params = [order.astype(jnp.float32)] + metric
    zero = jnp.zeros((8, LANES), jnp.float32)

    def along_x(side, shifts):
        edge = 7 * side
        lines = [ty[0][edge], ty[1][edge]] + params + [codes[side].astype(jnp.float32), zero]
        return packed([tx[side], x_ends[side], x_rows[side], lines], elem >> 2, shifts)

    left = along_x(0, (0, 4, 8, 12))
    right = along_x(1, (-12, -8, -4, 0))
    store_face(chip_send, [jnp.where(first_core, r, l) for l, r in zip(left, right)])
    store_face(blk_send, [jnp.where(first_core, l, r) for l, r in zip(left, right)])


def make_row_messages(q, tab, order, metric, traces, up, down):
    tx, ty = traces[:2], traces[2:]
    _, elem, _ = lane_ids()
    y_ends = y_faces(q, tab)
    y_rows = end_rows(q, tab, lambda n: [q[node(i, n), :] for i in range(8)])
    zero = jnp.zeros((8, LANES), jnp.float32)
    for side, ref, shifts in ((0, down, (0, 1, 2, 3)), (1, up, (-3, -2, -1, 0))):
        edge = 7 * side
        lines = [tx[0][edge], tx[1][edge], order] + metric + [zero, zero]
        store_face(
            ref, packed([ty[side], y_ends[side], y_rows[side], lines], elem & 3, shifts)
        )


def sides_of(paired_ref, other_ref, first):
    pair = load_face(paired_ref.at[jnp.where(first, 1, 0)])
    other = load_face(other_ref)
    before = [jnp.where(first, o, p) for o, p in zip(other, pair)]
    after = [jnp.where(first, p, o) for o, p in zip(other, pair)]
    return before, after


def places(core_ref, row_ref):
    return core_ref[0] == 0, lax.rem(row_ref[0], 2) == 0


def halo_step(messages, traces, wall, columns, tab, q_buf):
    left, right, below, above = messages
    lane, elem, var = lane_ids()
    group, pos = elem >> 2, elem & 3
    base = lane - elem
    across_rows = group >= 2
    is_high = (group & 1) == 0

    def collected(block, kind):
        at = base + jnp.where(across_rows, pos * 4 + kind, kind * 4 + pos)
        out = jnp.take_along_axis(left[block], at, axis=1)
        for g, message in ((1, right), (2, below), (3, above)):
            out = jnp.where(group == g, jnp.take_along_axis(message[block], at, axis=1), out)
        return out

    table_for(columns, collected(2, 3)[0:1, :], tab)
    lift = tab[pl.ds(LIFT_AT, 8), :]
    metric_x, metric_y, metric_z = [collected(3 + d, 3) for d in range(3)]
    metric_n = jnp.where(across_rows, metric_y, metric_x)
    metric_t = jnp.where(across_rows, metric_x, metric_y)
    codes = jnp.where(across_rows, 0.0, collected(6, 3)).astype(jnp.int32)
    by_x, by_y, by_z = [coupling_of(d) for d in range(3)]

    def mixed(a, b):
        return tuple(jnp.where(across_rows, y, x) for x, y in zip(a, b))

    couple_n, couple_t = mixed(by_x, by_y), mixed(by_y, by_x)

    def factor(d, sign):
        return jnp.float32(jump_factor(d, sign))

    factor_n = jnp.where(
        across_rows,
        jnp.where(is_high, factor(1, -1.0), factor(1, 1.0)),
        jnp.where(is_high, factor(0, -1.0), factor(0, 1.0)),
    )
    factor_t = [
        jnp.where(across_rows, factor(0, sign), factor(1, sign)) for sign in (1.0, -1.0)
    ]
    flow_n = jnp.where(across_rows, mean_flow[1], mean_flow[0])
    flow_t = jnp.where(across_rows, mean_flow[0], mean_flow[1])

    def flux(x, flow, coupling):
        source, has = coupling
        return flow * x + has * jnp.take_along_axis(x, source, axis=1)

    face = [collected(a, 1) for a in range(8)]
    slope = [collected(a, 2) for a in range(8)]
    tx_low, tx_high, ty_low, ty_high = traces
    at = jnp.where(group == 0, pos, jnp.where(group == 1, 12 + pos, 4 * pos))
    at = base + jnp.where(group == 3, 4 * pos + 3, at)
    near = []
    for a in range(8):
        out = jnp.take_along_axis(tx_low[a], at, axis=1)
        for g, trace in ((1, tx_high), (2, ty_low), (3, ty_high)):
            out = jnp.where(group == g, jnp.take_along_axis(trace[a], at, axis=1), out)
        near.append(out)
    gap = [n - f for n, f in zip(from_common(tab, near), face)]
    gap = jump_with(gap, couple_n, factor_n)
    scale = metric_n * lift * jnp.where(is_high, -1.0, 1.0)
    rate = [
        scale * g - metric_n * flux(d, flow_n, couple_n) for g, d in zip(gap, slope)
    ]
    by_t = along_first(tab, D_AT, face)
    by_k = along_second(tab, DK_AT, face)
    scale_z = metric_z * lift
    sub = lax.broadcasted_iota(jnp.int32, (8, LANES), 0)
    weights = tab[pl.ds(W_AT, 8), :]
    at_low = jnp.where(sub == 0, scale_z, 0.0)
    at_high = -scale_z * weights

    def at_k(x, k):
        return jnp.take_along_axis(x, jnp.full((8, LANES), k, jnp.int32), axis=0)

    for a in range(8):
        low = at_k(face[a], 0)
        high = row_of(tab, W_AT + PMIN) * at_k(face[a], PMIN)
        for n in range(PMIN + 1, NQ):
            high = high + row_of(tab, W_AT + n) * at_k(face[a], n)
        gap_low = jump_flux([high - low], 2, 1.0)[0]
        gap_high = jump_flux([low - high], 2, -1.0)[0]
        rate[a] = (
            rate[a]
            - metric_t * flux(by_t[a], flow_t, couple_t)
            - metric_z * flux(by_k[a], mean_flow[2], by_z)
            + at_low * gap_low
            + at_high * gap_high
        )
    line_low, line_high = collected(0, 3), collected(1, 3)
    flip = jnp.where(var == 2, -1.0, 1.0).astype(jnp.float32)

    def corners(side, block_below, block_above):
        at = base + jnp.where(elem == (4 if side == 0 else 7), 15, 3)
        if side == 1:
            at = base + jnp.where(elem == 3, 3, 15)
        return (
            jnp.take_along_axis(below[block_below], at, axis=1),
            jnp.take_along_axis(above[block_above], at, axis=1),
        )

    from_below, _ = corners(0, 7, 7)
    at_wall = jnp.where(wall, flip * line_low, from_below)
    from_below, from_above = corners(0, 6, 6)
    corner = jnp.where(
        across_rows, jnp.where(group == 2, from_below, from_above), at_wall
    )
    near_low = jnp.where(pos == 0, corner, rolled(line_high, 1))
    _, beyond = corners(1, 7, 7)
    from_below, from_above = corners(1, 6, 6)
    corner = jnp.where(across_rows, jnp.where(group == 2, from_below, from_above), beyond)
    near_high = jnp.where(pos == 3, corner, rolled(line_low, -1))
    near_low, near_high = along_second(tab, BK_AT, [near_low, near_high])
    own_high = row_of(tab, W_AT + PMIN) * face[PMIN]
    for n in range(PMIN + 1, NQ):
        own_high = own_high + row_of(tab, W_AT + n) * face[n]
    scale = metric_t * lift
    gap_low = scale * jump_with([near_low - face[0]], couple_t, factor_t[0])[0]
    gap_high = scale * jump_with([near_high - own_high], couple_t, factor_t[1])[0]
    rate[0] = rate[0] + gap_low
    for n in range(PMIN, NQ):
        rate[n] = rate[n] - row_of(tab, W_AT + n) * gap_high
    middle = [f + time_step * r for f, r in zip(face, rate)]
    return turned(to_common(tab, middle), codes, q_buf)


def from_halo(face):
    lane, elem, _ = lane_ids()
    base = lane - elem
    at_below = base + 8 + (elem >> 2)
    at_above = base + 12 + (elem >> 2)
    return (
        face,
        [rolled(x, 8) for x in face],
        [jnp.take_along_axis(x, at_below, axis=1) for x in face],
        [jnp.take_along_axis(x, at_above, axis=1) for x in face],
    )


def gaps_to(q, tab, lift, traces, arrived, wall, metric, out):
    tx_low, tx_high, ty_low, ty_high = traces
    from_left, from_right, from_below, from_above = arrived
    _, elem, var = lane_ids()
    scale = lift * metric[0]
    low, high = x_faces(q, tab)
    near = [
        jnp.where(elem < 4, r, rolled(t, 4))
        for r, t in zip(from_left, tx_high)
    ]
    gap = jump_flux([n - o for n, o in zip(from_common(tab, near), low)], 0, 1.0)
    for j in range(8):
        out[node(0, j), :] = out[node(0, j), :] + scale * gap[j]
    near = [
        jnp.where(elem >= 12, r, rolled(t, -4))
        for r, t in zip(from_right, tx_low)
    ]
    gap = jump_flux([n - o for n, o in zip(from_common(tab, near), high)], 0, -1.0)
    gap = [scale * x for x in gap]
    for n in range(PMIN, NQ):
        w = row_of(tab, W_AT + n)
        for j in range(8):
            out[node(n, j), :] = out[node(n, j), :] - w * gap[j]
    scale = lift * metric[1]
    low, high = y_faces(q, tab)
    own_low = ty_low
    flip = jnp.where(var == 2, -1.0, 1.0).astype(jnp.float32)
    first = (elem & 3) == 0
    near = [
        jnp.where(first, jnp.where(wall, flip * o, r), rolled(t, 1))
        for r, t, o in zip(from_below, ty_high, own_low)
    ]
    gap = jump_flux([n - o for n, o in zip(from_common(tab, near), low)], 1, 1.0)
    for i in range(8):
        out[node(i, 0), :] = out[node(i, 0), :] + scale * gap[i]
    near = [
        jnp.where((elem & 3) == 3, r, rolled(t, -1))
        for r, t in zip(from_above, own_low)
    ]
    gap = jump_flux([n - o for n, o in zip(from_common(tab, near), high)], 1, -1.0)
    gap = [scale * x for x in gap]
    for n in range(PMIN, NQ):
        w = row_of(tab, W_AT + n)
        for i in range(8):
            out[node(i, n), :] = out[node(i, n), :] - w * gap[i]


def span_terms(q, tab, lift, metric, out):
    scale = lift * metric[2]
    low, high = z_faces(q, tab)
    gap_low = jump_flux([h - o for h, o in zip(high, low)], 2, 1.0)
    gap_high = jump_flux([o - h for h, o in zip(high, low)], 2, -1.0)
    sub = lax.broadcasted_iota(jnp.int32, (8, LANES), 0)
    at_low = jnp.where(sub == 0, scale, 0.0)
    at_high = -scale * tab[pl.ds(W_AT, 8), :]
    for i in range(8):
        for j in range(8):
            pick = jnp.full((8, LANES), j, jnp.int32)
            lo = jnp.take_along_axis(gap_low[i], pick, axis=0)
            hi = jnp.take_along_axis(gap_high[i], pick, axis=0)
            out[node(i, j), :] = out[node(i, j), :] + at_low * lo + at_high * hi


def volume_terms(q, tab, metric, out):
    couplings = [coupling_of(d) for d in range(3)]

    def flux(x, d):
        source, has = couplings[d]
        y = metric[d] * x
        mixed = has * jnp.take_along_axis(y, source, axis=1)
        return mixed if mean_flow[d] == 0.0 else mean_flow[d] * y + mixed

    for j in range(8):
        face = [q[node(i, j), :] for i in range(8)]
        for i, x in enumerate(along_first(tab, D_AT, face)):
            out[node(i, j), :] = -flux(x, 0)
    for i in range(8):
        face = [q[node(i, j), :] for j in range(8)]
        by_y = along_first(tab, D_AT, face)
        by_z = along_second(tab, DK_AT, face)
        for j in range(8):
            out[node(i, j), :] = out[node(i, j), :] - (flux(by_y[j], 1) + flux(by_z[j], 2))


def all_metrics(metric_ref):
    return [spread(lambda x, y, d=d: metric_ref[d, x, y], jnp.float32) for d in range(3)]


def all_codes(turn_ref):
    return [spread(lambda x, y, s=s: turn_ref[s, x, y], jnp.int32) for s in range(2)]


def kept_metrics(params):
    return [params[pl.ds(8 * d, 8), :] for d in range(3)]


def kept_codes(params):
    return [params[pl.ds(24 + 8 * s, 8), :].astype(jnp.int32) for s in range(2)]


def table_for(columns, level_row, tab):
    level = (lax.broadcasted_iota(jnp.int32, (LANES, LANES), 0) & 7) + PMIN
    one_hot = jnp.where(
        level.astype(jnp.float32) == jnp.broadcast_to(level_row, (LANES, LANES)), 1.0, 0.0
    ).astype(jnp.bfloat16)
    pad = jnp.zeros((LANES - 24, LANES), jnp.float32)
    for part in range(4):
        at = part * LANES
        size = min(LANES, TAB_ROWS - at)
        left = jnp.concatenate([columns[:, pl.ds(at, LANES)], pad[:8]], axis=0)
        cut = []
        for _ in range(3):
            cut.append(left.astype(jnp.bfloat16).astype(jnp.float32))
            left = left - cut[-1]
        block = jnp.concatenate([x[:8] for x in cut] + [pad], axis=0).T
        tab[pl.ds(at, size), :] = jnp.dot(
            block.astype(jnp.bfloat16), one_hot, preferred_element_type=jnp.float32
        )[:size]


def fetched(pairs, sems):
    copies = [pltpu.make_async_copy(a, b, sems.at[n]) for n, (a, b) in enumerate(pairs)]
    for copy in copies:
        copy.start()
    return copies


def first_kernel(
    fields, columns, orders_hbm, turn_hbm, metric_hbm, _, core_ref, row_ref, q, tab, params, *rest
):
    outs = rest[:6]
    flat, buf, orders, turn, metric_ref, sems = rest[6:]
    copies = fetched(
        [(orders_hbm, orders), (turn_hbm, turn), (metric_hbm, metric_ref)], sems
    )
    flat[pl.ds(80, 48), :] = jnp.zeros((48, 512), jnp.float32)
    for v in range(VARS):
        for x in range(4):
            flat[pl.ds(v * 16 + x * 4, 4), :] = fields[x, v]
    for copy in copies:
        copy.wait()
    order = spread(lambda x, y: orders[x, y].astype(jnp.float32), jnp.float32)
    metric, codes = all_metrics(metric_ref), all_codes(turn)
    for n, x in enumerate(metric + codes + [order]):
        params[pl.ds(8 * n, 8), :] = x.astype(jnp.float32)
    table_for(columns, order[0:1, :], tab)
    in_k = tab[pl.ds(A_AT, 8), :]
    for part in range(4):
        block = flat[:, pl.ds(part * LANES, LANES)].T
        for half in range(2):
            in_ik = in_k * row_of(tab, A_AT + part * 2 + half)
            for j in range(8):
                at = (half * 8 + j) * 8
                q[node(part * 2 + half, j), :] = (
                    block[at : at + 8] * in_ik * row_of(tab, A_AT + j)
                )
    first_core, _ = places(core_ref, row_ref)
    make_messages(q, tab, order, metric, codes, first_core, outs, buf)


def inner_kernel(q, tab, params, *rest):
    traces, (rate, up, down) = [load_face(ref) for ref in rest[:4]], rest[4:]
    metric = kept_metrics(params)
    make_row_messages(q, tab, params[pl.ds(40, 8), :], metric, traces, up, down)
    volume_terms(q, tab, metric, rate)
    span_terms(q, tab, tab[pl.ds(LIFT_AT, 8), :], metric, rate)


def second_kernel(up, down, chip, blk, inner, core_ref, row_ref, pair_send, row_send):
    first_core, even_row = places(core_ref, row_ref)
    left, right = sides_of(chip, blk, first_core)
    _, elem, _ = lane_ids()
    up, down = load_face(up), load_face(down)

    def with_corners(message, edge, y, line):
        at_left, at_right = elem == 3, elem == 15
        out = message[:6]
        out.append(
            jnp.where(
                at_left,
                rolled(left[edge], 3 - y),
                jnp.where(at_right, rolled(right[edge], 15 - y), message[6]),
            )
        )
        out.append(
            jnp.where(
                at_left,
                rolled(left[line], -9 - y),
                jnp.where(at_right, rolled(right[line], 3 - y), message[7]),
            )
        )
        return out

    up = with_corners(up, 7, 3, 1)
    down = with_corners(down, 0, 0, 0)
    store_face(pair_send, [jnp.where(even_row, u, d) for u, d in zip(up, down)])
    store_face(row_send, [jnp.where(even_row, d, u) for u, d in zip(up, down)])


def third_kernel(q, tab, params, inner, columns, migration_hbm, core_ref, row_ref, *rest):
    traces, arrived = rest[:4], rest[4:8]
    outs = rest[8:12]
    rate, middle, second, flat, slots, count, migration, halo_tab, buf, sems = rest[12:]
    copies = fetched([(migration_hbm, migration)], sems)
    first_core, even_row = places(core_ref, row_ref)
    wall = row_ref[0] == 0
    metric, codes = kept_metrics(params), kept_codes(params)
    lift = tab[pl.ds(LIFT_AT, 8), :]
    chip, blk, pair, row = arrived
    left, right = sides_of(chip, blk, first_core)
    below, above = sides_of(pair, row, even_row)
    own = [load_face(ref) for ref in traces]
    beside = halo_step((left, right, below, above), own, wall, columns, halo_tab, buf)
    near = (left, [rolled(x, 12) for x in right], below, [rolled(x, 3) for x in above])
    rate[...] = inner[...]
    gaps_to(q, tab, lift, own, near, wall, metric, rate)
    for n in range(64):
        at = pl.ds(8 * n, 8)
        middle[at, :] = q[at, :] + time_step * rate[at, :]
    x_ends, y_ends = x_faces(middle, tab), y_faces(middle, tab)
    own = [turned(to_common(tab, x_ends[side]), codes[side], buf) for side in range(2)]
    own = own + [to_common(tab, y_ends[side]) for side in range(2)]
    volume_terms(middle, tab, metric, second)
    span_terms(middle, tab, lift, metric, second)
    gaps_to(middle, tab, lift, own, from_halo(beside), wall, metric, second)
    copies[0].wait()
    for part in range(4):
        at = pl.ds(part * LANES, LANES)
        flat[:, 0, at] = ((0.5 * time_step) * (rate[at, :] + second[at, :])).T
    slots[...] = jnp.zeros_like(slots)
    for m in range(SPREAD):
        count[m] = 0
    for e in range(NB):
        m = migration[0, 0, 0, e]
        c = count[m]
        count[m] = c + 1
        slot = jnp.where(core_ref[0] == 0, m, SPREAD - 1 - m) * CAP + c
        for v in range(VARS):
            slots[slot, v] = flat[v * 16 + e]
    at = 0
    for out in outs:
        size = out.shape[0]
        out[...] = slots[pl.ds(at, size)]
        at += size


def last_kernel(far, own, near, core_ref, chip, relayed, out, sems):
    def put(groups):
        copies = [
            pltpu.make_async_copy(piece, out.at[pl.ds(m * CAP, CAP)], sems.at[m])
            for m, piece in enumerate(groups)
        ]
        for copy in copies:
            copy.start()
        for copy in copies:
            copy.wait()

    first = far.at[pl.ds(0, CAP)]

    @pl.when(core_ref[0] == 0)
    def _():
        put([first, chip.at[1], own, relayed.at[1, pl.ds(CAP, CAP)], near])

    @pl.when(core_ref[0] != 0)
    def _():
        put([near, relayed.at[0, pl.ds(CAP, CAP)], own, chip.at[0], first])


def f32(*shape):
    return jax.ShapeDtypeStruct(shape, jnp.float32)


VMEM = pl.BlockSpec(memory_space=pltpu.VMEM)
SMEM = pl.BlockSpec(memory_space=pltpu.SMEM)
HBM = pl.BlockSpec(memory_space=pltpu.HBM)
ANY = pl.BlockSpec(memory_space=pl.ANY)
PARAMS = pltpu.CompilerParams(vmem_limit_bytes=32 * 1024 * 1024)
FACE = f32(64, LANES)
VOLUME = f32(512, LANES)


def pairs_of(count, first):
    return [[n, n + 1] for n in range(first, count - 1, 2)]


def swapped(array, axis, wraps):
    count = lax.axis_size(axis)
    pairs = [(a, b) for a, b in pairs_of(count, 1)]
    if wraps:
        pairs.append((count - 1, 0))
    return lax.ppermute(array, axis, pairs + [(b, a) for a, b in pairs])


def paired(array, axis):
    return lax.all_gather(array, axis, axis_index_groups=pairs_of(lax.axis_size(axis), 0))


def hopped(array, outward):
    count = lax.axis_size("blk")
    step = [-2, 2] if outward else [2, -2]
    return lax.ppermute(array, "blk", [(n, (n + step[n % 2]) % count) for n in range(count)])


def vmem(*shape):
    return pltpu.VMEM(shape, jnp.float32)


def sems(count):
    return pltpu.SemaphoreType.DMA((count,))


def local(fields, orders, metric, face_turn, migration):
    by_var = jnp.transpose(fields, (0, 2, 1, 3))
    core = lax.rem(lax.axis_index("blk").astype(jnp.int32), 2).reshape(1)
    row = lax.axis_index("row").astype(jnp.int32).reshape(1)
    columns = jnp.asarray(table_columns())
    targets = jnp.transpose(migration, (0, 1, 3, 2))
    q, tab, params, *faces = pl.pallas_call(
        first_kernel,
        out_shape=[VOLUME, f32(TAB_ROWS, LANES), f32(48, LANES)] + [FACE] * 6,
        in_specs=[VMEM] * 2 + [HBM] * 3 + [ANY] + [SMEM] * 2,
        out_specs=[VMEM] * 9,
        scratch_shapes=[
            vmem(LANES, 512),
            vmem(64, LANES),
            pltpu.SMEM((4, 4), jnp.int32),
            pltpu.SMEM((2, 4, 4), jnp.int32),
            pltpu.SMEM((3, 4, 4), jnp.float32),
            sems(3),
        ],
        compiler_params=PARAMS,
    )(by_var, columns, orders, face_turn, metric, targets, core, row)
    chip_send, blk_send = faces[4:]
    blk = swapped(blk_send, "blk", True)
    chip = paired(chip_send, "blk")
    inner, up, down = pl.pallas_call(
        inner_kernel,
        out_shape=[VOLUME, FACE, FACE],
        in_specs=[VMEM] * 7,
        out_specs=[VMEM] * 3,
        compiler_params=PARAMS,
        cost_estimate=pl.CostEstimate(
            flops=40_000_000, bytes_accessed=6_000_000, transcendentals=0
        ),
    )(q, tab, params, *faces[:4])
    pair_send, row_send = pl.pallas_call(
        second_kernel,
        out_shape=[FACE] * 2,
        in_specs=[VMEM] * 4 + [ANY] + [SMEM] * 2,
        out_specs=[VMEM] * 2,
        compiler_params=PARAMS,
    )(up, down, chip, blk, inner, core, row)
    beyond = swapped(row_send, "row", False)
    pair = paired(pair_send, "row")
    outward, own, same_chip, inward = pl.pallas_call(
        third_kernel,
        out_shape=[f32(n, VARS, 1, 512) for n in (2 * CAP, CAP, CAP, CAP)],
        in_specs=[VMEM] * 5 + [HBM] + [SMEM] * 2 + [VMEM] * 8,
        out_specs=[VMEM] * 4,
        scratch_shapes=[
            vmem(512, LANES),
            vmem(512, LANES),
            vmem(512, LANES),
            vmem(LANES, 1, 512),
            vmem(SPREAD * CAP, VARS, 1, 512),
            pltpu.SMEM((8,), jnp.int32),
            pltpu.SMEM((1, 1, 1, NB), jnp.int32),
            vmem(TAB_ROWS, LANES),
            vmem(64, LANES),
            sems(1),
        ],
        compiler_params=PARAMS,
    )(
        q, tab, params, inner, columns, targets, core, row,
        *faces[:4], chip, blk, pair, beyond,
    )
    far = hopped(outward, True)
    near = hopped(inward, False)
    chip = paired(same_chip, "blk")
    relayed = paired(far, "blk")
    moved = pl.pallas_call(
        last_kernel,
        out_shape=f32(SPREAD * CAP, VARS, 1, 512),
        in_specs=[ANY] * 3 + [SMEM] + [ANY] * 2,
        out_specs=HBM,
        scratch_shapes=[sems(SPREAD)],
        compiler_params=PARAMS,
    )(far, own, near, core, chip, relayed)
    return jnp.transpose(moved, (2, 0, 1, 3)).reshape(1, 1, SPREAD * CAP, VARS, 512)


def solution(mesh):
    placed = (
        P("blk", "row", None, None),
        P("blk", "row"),
        P(None, "blk", "row"),
        P(None, "blk", "row"),
        P("blk", "row", None, None),
    )
    return jax.shard_map(
        local,
        mesh=mesh,
        in_specs=placed,
        out_specs=P("blk", "row", None, None, None),
        check_vma=False,
    )
```
